32 devices in a mesh: vars: 4 (over z), dp: 8 (over y, x, core).
Axes of the slice: x: 2, y: 2, z: 4, core: 2. Of those that a mesh axis runs over, the one named last changes fastest.
Arguments:
- fields: bfloat16 [72, 8, 4, 4, 1024], P('vars', 'dp'), may hold values from -6 to 6
- var_ids: int32 [72], P('vars'), may hold values from 0 to 71, each once
- segments: int32 [8, 4, 1024], P('dp', 'vars'), may hold values from 0 to 3, never falling along the last dimension, each value on 1 to 512 neighbouring positions
- condition: bfloat16 [8, 4, 384], P('dp', 'vars'), may hold values from -5 to 5
- cotangent: bfloat16 [8, 4, 1024, 384], P('dp', 'vars'), may hold values from -6 to 6
- slot_weights: float32 [72, 5, 384], P('vars'), may hold values from -3 to 3
- slot_momentum: float32 [72, 5, 384], P('vars'), may hold values from -2 to 2
- slot_average: float32 [72, 5, 384], P('vars'), may hold values from -3 to 3
- square: float32 [4, 384, 384], P(None, 'dp'), may hold values from -0.3125 to 0.3125
- square_momentum: float32 [4, 384, 384], P(None, 'dp'), may hold values from -4 to 4
- square_average: float32 [4, 384, 384], P(None, 'dp'), may hold values from -0.3125 to 0.3125
- wide: float32 [384, 3456], P('dp'), may hold values from -0.3125 to 0.3125
- wide_momentum: float32 [384, 3456], P('dp'), may hold values from -4 to 4
- wide_average: float32 [384, 3456], P('dp'), may hold values from -0.3125 to 0.3125
- mlp: float32 [2, 384, 1536], P(None, 'dp'), may hold values from -0.21875 to 0.21875
- mlp_momentum: float32 [2, 384, 1536], P(None, 'dp'), may hold values from -4 to 4
- mlp_average: float32 [2, 384, 1536], P(None, 'dp'), may hold values from -0.21875 to 0.21875
- vectors: float32 [11, 384], replicated, may hold values from -3 to 3
- vectors_momentum: float32 [11, 384], replicated, may hold values from -4 to 4
- vectors_average: float32 [11, 384], replicated, may hold values from -3 to 3
Outputs:
- block_out: bfloat16 [8, 4, 1024, 384], P('dp', 'vars')
- field_grad: float32 [72, 8, 4, 4, 1024], P('vars', 'dp')
- slot_grad: float32 [72, 5, 384], P('vars')
- slot_new: float32 [72, 5, 384], P('vars')
- slot_momentum_new: float32 [72, 5, 384], P('vars')
- slot_average_new: float32 [72, 5, 384], P('vars')
- square_grad: float32 [4, 384, 384], P(None, 'dp')
- square_new: float32 [4, 384, 384], P(None, 'dp')
- square_momentum_new: float32 [4, 384, 384], P(None, 'dp')
- square_average_new: float32 [4, 384, 384], P(None, 'dp')
- wide_grad: float32 [384, 3456], P('dp')
- wide_new: float32 [384, 3456], P('dp')
- wide_momentum_new: float32 [384, 3456], P('dp')
- wide_average_new: float32 [384, 3456], P('dp')
- mlp_grad: float32 [2, 384, 1536], P(None, 'dp')
- mlp_new: float32 [2, 384, 1536], P(None, 'dp')
- mlp_momentum_new: float32 [2, 384, 1536], P(None, 'dp')
- mlp_average_new: float32 [2, 384, 1536], P(None, 'dp')
- vectors_grad: float32 [11, 384], replicated
- vectors_new: float32 [11, 384], replicated
- vectors_momentum_new: float32 [11, 384], replicated
- vectors_average_new: float32 [11, 384], replicated
The draws below stay inside these ranges and needn't reach their ends.
Inputs may be any that keep to these rules, and one draw needn't show every extreme that they name: Each number appears once; slot v holds variable var_ids[v] when that is below 69 and holds no variable otherwise. `segments`: ids never fall along a sequence; a segment has 1 to 512 patch slots, and one has exactly that many.
All inputs are finite; a program needn't handle non-finite values.
Results may differ from the reference program's by a relative error of at most 0.014.
Values may be sent and summed in bfloat16 or wider, within the bound.
A program may use at most 448 MiB of HBM per device.

```python
import math
import jax
import jax.numpy as jnp
import numpy as np
from jax import lax

D = 384
FF = 1536
HEADS = 6
HDIM = 64
PATCH = 4
NVARS = 69
SEGS = 4
VEC = 11
SEQ = 1024
VSLOTS = 72
N_VARS = 4
N_DP = 8


def steps_of(stream_key, extent, pieces, smallest, largest):
    def one(dim, blocks):
        draws = jax.random.uniform(jax.random.fold_in(jax.random.fold_in(stream_key, 6), dim), (blocks,), jnp.float32, smallest / len(pieces), largest / len(pieces))
        return jnp.repeat(jnp.exp(draws), extent[dim] // blocks).reshape((-1,) + (1,) * (len(extent) - dim - 1))

    factor_of = one(*pieces[0])
    for cut in pieces[1:]:
        factor_of = factor_of * one(*cut)
    return factor_of


def profile(number_of, total, bound, skew):
    loads = [(1 << 20) // math.isqrt(grade ** skew) + 1 for grade in range(2, number_of + 1)]
    spare, given = total - bound - (number_of - 1), [1] * (number_of - 1)
    while spare > 0:
        movable = [i for i in range(number_of - 1) if given[i] < bound]
        mass, budget = sum([loads[i] for i in movable]), spare
        for i in movable:
            addition = min(bound - given[i], max(1, budget * loads[i] // mass), spare)
            given[i] = given[i] + addition
            spare = spare - addition
    return np.array([bound] + given)


def ragged(stream_key, number_of, total, limit, skew):
    if number_of == 2:
        one = jax.random.randint(stream_key, (), max(1, total - limit), min(limit, total - 1) + 1)
        return jnp.stack([one, total - one])
    tallies = jnp.asarray(profile(number_of, total, limit, skew), jnp.int32)
    twos = (number_of - 1) // 2
    donor, sink = tallies[1:1 + 2 * twos:2], tallies[2:2 + 2 * twos:2]
    slack = jnp.minimum(donor - 1, limit - sink)
    shifted = jax.random.randint(jax.random.fold_in(stream_key, 1), (twos,), 0, 1 << 20) % (slack + 1)
    tallies = tallies.at[1:1 + 2 * twos:2].set(donor - shifted).at[2:2 + 2 * twos:2].set(sink + shifted)
    return tallies[jax.random.permutation(jax.random.fold_in(stream_key, 2), number_of)]


def bell_draw(own_key, dims, width, bound, pieces=(), dtype=jnp.bfloat16):
    array = width * jax.random.normal(own_key, dims, jnp.float32)
    if pieces:
        array = array * steps_of(own_key, dims, pieces, -0.22, 0.18)
    return jnp.clip(array, -bound, bound).astype(dtype)


def setup_inputs(seed: int = 0) -> dict:
    arg_keys = jax.random.split(jax.random.key(seed), 21)
    fields = bell_draw(arg_keys[0], (VSLOTS, N_DP, N_VARS, PATCH, SEQ), 1.0, 6.0, ((0, 4), (1, 8)))
    var_ids = jax.random.permutation(arg_keys[1], VSLOTS).astype(jnp.int32)
    segments = jax.vmap(lambda own: jnp.searchsorted(jnp.cumsum(ragged(own, SEGS, SEQ, SEQ // 2, 0)), jnp.arange(SEQ), side="right"))(jax.random.split(arg_keys[2], N_DP * N_VARS)).reshape((N_DP, N_VARS, SEQ)).astype(jnp.int32)
    condition = bell_draw(arg_keys[3], (N_DP, N_VARS, D), 1.0, 5.0, ((0, 8), (1, 4)))
    cotangent = bell_draw(arg_keys[4], (N_DP, N_VARS, SEQ, D), 1.0, 6.0, ((0, 8), (1, 4)))
    slot_weights = bell_draw(arg_keys[5], (VSLOTS, PATCH + 1, D), 0.5, 3.0, ((0, 4),), jnp.float32)
    slot_momentum = bell_draw(arg_keys[6], (VSLOTS, PATCH + 1, D), 0.3, 2.0, ((0, 4),), jnp.float32)
    slot_average = bell_draw(arg_keys[7], (VSLOTS, PATCH + 1, D), 0.5, 3.0, ((0, 4),), jnp.float32)
    square = bell_draw(arg_keys[8], (4, D, D), D ** -0.5, 0.3125, ((1, 8),), jnp.float32)
    square_momentum = bell_draw(arg_keys[9], (4, D, D), 1.0, 4.0, ((1, 8),), jnp.float32)
    square_average = bell_draw(arg_keys[10], (4, D, D), D ** -0.5, 0.3125, ((1, 8),), jnp.float32)
    wide = bell_draw(arg_keys[11], (D, 9 * D), D ** -0.5, 0.3125, ((0, 8),), jnp.float32)
    wide_momentum = bell_draw(arg_keys[12], (D, 9 * D), 1.0, 4.0, ((0, 8),), jnp.float32)
    wide_average = bell_draw(arg_keys[13], (D, 9 * D), D ** -0.5, 0.3125, ((0, 8),), jnp.float32)
    mlp = bell_draw(arg_keys[14], (2, D, FF), (2 * D) ** -0.5, 0.21875, ((1, 8),), jnp.float32)
    mlp_momentum = bell_draw(arg_keys[15], (2, D, FF), 1.0, 4.0, ((1, 8),), jnp.float32)
    mlp_average = bell_draw(arg_keys[16], (2, D, FF), (2 * D) ** -0.5, 0.21875, ((1, 8),), jnp.float32)
    vectors = bell_draw(arg_keys[17], (VEC, D), 0.5, 3.0, (), jnp.float32)
    vectors_momentum = bell_draw(arg_keys[18], (VEC, D), 1.0, 4.0, (), jnp.float32)
    vectors_average = bell_draw(arg_keys[19], (VEC, D), 0.5, 3.0, (), jnp.float32)
    return {"fields": fields, "var_ids": var_ids, "segments": segments, "condition": condition, "cotangent": cotangent, "slot_weights": slot_weights, "slot_momentum": slot_momentum, "slot_average": slot_average, "square": square, "square_momentum": square_momentum, "square_average": square_average, "wide": wide, "wide_momentum": wide_momentum, "wide_average": wide_average, "mlp": mlp, "mlp_momentum": mlp_momentum, "mlp_average": mlp_average, "vectors": vectors, "vectors_momentum": vectors_momentum, "vectors_average": vectors_average}


NEGATIVE = -1e+30
EPSILON = 1e-06
MOMENTUM = 0.9
RATE = 0.05
EMBED_RATE = 0.5
AVERAGE_DECAY = 0.9
HIGHEST = lax.Precision.HIGHEST

@jax.custom_vjp
def low(v):
    return lax.optimization_barrier(v.astype(jnp.bfloat16)).astype(jnp.float32)

@jax.custom_vjp
def low_back(v):
    return v

def low_keep(v):
    return (low(v), None)

def low_pass(kept, grad):
    return (grad,)

def back_keep(v):
    return (v, None)

def back_low(kept, grad):
    return (low(grad),)
low.defvjp(low_keep, low_pass)
low_back.defvjp(back_keep, back_low)

def normalize(values):
    center = values - lax.optimization_barrier(jnp.mean(values, axis=-1, keepdims=True))
    return center * lax.rsqrt(lax.optimization_barrier(jnp.mean(center * center, axis=-1, keepdims=True)) + EPSILON)

def renew(weight, momentum, average, gradient, step_rate):
    new_momentum = MOMENTUM * momentum + gradient
    new_weight = weight - step_rate * (gradient + MOMENTUM * new_momentum)
    new_average = AVERAGE_DECAY * average + (1.0 - AVERAGE_DECAY) * new_weight
    return (gradient, new_weight, new_momentum, new_average)

def sequence_output(item, slot_weights, square, wide, mlp, vectors, key_vectors, valid):
    patches, segment, condition = item
    scale = HDIM ** (-0.5)
    embed = low(jnp.einsum('vps,vpd->vsd', patches, slot_weights[:, :PATCH], precision=HIGHEST) + slot_weights[:, PATCH][:, None, :])
    pool_raw = low_back(jnp.einsum('vsd,dh->vsh', embed, key_vectors, precision=HIGHEST))
    pool_score = jnp.where(valid[:, None, None], pool_raw * scale, NEGATIVE)
    pool_prob = jax.nn.softmax(pool_score, axis=0)
    slot_value = low_back(jnp.einsum('vsd,de->vse', embed, square[1], precision=HIGHEST))
    pooled = lax.optimization_barrier(jnp.sum(jnp.repeat(pool_prob, HDIM, axis=2) * slot_value, axis=0)) + vectors[1]
    pooled = low(low_back(pooled))
    start = low_back(jnp.dot(pooled, square[2], precision=HIGHEST) + vectors[2])
    cond = low(jax.nn.silu(condition))
    modulation = jnp.dot(cond[None], wide[:, 3 * D:], precision=HIGHEST)[0] + vectors[5:].reshape(-1)
    modulation = modulation.reshape(6, D)
    input_one = low(normalize(start) * (1.0 + modulation[1]) + modulation[0])
    triple = low(low_back(jnp.dot(input_one, wide[:, :3 * D], precision=HIGHEST)))
    queries = triple[:, :D].reshape(SEQ, HEADS, HDIM)
    keys = triple[:, D:2 * D].reshape(SEQ, HEADS, HDIM)
    values = triple[:, 2 * D:].reshape(SEQ, HEADS, HDIM)
    att_raw = low_back(jnp.einsum('shk,thk->hst', queries, keys, precision=HIGHEST))
    same = segment[:, None] == segment[None, :]
    logits = jnp.where(same[None], att_raw * scale, NEGATIVE)
    att_prob = low(jax.nn.softmax(logits, axis=-1))
    attended = jnp.einsum('hst,thk->shk', att_prob, values, precision=HIGHEST).reshape(SEQ, D)
    attended = low(low_back(attended))
    att_branch = low_back(jnp.dot(attended, square[3], precision=HIGHEST) + vectors[3])
    middle = start + modulation[2] * att_branch
    input_two = low(normalize(middle) * (1.0 + modulation[4]) + modulation[3])
    up = low_back(jnp.dot(input_two, mlp[0], precision=HIGHEST))
    activation = low(jax.nn.gelu(up))
    mlp_branch = low_back(jnp.dot(activation, mlp[1].T, precision=HIGHEST) + vectors[4])
    return middle + modulation[5] * mlp_branch

def reference(fields, var_ids, segments, condition, cotangent, slot_weights, slot_momentum, slot_average, square, square_momentum, square_average, wide, wide_momentum, wide_average, mlp, mlp_momentum, mlp_average, vectors, vectors_momentum, vectors_average):
    count = N_DP * N_VARS
    valid = var_ids < NVARS
    patches = jnp.transpose(fields.astype(jnp.float32).reshape(VSLOTS, count, PATCH, SEQ), (1, 0, 2, 3))
    segment_all = segments.reshape(count, SEQ)
    condition_all = condition.astype(jnp.float32).reshape(count, D)
    grad_out = cotangent.astype(jnp.float32).reshape(count, SEQ, D) * (1.0 / math.sqrt(count * SEQ))

    def forward(params, patch_values):
        slot_w, square_w, wide_w, mlp_w, vector_w = params
        square_low = low(square_w)
        wide_low = low(wide_w)
        mlp_low = low(mlp_w)
        key_vectors = low(jnp.einsum('dhk,hk->dh', square_low[0].reshape(D, HEADS, HDIM), vector_w[0].reshape(HEADS, HDIM), precision=HIGHEST))

        def one_sequence(item):
            return sequence_output(item, slot_w, square_low, wide_low, mlp_low, vector_w, key_vectors, valid)
        return lax.map(jax.checkpoint(one_sequence), (patch_values, segment_all, condition_all))
    params = (slot_weights, square, wide, mlp, vectors)
    output, pullback = jax.vjp(forward, params, patches)
    grads, patch_grad = pullback(grad_out)
    block_out = output.reshape(N_DP, N_VARS, SEQ, D).astype(jnp.bfloat16)
    field_grad = jnp.transpose(patch_grad, (1, 0, 2, 3)).reshape(VSLOTS, N_DP, N_VARS, PATCH, SEQ)
    slot_out = renew(slot_weights, slot_momentum, slot_average, grads[0], EMBED_RATE)
    square_out = renew(square, square_momentum, square_average, grads[1], RATE)
    wide_out = renew(wide, wide_momentum, wide_average, grads[2], RATE)
    mlp_out = renew(mlp, mlp_momentum, mlp_average, grads[3], RATE)
    vector_out = renew(vectors, vectors_momentum, vectors_average, grads[4], RATE)
    return (block_out, field_grad, slot_out[0], slot_out[1], slot_out[2], slot_out[3], square_out[0], square_out[1], square_out[2], square_out[3], wide_out[0], wide_out[1], wide_out[2], wide_out[3], mlp_out[0], mlp_out[1], mlp_out[2], mlp_out[3], vector_out[0], vector_out[1], vector_out[2], vector_out[3])
```

```python
import functools
import math

import jax
import jax.numpy as jnp
from jax import lax
from jax.experimental import pallas as pl
from jax.experimental.pallas import tpu as pltpu
from jax.sharding import PartitionSpec as P

D = 384
HEADS = 6
HDIM = 64
PATCH = 4
NVARS = 69


NEGATIVE = -1e30
EPSILON = 1e-06
MOMENTUM = 0.9
RATE = 0.05
EMBED_RATE = 0.5
AVERAGE_DECAY = 0.9
HIGHEST = lax.Precision.HIGHEST


def normalize(values):
    center = values - jnp.mean(values, axis=-1, keepdims=True)
    inverse = lax.rsqrt(jnp.mean(center * center, axis=-1, keepdims=True) + EPSILON)
    return (center * inverse, inverse)


def normalize_back(grad_normed, normed, inverse):
    first = jnp.mean(grad_normed, axis=-1, keepdims=True)
    second = jnp.mean(grad_normed * normed, axis=-1, keepdims=True)
    return inverse * (grad_normed - first - normed * second)


def contract_rows(left, right):
    return lax.dot_general(
        left, right, (((0,), (0,)), ((), ())), preferred_element_type=jnp.float32
    )


def contract_cols(left, right):
    return lax.dot_general(
        left, right, (((1,), (1,)), ((), ())), preferred_element_type=jnp.float32
    )


def renew(weight, momentum, average, gradient, step_rate):
    new_momentum = MOMENTUM * momentum + gradient
    new_weight = weight - step_rate * (gradient + MOMENTUM * new_momentum)
    new_average = AVERAGE_DECAY * average + (1.0 - AVERAGE_DECAY) * new_weight
    return (gradient, new_weight, new_momentum, new_average)


def split_high(values):
    high = values.astype(jnp.bfloat16)
    return high, (values - high.astype(jnp.float32)).astype(jnp.bfloat16)


def pool_forward(patches, score_map, value_map, valid):
    ones = jnp.ones_like(patches[:1])
    full = jnp.concatenate([patches, ones], axis=0)
    raw = jnp.einsum("pvs,pvh->hvs", full, score_map, precision=HIGHEST)
    scores = jnp.where(valid[None, :, None], raw * HDIM ** (-0.5), NEGATIVE)
    probs = jax.nn.softmax(scores, axis=1)
    mixed = (probs[:, None] * full[None]).astype(jnp.bfloat16)
    high, below = split_high(value_map)
    mean = jnp.einsum(
        "hpvs,pvhk->shk", mixed, high, preferred_element_type=jnp.float32
    ) + jnp.einsum("hpvs,pvhk->shk", mixed, below, preferred_element_type=jnp.float32)
    return full, probs, mixed, mean.reshape(mean.shape[0], D)


def pool_backward(full, probs, mixed, mean, score_map, value_map, grad_pooled):
    length = grad_pooled.shape[0]
    grad_heads = grad_pooled.reshape(length, HEADS, HDIM)
    high, below = split_high(value_map)
    cross = jnp.einsum(
        "pvhk,shk->hpvs", high, grad_heads, preferred_element_type=jnp.float32
    ) + jnp.einsum("pvhk,shk->hpvs", below, grad_heads, preferred_element_type=jnp.float32)
    along = jnp.sum(cross * full[None], axis=1)
    along_mean = jnp.sum(
        (grad_pooled.astype(jnp.float32) * mean).reshape(length, HEADS, HDIM), axis=-1
    )
    grad_scores = (probs * (along - along_mean.T[:, None]) * HDIM ** (-0.5)).astype(jnp.bfloat16)
    grad_float = grad_scores.astype(jnp.float32)
    grad_map = jnp.einsum("hpvs,shk->pvhk", mixed, grad_heads, preferred_element_type=jnp.float32)
    grad_key = jnp.einsum("pvs,hvs->pvh", full, grad_float, precision=HIGHEST)
    field = jnp.sum(probs[:, None] * cross[:, :PATCH], axis=0) + jnp.einsum(
        "hvs,pvh->pvs", grad_float, score_map[:PATCH], precision=HIGHEST
    )
    return grad_map.reshape(grad_map.shape[:2] + (D,)), grad_key, field


CHUNKS = 4
CHUNK = 12
WIDTH = 128
VEC_ROWS = 16
MESH = pl.DeviceIdType.MESH


def flip(index, mask, bits):
    total = 0
    for bit in range(bits):
        own = (index // 2**bit) % 2
        total = total + (1 - own if (mask >> bit) & 1 else own) * 2**bit
    return total


def rounds_of(bits, backward):
    order = list(range(bits))
    return order[::-1] if backward else order


def mask_of(order, level, entry):
    mask = 0
    for place, bit in enumerate(order[level:]):
        if (entry >> (len(order) - level - 1 - place)) & 1:
            mask |= 1 << bit
    return mask


def greet(dp, here, bits, groups):
    barrier = pltpu.get_barrier_semaphore()
    for bit in range(bits):
        pl.semaphore_signal(
            barrier, inc=1, device_id={"dp": flip(dp, 1 << bit, bits)}, device_id_type=MESH
        )
    for step in range(1, groups):
        pl.semaphore_signal(
            barrier, inc=1, device_id={"vars": (here + step) % groups}, device_id_type=MESH
        )
    pl.semaphore_wait(barrier, bits + groups - 1)


class Copies:
    def __init__(self, send_sem, recv_sem):
        self.send_sem, self.recv_sem = send_sem, recv_sem
        self.started = []

    def start(self, source, target, device):
        place = len(self.started)
        copy = pltpu.make_async_remote_copy(
            src_ref=source,
            dst_ref=target,
            send_sem=self.send_sem.at[place],
            recv_sem=self.recv_sem.at[place],
            device_id=device,
            device_id_type=MESH,
        )
        copy.start()
        self.started.append(copy)
        return copy

    def finish(self):
        for copy in self.started:
            copy.wait_send()


def spread_steps(copies, ref, dp, bits):
    order = list(range(1, bits)) + [0]
    for level, bit in enumerate(order):
        batch = []
        for entry in range(2**level):
            mask = sum(1 << order[i] for i in range(level) if (entry >> i) & 1)
            block = flip(dp, mask, bits)
            batch.append(
                copies.start(ref.at[block], ref.at[block], {"dp": flip(dp, 1 << bit, bits)})
            )
        yield
        for copy in batch:
            copy.wait_recv()


def reduce_kernel(
    count,
    groups,
    g_ref,
    vec_ref,
    field_ref,
    sum_ref,
    slot_ref,
    vec_all,
    field_out,
    recv0,
    acc,
    send_x,
    recv_x,
    zsend,
    zrecv,
    zown,
    total,
    send_sem,
    recv_sem,
):
    bits = count.bit_length() - 1
    lower = bits - 1
    dp, here = lax.axis_index("dp"), lax.axis_index("vars")
    core, pair = dp % 2, dp // 2
    greet(dp, here, bits, groups)
    copies = Copies(send_sem, recv_sem)
    half = CHUNK // 2
    share = CHUNK // groups
    other = {"dp": dp + 1 - 2 * core}

    field_copies = [
        copies.start(
            field_ref.at[(here + step) % groups],
            field_out.at[here],
            {"vars": (here + step) % groups},
        )
        for step in range(1, groups)
    ]
    level0 = {}
    for chunk in range(CHUNKS):
        for side in range(2):
            piece = 2 * chunk + side
            level0[piece] = copies.start(
                g_ref.at[:, 1 - core, pl.ds(piece * half, half)],
                recv0.at[piece],
                other,
            )
    vec_copies = [
        copies.start(
            vec_ref, vec_all.at[dp, here], {"vars": (here + step) % groups}
        )
        for step in range(1, groups)
    ]
    vec_all[dp, here] = vec_ref[...]
    for side in range(1):
        field_out[here] = field_ref[here]
    for copy in vec_copies:
        copy.wait_recv()
    vec_steps = spread_steps(copies, vec_all, dp, bits)
    next(vec_steps)

    crossing = {}

    def send_level(piece, level):
        order = rounds_of(lower, piece % 2)
        entries = 2 ** (lower - 1 - level)
        low = 2**lower - 2 ** (lower - level)
        partner = {"dp": 2 * flip(pair, 1 << order[level], lower) + core}
        crossing[piece, level] = copies.start(
            send_x.at[piece, pl.ds(low, entries)],
            recv_x.at[piece, pl.ds(low, entries)],
            partner,
        )

    def first(piece):
        order = rounds_of(lower, piece % 2)
        level0[piece].wait_recv()
        kept = 2 ** (lower - 1)
        for entry in range(2**lower):
            block = flip(pair, mask_of(order, 0, entry), lower)
            value = g_ref[block, core, pl.ds(piece * half, half)].astype(jnp.float32) + recv0[
                piece, block
            ].astype(jnp.float32)
            if entry < kept:
                acc[piece, entry] = value
            else:
                send_x[piece, entry - kept] = value.astype(jnp.bfloat16)
        send_level(piece, 0)

    def later(piece, level):
        crossing[piece, level].wait_recv()
        entries = 2 ** (lower - 1 - level)
        low = 2**lower - 2 ** (lower - level)
        kept = entries // 2
        for entry in range(entries):
            value = acc[piece, entry] + recv_x[piece, low + entry].astype(jnp.float32)
            if entries > 1 and entry >= kept:
                send_x[piece, low + entries + entry - kept] = value.astype(jnp.bfloat16)
            else:
                acc[piece, entry] = value
        if level + 1 < lower:
            send_level(piece, level + 1)

    across, around = {}, {}

    def send_z(chunk):
        for side in range(2):
            zsend[chunk, pl.ds(side * half, half)] = acc[2 * chunk + side, 0].astype(jnp.bfloat16)
            zown[chunk, pl.ds(side * half, half)] = acc[2 * chunk + side, 0]
        across[chunk] = [
            copies.start(
                zsend.at[chunk, pl.ds(((here + step) % groups) * share, share)],
                zrecv.at[chunk, step - 1],
                {"vars": (here + step) % groups},
            )
            for step in range(1, groups)
        ]

    def sum_z(chunk):
        for copy in across[chunk]:
            copy.wait_recv()
        value = zown[chunk, pl.ds(here * share, share)]
        for step in range(1, groups):
            value = value + zrecv[chunk, step - 1].astype(jnp.float32)
        total[chunk, pl.ds(here * share, share)] = value.astype(jnp.bfloat16)
        back = share
        if chunk == CHUNKS - 1:
            back = share - 1
            slot_ref[dp] = value[share - 1]
        around[chunk] = [
            copies.start(
                total.at[chunk, pl.ds(here * share, back)],
                total.at[chunk, pl.ds(here * share, back)],
                {"vars": (here + step) % groups},
            )
            for step in range(1, groups)
        ]

    def finish(chunk):
        for copy in around[chunk]:
            copy.wait_recv()
        if chunk < CHUNKS - 1:
            sum_ref[pl.ds(chunk * CHUNK, CHUNK)] = total[chunk].astype(jnp.float32)
        else:
            for group in range(groups):
                place = pl.ds(chunk * CHUNK + group * (share - 1), share - 1)
                sum_ref[place] = total[chunk, pl.ds(group * share, share - 1)].astype(jnp.float32)

    def pieces(act):
        def both(chunk):
            act(2 * chunk)
            act(2 * chunk + 1)

        return both

    stages = [pieces(first)]
    stages += [pieces(lambda piece, level=level: later(piece, level)) for level in range(lower)]
    stages += [send_z, sum_z, finish]
    slot_steps = None
    for tick in range(CHUNKS + len(stages) - 1):
        for stage in reversed(range(len(stages))):
            chunk = tick - stage
            if 0 <= chunk < CHUNKS:
                stages[stage](chunk)
        next(vec_steps, None)
        if tick == CHUNKS + len(stages) - 3:
            slot_steps = spread_steps(copies, slot_ref, dp, bits)
            next(slot_steps)
    for _ in vec_steps:
        pass
    for _ in slot_steps:
        pass
    for copy in field_copies:
        copy.wait_recv()
    copies.finish()


def reduce_all(count, groups, grads, vec, field):
    bits = count.bit_length() - 1
    lower = bits - 1
    rows = grads.shape[2]
    half = CHUNK // 2
    pieces = 2 * CHUNKS
    share = CHUNK // groups
    copies = (groups - 1) * (2 + 2 * CHUNKS) + pieces * bits + 2 * (count - 1)
    bfloat = jnp.bfloat16
    vmem = pl.BlockSpec(memory_space=pltpu.VMEM)
    grads = grads.reshape(count // 2, 2, CHUNKS * CHUNK, rows, WIDTH)
    return pl.pallas_call(
        functools.partial(reduce_kernel, count, groups),
        out_shape=(
            jax.ShapeDtypeStruct((CHUNKS * CHUNK - groups, rows, WIDTH), jnp.float32),
            jax.ShapeDtypeStruct((count, rows, WIDTH), jnp.float32),
            jax.ShapeDtypeStruct((count, groups) + vec.shape, jnp.float32),
            jax.ShapeDtypeStruct(field.shape, field.dtype),
        ),
        in_specs=[vmem] * 3,
        out_specs=(vmem,) * 4,
        scratch_shapes=[
            pltpu.VMEM((pieces, count // 2, half, rows, WIDTH), bfloat),
            pltpu.VMEM((pieces, count // 4, half, rows, WIDTH), jnp.float32),
            pltpu.VMEM((pieces, count // 2 - 1, half, rows, WIDTH), bfloat),
            pltpu.VMEM((pieces, count // 2 - 1, half, rows, WIDTH), bfloat),
            pltpu.VMEM((CHUNKS, CHUNK, rows, WIDTH), bfloat),
            pltpu.VMEM((CHUNKS, groups - 1, share, rows, WIDTH), bfloat),
            pltpu.VMEM((CHUNKS, CHUNK, rows, WIDTH), jnp.float32),
            pltpu.VMEM((CHUNKS, CHUNK, rows, WIDTH), bfloat),
            pltpu.SemaphoreType.DMA((copies,)),
            pltpu.SemaphoreType.DMA((copies,)),
        ],
        compiler_params=pltpu.CompilerParams(
            collective_id=0, has_side_effects=True, vmem_limit_bytes=60 << 20
        ),
    )(grads, vec, field)


def pack_rows(matrix, count, rows):
    own = matrix.shape[0] // count
    blocks = matrix.reshape(count, own, matrix.shape[1] // WIDTH, WIDTH)
    blocks = jnp.transpose(blocks, (0, 2, 1, 3)).astype(jnp.bfloat16)
    return jnp.pad(blocks, ((0, 0), (0, 0), (0, rows - own), (0, 0)))


def pack_slots(grad_slot, count, groups, rows):
    flat = grad_slot.reshape(groups, -1, WIDTH)
    own = -(-flat.shape[1] // count)
    flat = jnp.pad(flat, ((0, 0), (0, own * count - flat.shape[1]), (0, 0)))
    flat = jnp.transpose(flat.reshape(groups, count, own, WIDTH), (1, 0, 2, 3))
    return jnp.pad(flat.astype(jnp.bfloat16), ((0, 0), (0, 0), (0, rows - own), (0, 0)))


def unpack_slots(blocks, shape):
    flat = math.prod(shape) // WIDTH
    own = -(-flat // blocks.shape[0])
    return blocks[:, :own].reshape(-1, WIDTH)[:flat].reshape(shape)


def unpack_columns(blocks, own):
    return jnp.transpose(blocks[:, :own], (1, 0, 2)).reshape(own, -1)


def on_device(
    fields,
    var_ids,
    segments,
    condition,
    cotangent,
    slot_weights,
    slot_momentum,
    slot_average,
    square,
    square_momentum,
    square_average,
    wide,
    wide_momentum,
    wide_average,
    mlp,
    mlp_momentum,
    mlp_average,
    vectors,
    vectors_momentum,
    vectors_average,
):
    bfloat = jnp.bfloat16
    length = fields.shape[4]
    scale = HDIM ** (-0.5)
    square_full, wide_full, mlp_full = (
        lax.all_gather(square.astype(bfloat), "dp", axis=1, tiled=True),
        lax.all_gather(wide.astype(bfloat), "dp", axis=0, tiled=True),
        lax.all_gather(mlp.astype(bfloat), "dp", axis=1, tiled=True),
    )
    key_weight, value_weight, out_weight, proj_weight = (
        square_full[0],
        square_full[1],
        square_full[2],
        square_full[3],
    )
    qkv_weight = wide_full[:, : 3 * D]
    ada_weight = wide_full[:, 3 * D :]
    up_weight, down_weight = (mlp_full[0], mlp_full[1])
    key_vectors = (
        jnp.einsum(
            "dhk,hk->dh",
            key_weight.astype(jnp.float32).reshape(D, HEADS, HDIM),
            vectors[0].reshape(HEADS, HDIM),
            precision=HIGHEST,
        )
        .astype(bfloat)
        .astype(jnp.float32)
    )
    value_float = value_weight.astype(jnp.float32)
    slots_all = lax.all_gather(slot_weights, "vars", axis=0, tiled=True)
    valid = lax.all_gather(var_ids, "vars", axis=0, tiled=True) < NVARS
    own_fields = lax.all_to_all(fields[:, 0], "vars", split_axis=1, concat_axis=0, tiled=True)
    patches = jnp.transpose(own_fields[:, 0], (1, 0, 2)).astype(jnp.float32)
    score_map = jnp.einsum("vpd,dh->pvh", slots_all, key_vectors, precision=HIGHEST)
    value_map = jnp.einsum("vpd,de->pve", slots_all, value_float, precision=HIGHEST)
    value_map = value_map.reshape(value_map.shape[:2] + (HEADS, HDIM))
    full, probs_pool, mixed, mean_own = pool_forward(patches, score_map, value_map, valid)
    pooled_low = (mean_own + vectors[1]).astype(bfloat)
    start = jnp.dot(pooled_low, out_weight, preferred_element_type=jnp.float32) + vectors[2]
    cond_low = jax.nn.silu(condition[0, 0].astype(jnp.float32)).astype(bfloat)
    cond_float = cond_low.astype(jnp.float32)
    modulation = jnp.dot(cond_low[None], ada_weight, preferred_element_type=jnp.float32)[
        0
    ] + vectors[5:].reshape(-1)
    modulation = modulation.reshape(6, D)
    shift_one, scale_one, gate_one = (modulation[0], modulation[1], modulation[2])
    shift_two, scale_two, gate_two = (modulation[3], modulation[4], modulation[5])
    normed_one, inverse_one = normalize(start)
    input_one = (normed_one * (1.0 + scale_one) + shift_one).astype(bfloat)
    triple = jnp.dot(input_one, qkv_weight, preferred_element_type=jnp.float32).astype(bfloat)
    queries = triple[:, :D].reshape(length, HEADS, HDIM)
    keys = triple[:, D : 2 * D].reshape(length, HEADS, HDIM)
    values = triple[:, 2 * D :].reshape(length, HEADS, HDIM)
    segment = segments[0, 0]
    same = segment[:, None] == segment[None, :]
    raw = jnp.einsum("shk,thk->hst", queries, keys, preferred_element_type=jnp.float32)
    logits = jnp.where(same[None], raw * scale, NEGATIVE)
    top = jnp.max(logits, axis=-1, keepdims=True)
    weights = jnp.exp(logits - top)
    total = jnp.sum(weights, axis=-1, keepdims=True)
    log_total = top + jnp.log(total)
    probs = weights / total
    attended = (
        jnp.einsum("hst,thk->shk", probs.astype(bfloat), values, preferred_element_type=jnp.float32)
        .reshape(length, D)
        .astype(bfloat)
    )
    att_branch = jnp.dot(attended, proj_weight, preferred_element_type=jnp.float32) + vectors[3]
    middle = start + gate_one * att_branch
    normed_two, inverse_two = normalize(middle)
    input_two = (normed_two * (1.0 + scale_two) + shift_two).astype(bfloat)
    up = jnp.dot(input_two, up_weight, preferred_element_type=jnp.float32)
    activation, gelu_back = jax.vjp(jax.nn.gelu, up)
    activation = activation.astype(bfloat)
    mlp_branch = contract_cols(activation, down_weight) + vectors[4]
    result = middle + gate_two * mlp_branch
    block_out = result.astype(bfloat)[None, None]
    tokens_all = lax.axis_size("vars") * lax.axis_size("dp") * length
    grad_result = cotangent[0, 0].astype(jnp.float32) * (1.0 / math.sqrt(tokens_all))
    grad_gate_two = jnp.sum(grad_result * mlp_branch, axis=0)
    grad_mlp_branch = (grad_result * gate_two).astype(bfloat)
    grad_down_bias = jnp.sum(grad_mlp_branch.astype(jnp.float32), axis=0)
    grad_down = contract_rows(grad_mlp_branch, activation)
    grad_activation = jnp.dot(grad_mlp_branch, down_weight, preferred_element_type=jnp.float32)
    grad_up = gelu_back(grad_activation)[0].astype(bfloat)
    grad_up_weight = contract_rows(input_two, grad_up)
    grad_input_two = contract_cols(grad_up, up_weight)
    grad_scale_two = jnp.sum(grad_input_two * normed_two, axis=0)
    grad_shift_two = jnp.sum(grad_input_two, axis=0)
    grad_middle = grad_result + normalize_back(
        grad_input_two * (1.0 + scale_two), normed_two, inverse_two
    )
    grad_gate_one = jnp.sum(grad_middle * att_branch, axis=0)
    grad_att_branch = (grad_middle * gate_one).astype(bfloat)
    grad_proj_bias = jnp.sum(grad_att_branch.astype(jnp.float32), axis=0)
    grad_proj = contract_rows(attended, grad_att_branch)
    grad_attended = (
        contract_cols(grad_att_branch, proj_weight).astype(bfloat).reshape(length, HEADS, HDIM)
    )
    again = jnp.exp(logits - log_total)
    grad_probs = jnp.einsum(
        "shk,thk->hst", grad_attended, values, preferred_element_type=jnp.float32
    )
    grad_values = jnp.einsum(
        "hst,shk->thk", again.astype(bfloat), grad_attended, preferred_element_type=jnp.float32
    )
    inner = jnp.sum(again * grad_probs, axis=-1, keepdims=True)
    grad_raw = (again * (grad_probs - inner) * scale).astype(bfloat)
    grad_queries = jnp.einsum("hst,thk->shk", grad_raw, keys, preferred_element_type=jnp.float32)
    grad_keys = jnp.einsum("hst,shk->thk", grad_raw, queries, preferred_element_type=jnp.float32)
    grad_triple = jnp.concatenate(
        [
            grad_queries.reshape(length, D),
            grad_keys.reshape(length, D),
            grad_values.reshape(length, D),
        ],
        axis=1,
    ).astype(bfloat)
    grad_qkv = contract_rows(input_one, grad_triple)
    grad_input_one = contract_cols(grad_triple, qkv_weight)
    grad_scale_one = jnp.sum(grad_input_one * normed_one, axis=0)
    grad_shift_one = jnp.sum(grad_input_one, axis=0)
    grad_start = grad_middle + normalize_back(
        grad_input_one * (1.0 + scale_one), normed_one, inverse_one
    )
    grad_modulation = jnp.stack(
        [
            grad_shift_one,
            grad_scale_one,
            grad_gate_one,
            grad_shift_two,
            grad_scale_two,
            grad_gate_two,
        ]
    )
    grad_start_low = grad_start.astype(bfloat)
    grad_out_weight = contract_rows(pooled_low, grad_start_low)
    grad_out_bias = jnp.sum(grad_start_low.astype(jnp.float32), axis=0)
    grad_pooled = contract_cols(grad_start_low, out_weight).astype(bfloat)
    grad_value_bias = jnp.sum(grad_pooled.astype(jnp.float32), axis=0)
    grad_map, grad_key, field = pool_backward(
        full, probs_pool, mixed, mean_own, score_map, value_map, grad_pooled
    )
    grad_value_weight = jnp.einsum("vpd,pve->de", slots_all, grad_map, precision=HIGHEST)
    grad_key_vectors = jnp.einsum("vpd,pvh->dh", slots_all, grad_key, precision=HIGHEST)
    grad_slot = jnp.einsum("pve,de->vpd", grad_map, value_float, precision=HIGHEST) + jnp.einsum(
        "pvh,dh->vpd", grad_key, key_vectors, precision=HIGHEST
    )
    query_heads = vectors[0].reshape(HEADS, HDIM)
    grad_query = jnp.einsum(
        "dhk,dh->hk",
        key_weight.astype(jnp.float32).reshape(D, HEADS, HDIM),
        grad_key_vectors,
        precision=HIGHEST,
    ).reshape(D)
    count, groups = lax.axis_size("dp"), lax.axis_size("vars")
    own = square.shape[1]
    rows = -(-own // 16) * 16
    pack = functools.partial(pack_rows, count=count, rows=rows)
    spread = jnp.pad(grad_key_vectors, ((0, 0), (0, 2 * WIDTH - HEADS)))
    mixture = jnp.concatenate([grad_out_weight, grad_value_weight, spread], axis=1)
    slots_packed = pack_slots(grad_slot, count, groups, rows)
    mixture = pack(mixture).reshape(count, groups, 2, rows, WIDTH)
    mixture = jnp.concatenate([mixture, slots_packed[:, :, None]], axis=2)
    grads = jnp.concatenate(
        [
            pack(grad_up_weight),
            pack(grad_down),
            pack(grad_qkv),
            pack(grad_proj),
            mixture.reshape(count, CHUNK, rows, WIDTH),
        ],
        axis=1,
    )
    biases = [grad_query, grad_value_bias, grad_out_bias, grad_proj_bias, grad_down_bias]
    vec = jnp.concatenate(
        [
            jnp.stack(biases),
            grad_modulation,
            cond_float[None],
            jnp.zeros((VEC_ROWS - 12, D), jnp.float32),
        ]
    )
    field = jnp.transpose(field, (1, 0, 2)).reshape(groups, -1, length).astype(bfloat)
    field = jnp.pad(field, ((0, 0), (0, -field.shape[1] % 16), (0, 0)))
    sums, slot_blocks, vec_all, field_back = reduce_all(count, groups, grads, vec, field)
    field_rows = slot_weights.shape[0] * PATCH
    field_back = field_back[:, :field_rows].reshape(groups, -1, PATCH, length)
    field_grad = jnp.transpose(field_back.astype(jnp.float32), (1, 0, 2, 3))[:, None]
    grad_slot = unpack_slots(slot_blocks, slot_weights.shape)
    vec_all = vec_all.reshape(-1, VEC_ROWS, D)
    grad_vectors = jnp.sum(vec_all[:, :11], axis=0)
    first_row = lax.axis_index("dp") * own
    conditions = lax.dynamic_slice_in_dim(vec_all[:, 11], first_row, own, axis=1)
    grad_ada = lax.dot_general(
        conditions,
        vec_all[:, 5:11].reshape(-1, 6 * D),
        (((0,), (0,)), ((), ())),
        precision=HIGHEST,
    )
    take = functools.partial(unpack_columns, own=own)
    grad_mlp = jnp.stack([take(sums[:12]), take(sums[12:24])])
    grad_wide = jnp.concatenate([take(sums[24:33]), grad_ada], axis=1)
    grad_key_own = sums[42, :own, :HEADS]
    grad_key_weight = (grad_key_own[:, :, None] * query_heads[None]).reshape(own, D)
    grad_square = jnp.stack(
        [grad_key_weight, take(sums[39:42]), take(sums[36:39]), take(sums[33:36])]
    )
    slot_out = renew(slot_weights, slot_momentum, slot_average, grad_slot, EMBED_RATE)
    square_out = renew(square, square_momentum, square_average, grad_square, RATE)
    wide_out = renew(wide, wide_momentum, wide_average, grad_wide, RATE)
    mlp_out = renew(mlp, mlp_momentum, mlp_average, grad_mlp, RATE)
    vector_out = renew(vectors, vectors_momentum, vectors_average, grad_vectors, RATE)
    return (
        block_out,
        field_grad,
        slot_out[0],
        slot_out[1],
        slot_out[2],
        slot_out[3],
        square_out[0],
        square_out[1],
        square_out[2],
        square_out[3],
        wide_out[0],
        wide_out[1],
        wide_out[2],
        wide_out[3],
        mlp_out[0],
        mlp_out[1],
        mlp_out[2],
        mlp_out[3],
        vector_out[0],
        vector_out[1],
        vector_out[2],
        vector_out[3],
    )


def solution(mesh):
    placed = (
        P("vars", "dp", None, None, None),
        P("vars"),
        P("dp", "vars", None),
        P("dp", "vars", None),
        P("dp", "vars", None, None),
        P("vars", None, None),
        P("vars", None, None),
        P("vars", None, None),
        P(None, "dp", None),
        P(None, "dp", None),
        P(None, "dp", None),
        P("dp", None),
        P("dp", None),
        P("dp", None),
        P(None, "dp", None),
        P(None, "dp", None),
        P(None, "dp", None),
        P(),
        P(),
        P(),
    )
    return jax.shard_map(
        on_device,
        mesh=mesh,
        in_specs=placed,
        out_specs=(
            P("dp", "vars", None, None),
            P("vars", "dp", None, None, None),
            P("vars", None, None),
            P("vars", None, None),
            P("vars", None, None),
            P("vars", None, None),
            P(None, "dp", None),
            P(None, "dp", None),
            P(None, "dp", None),
            P(None, "dp", None),
            P("dp", None),
            P("dp", None),
            P("dp", None),
            P("dp", None),
            P(None, "dp", None),
            P(None, "dp", None),
            P(None, "dp", None),
            P(None, "dp", None),
            P(),
            P(),
            P(),
            P(),
        ),
        check_vma=False,
    )
```

```python
import functools
import math

import jax
import jax.numpy as jnp
from jax import lax
from jax.experimental import pallas as pl
from jax.experimental.pallas import tpu as pltpu
from jax.sharding import PartitionSpec as P

D = 384
HEADS = 6
HDIM = 64
PATCH = 4
NVARS = 69


NEGATIVE = -1e30
EPSILON = 1e-06
GELU_ROOT = math.sqrt(2.0 / math.pi)
GELU_CUBE = 0.044715
WIDTH = 128
VEC_ROWS = 16
MOMENTUM = 0.9
RATE = 0.05
EMBED_RATE = 0.5
AVERAGE_DECAY = 0.9
HIGHEST = lax.Precision.HIGHEST


def contract_cols(left, right):
    return lax.dot_general(
        left, right, (((1,), (1,)), ((), ())), preferred_element_type=jnp.float32
    )


def renew(weight, momentum, average, gradient, step_rate):
    new_momentum = MOMENTUM * momentum + gradient
    new_weight = weight - step_rate * (gradient + MOMENTUM * new_momentum)
    new_average = AVERAGE_DECAY * average + (1.0 - AVERAGE_DECAY) * new_weight
    return (gradient, new_weight, new_momentum, new_average)


TILE = 256
SLOT_ROWS = 80
AUGMENT = 80
FAR = -1e30


def matmul(left, right):
    return lax.dot_general(
        left, right, (((1,), (0,)), ((), ())), preferred_element_type=jnp.float32
    )


def halves(values):
    high = values.astype(jnp.bfloat16)
    return high, (values - high.astype(jnp.float32)).astype(jnp.bfloat16)


def fold(values):
    total = values[:, :WIDTH]
    for start in range(WIDTH, values.shape[1], WIDTH):
        total = total + values[:, start : start + WIDTH]
    return total


def block_kernel(
    tokens_all,
    groups,
    slots_each,
    ids_ref,
    fields_ref,
    slots_ref,
    mask_ref,
    square_ref,
    qkv_ref,
    mlp_ref,
    cols_ref,
    segment_ref,
    cot_ref,
    out_ref,
    grad_ref,
    slot_ref,
    vec_ref,
    field_ref,
    out_t,
    qkv_t,
    proj_t,
    up_t,
    down_t,
    slots_t,
    value_map,
    value_cols,
    score_map,
    probs,
    pooled,
    start,
    inverse,
    input_one,
    query,
    key,
    key_t,
    value,
    value_t,
    raw,
    mixed,
    log_sum,
    attended,
    input_two,
    active,
    grad_up,
    grad_branch,
    grad_mid,
    grad_att,
    grad_out,
    inner,
    grad_triple,
    map_acc,
    key_acc,
    column_acc,
    keyvec_ref,
    spans_ref,
):
    bfloat, flt = jnp.bfloat16, jnp.float32
    length = cot_ref.shape[0]
    tiles = length // TILE
    depth = D
    each = slots_each
    team_size = raw.shape[1]
    scale = HDIM ** (-0.5)

    def lanes(i):
        return pl.ds(pl.multiple_of(i * TILE, TILE), TILE)

    def column(which):
        return cols_ref[:, which : which + 1]

    out_t[...] = square_ref[2].astype(flt).T.astype(bfloat)
    proj_t[...] = square_ref[3].astype(flt).T.astype(bfloat)
    for block in range(3):
        part = slice(block * depth, (block + 1) * depth)
        qkv_t[part] = qkv_ref[:, part].astype(flt).T.astype(bfloat)
    for block in range(4):
        part = slice(block * depth, (block + 1) * depth)
        up_t[part] = mlp_ref[0, :, part].astype(flt).T.astype(bfloat)
        down_t[part] = mlp_ref[1, :, part].astype(flt).T.astype(bfloat)
    asked = cols_ref[:, 10:11]
    lane = lax.broadcasted_iota(jnp.int32, (depth, WIDTH), 1)
    head_of = lax.broadcasted_iota(jnp.int32, (depth, WIDTH), 0) // HDIM
    asked_high, asked_low = halves(jnp.where(lane == head_of, asked, 0.0))
    keyvec_ref[...] = (
        matmul(square_ref[0], asked_high) + matmul(square_ref[0], asked_low)
    ).astype(bfloat)
    firsts = [ids_ref[0, i * TILE] for i in range(tiles)]
    lasts = [ids_ref[0, (i + 1) * TILE - 1] for i in range(tiles)]
    for i in range(tiles):
        spans_ref[i, 0] = sum((lasts[j] < firsts[i]).astype(jnp.int32) for j in range(tiles))
        spans_ref[i, 1] = sum((firsts[j] <= lasts[i]).astype(jnp.int32) for j in range(tiles))
    slots = slots_ref[...]
    slots_high, slots_low = halves(slots)
    value_weight = square_ref[1]
    value_rows = matmul(slots_high, value_weight) + matmul(slots_low, value_weight)
    score_map[...] = matmul(slots_high, keyvec_ref[...]) + matmul(slots_low, keyvec_ref[...])
    turned_high, turned_low = halves(slots.T)
    slots_t[0] = turned_high
    slots_t[1] = turned_low
    value_turned = value_rows.T
    rows_high, rows_low = halves(value_turned)
    for head in range(HEADS):
        part = slice(head * HDIM, (head + 1) * HDIM)
        value_map[head, :HDIM] = rows_high[part]
        value_map[head, HDIM:] = rows_low[part]
        both = jnp.concatenate([value_turned[part], value_turned[part]], axis=0).T
        high = both.astype(bfloat)
        low = (both - high.astype(flt)).astype(bfloat)
        lane = lax.broadcasted_iota(jnp.int32, both.shape, 1)
        value_cols[head] = jnp.where(lane < HDIM, high.astype(flt), low.astype(flt)).astype(bfloat)
    column_acc[...] = jnp.zeros_like(column_acc)
    map_acc[...] = jnp.zeros_like(map_acc)
    key_acc[...] = jnp.zeros_like(key_acc)
    grad_triple[...] = jnp.zeros_like(grad_triple)

    def fields_at(i):
        return [fields_ref[p, :, lanes(i)].astype(flt) for p in range(PATCH)]

    def score_col(p, head):
        return score_map[p * SLOT_ROWS : (p + 1) * SLOT_ROWS, head : head + 1]

    def mixture(prob, fields):
        return jnp.concatenate([prob * f for f in fields] + [prob], axis=0).astype(bfloat)

    def normalize_cols(values):
        center = values - jnp.mean(values, axis=0, keepdims=True)
        inv = lax.rsqrt(jnp.mean(center * center, axis=0, keepdims=True) + EPSILON)
        return center * inv, inv

    def normalize_cols_back(grad, normed, inv):
        first = jnp.mean(grad, axis=0, keepdims=True)
        second = jnp.mean(grad * normed, axis=0, keepdims=True)
        return inv * (grad - first - normed * second)

    @pl.loop(0, tiles)
    def _(i):
        at = lanes(i)
        fields = fields_at(i)
        for head in range(HEADS):
            score = score_col(PATCH, head) + mask_ref[:, 0:1]
            for p in range(PATCH):
                score = score + score_col(p, head) * fields[p]
            score = score * scale
            weight = jnp.exp(score - jnp.max(score, axis=0, keepdims=True))
            prob = weight / jnp.sum(weight, axis=0, keepdims=True)
            probs[head, :, at] = prob
            both = matmul(value_map[head], mixture(prob, fields))
            part = slice(head * HDIM, (head + 1) * HDIM)
            total = both[:HDIM] + both[HDIM:] + cols_ref[part, 0:1]
            pooled[part, at] = total.astype(bfloat)
        begin = matmul(out_t[...], pooled[:, at]) + column(1)
        start[:, at] = begin
        normed, inv = normalize_cols(begin)
        inverse[0:1, at] = inv
        low = (normed * (1.0 + column(5)) + column(4)).astype(bfloat)
        input_one[:, at] = low
        segment = segment_ref[:, at]
        ident = lax.broadcasted_iota(jnp.int32, (AUGMENT - HDIM, TILE), 0)
        hot = jnp.where(ident == segment, 1.0, 0.0)
        cold = jnp.where((ident != segment) & (ident < 4), FAR, 0.0)
        for head in range(HEADS):
            part = slice(head * HDIM, (head + 1) * HDIM)
            queries = matmul(qkv_t[part], low).astype(bfloat).astype(flt) * scale
            query[head, :, at] = jnp.concatenate([queries, hot], axis=0).astype(bfloat)
            part = slice(depth + head * HDIM, depth + (head + 1) * HDIM)
            keys = matmul(qkv_t[part], low).astype(bfloat)
            key_t[head * HDIM : (head + 1) * HDIM, at] = keys
            long = jnp.concatenate([keys.astype(flt), cold], axis=0)
            key[head, at] = long.T.astype(bfloat)
            part = slice(2 * depth + head * HDIM, 2 * depth + (head + 1) * HDIM)
            values = matmul(qkv_t[part], low).astype(bfloat)
            value[head, at] = values.astype(flt).T.astype(bfloat)
            value_t[head, :HDIM, at] = values
            value_t[head, HDIM:, at] = jnp.ones((AUGMENT - HDIM, TILE), bfloat)

    @pl.loop(0, tiles)
    def _(i):
        at = lanes(i)
        low, high = spans_ref[i, 0], spans_ref[i, 1]

        mixed[...] = jnp.zeros_like(mixed)
        for base in range(0, HEADS, team_size):
            team = range(base, base + team_size)

            def scores(j, tops, team=team, base=base):
                new = []
                for head in team:
                    logits = matmul(key[head, lanes(j)], query[head, :, at])
                    raw[j, head - base] = logits
                    top = jnp.max(logits, axis=0, keepdims=True)
                    new.append(jnp.maximum(tops[head - base], top))
                return tuple(new)

            none = tuple(jnp.full((1, TILE), FAR, flt) for _ in team)
            tops = lax.fori_loop(low, high, scores, none)

            def blend(j, totals, team=team, base=base, tops=tops):
                new = []
                for head in team:
                    weight = jnp.exp(raw[j, head - base] - tops[head - base])
                    new.append(totals[head - base] + jnp.sum(weight, axis=0, keepdims=True))
                    mixed[head] += matmul(value_t[head, :, lanes(j)], weight.astype(bfloat))
                return tuple(new)

            zero = tuple(jnp.zeros((1, TILE), flt) for _ in team)
            totals = lax.fori_loop(low, high, blend, zero)
            for head in team:
                part = slice(head * HDIM, (head + 1) * HDIM)
                whole = mixed[head, :HDIM] / mixed[head, HDIM : HDIM + 1]
                upper, rest = halves(whole)
                attended[part, at] = upper
                grad_out[part, at] = rest
                log_sum[head : head + 1, at] = tops[head - base] + jnp.log(totals[head - base])

    rate = 1.0 / math.sqrt(tokens_all)

    @pl.loop(0, tiles)
    def _(i):
        at = lanes(i)
        att = attended[:, at]
        att_branch = matmul(proj_t[...], att) + column(2)
        mid = start[:, at] + column(6) * att_branch
        normed, inv = normalize_cols(mid)
        low = (normed * (1.0 + column(8)) + column(7)).astype(bfloat)
        input_two[:, at] = low
        out = column(3) + jnp.zeros((depth, TILE), flt)
        for block in range(HEADS):
            part = slice(block * TILE, (block + 1) * TILE)
            up = matmul(up_t[part], low)
            square = up * up
            curve = jnp.tanh(up * (GELU_ROOT + (GELU_ROOT * GELU_CUBE) * square))
            half = 0.5 + 0.5 * curve
            act = (up * half).astype(bfloat)
            active[part, at] = act
            slope = half + (0.5 * up) * (1.0 - curve * curve) * (
                GELU_ROOT + (3.0 * GELU_ROOT * GELU_CUBE) * square
            )
            raw[block // team_size, block % team_size] = slope
            out = out + matmul(mlp_ref[1, :, part], act)
        result = mid + column(9) * out
        rows = pl.ds(pl.multiple_of(i * TILE, TILE), TILE)
        out_ref[rows] = result.T.astype(bfloat)
        grad = cot_ref[rows].astype(flt).T * rate
        column_acc[9] += fold(grad * out)
        low_grad = (grad * column(9)).astype(bfloat)
        grad_branch[:, at] = low_grad
        column_acc[3] += fold(low_grad.astype(flt))
        grad_in = jnp.zeros((depth, TILE), flt)
        for block in range(HEADS):
            part = slice(block * TILE, (block + 1) * TILE)
            ups = (matmul(down_t[part], low_grad) * raw[block // team_size, block % team_size]).astype(bfloat)
            grad_up[part, at] = ups
            grad_in = grad_in + matmul(mlp_ref[0, :, part], ups)
        column_acc[8] += fold(grad_in * normed)
        column_acc[7] += fold(grad_in)
        grad = grad + normalize_cols_back(grad_in * (1.0 + column(8)), normed, inv)
        grad_mid[:, at] = grad
        column_acc[6] += fold(grad * att_branch)
        low_grad = (grad * column(6)).astype(bfloat)
        grad_att[:, at] = low_grad
        column_acc[2] += fold(low_grad.astype(flt))
        grads = matmul(square_ref[3], low_grad)
        low_grad = grads.astype(bfloat)
        whole = att.astype(flt) + grad_out[:, at].astype(flt)
        product = low_grad.astype(flt) * whole
        grad_out[:, at] = low_grad
        for head in range(HEADS):
            part = slice(head * HDIM, (head + 1) * HDIM)
            inner[head : head + 1, at] = jnp.sum(product[part], axis=0, keepdims=True)

    def weight_grad(left, right, rows, base):
        for block in range(0, rows, TILE):
            size = min(TILE, rows - block)
            grads = contract_cols(left[...], right[block : block + size])
            for piece in range(size // WIDTH):
                place = base + block // WIDTH + piece
                grad_ref[place] = grads[:, piece * WIDTH : (piece + 1) * WIDTH].astype(bfloat)

    weight_grad(input_two, grad_up, 4 * depth, 0)
    weight_grad(grad_branch, active, 4 * depth, 12)
    weight_grad(attended, grad_att, depth, 33)

    @pl.loop(0, tiles)
    def _(i):
        at = lanes(i)

        @pl.loop(spans_ref[i, 0], spans_ref[i, 1])
        def _(j):
            to = lanes(j)
            for head in range(HEADS):
                part = slice(head * HDIM, (head + 1) * HDIM)
                queries = query[head, :, at]
                logits = matmul(key[head, to], queries)
                prob = jnp.exp(logits - log_sum[head : head + 1, at])
                grads = grad_out[part, at]
                back = matmul(value[head, to], grads)
                grad_raw = (prob * (back - inner[head : head + 1, at])).astype(bfloat)
                grad_triple[part, at] += matmul(key_t[part, to], grad_raw)
                part = slice(depth + head * HDIM, depth + (head + 1) * HDIM)
                grad_triple[part, to] += contract_cols(queries[:HDIM], grad_raw)
                part = slice(2 * depth + head * HDIM, 2 * depth + (head + 1) * HDIM)
                grad_triple[part, to] += contract_cols(grads, prob.astype(bfloat))

    @pl.loop(0, tiles)
    def _(i):
        at = lanes(i)
        grad_in = jnp.zeros((depth, TILE), flt)
        for block in range(3):
            part = slice(block * depth, (block + 1) * depth)
            grads = grad_triple[part, at]
            if block == 0:
                grads = grads * scale
            grads = grads.astype(bfloat)
            active[part, at] = grads
            grad_in = grad_in + matmul(qkv_ref[:, part], grads)
        inv = inverse[0:1, at]
        begin = start[:, at]
        normed = (begin - jnp.mean(begin, axis=0, keepdims=True)) * inv
        column_acc[5] += fold(grad_in * normed)
        column_acc[4] += fold(grad_in)
        grad = grad_mid[:, at] + normalize_cols_back(grad_in * (1.0 + column(5)), normed, inv)
        low_grad = grad.astype(bfloat)
        attended[:, at] = low_grad
        column_acc[1] += fold(low_grad.astype(flt))
        grads = matmul(square_ref[2], low_grad).astype(bfloat)
        column_acc[0] += fold(grads.astype(flt))
        fields = fields_at(i)
        field_grads = [jnp.zeros((SLOT_ROWS, TILE), flt) for _ in range(PATCH)]
        for head in range(HEADS):
            part = slice(head * HDIM, (head + 1) * HDIM)
            own = grads[part]
            prob = probs[head, :, at]
            cross = matmul(value_cols[head], jnp.concatenate([own, own], axis=0))
            pieces = [cross[p * SLOT_ROWS : (p + 1) * SLOT_ROWS] for p in range(PATCH + 1)]
            along = pieces[PATCH]
            for p in range(PATCH):
                along = along + pieces[p] * fields[p]
            center = jnp.sum(prob * along, axis=0, keepdims=True)
            grad_score = (prob * (along - center) * scale).astype(bfloat).astype(flt)
            for p in range(PATCH):
                field_grads[p] = (
                    field_grads[p] + prob * pieces[p] + grad_score * score_col(p, head)
                )
                key_acc[head, p] += fold(fields[p] * grad_score)
            key_acc[head, PATCH] += fold(grad_score)
            map_acc[part] += contract_cols(own, mixture(prob, fields))
        for group in range(groups):
            pieces = [grad[group * each : (group + 1) * each] for grad in field_grads]
            pieces.append(jnp.zeros((field_ref.shape[1] - PATCH * each, TILE), flt))
            field_ref[group, :, at] = jnp.concatenate(pieces, axis=0).astype(bfloat)

    weight_grad(input_one, active, 3 * depth, 24)
    weight_grad(pooled, attended, depth, 36)
    maps_high, maps_low = halves(map_acc[...])
    value_grad = (
        contract_cols(slots_t[0], maps_high)
        + contract_cols(slots_t[0], maps_low)
        + contract_cols(slots_t[1], maps_high)
    )
    for piece in range(3):
        part = slice(piece * WIDTH, (piece + 1) * WIDTH)
        grad_ref[39 + piece] = value_grad[:, part].astype(bfloat)
    lane = lax.broadcasted_iota(jnp.int32, (SLOT_ROWS, WIDTH), 1)
    keys = []
    for p in range(PATCH + 1):
        rows = jnp.zeros((SLOT_ROWS, WIDTH), flt)
        for head in range(HEADS):
            rows = rows + jnp.where(
                lane == head, jnp.sum(key_acc[head, p], axis=1, keepdims=True), 0.0
            )
        keys.append(rows)
    keys = jnp.concatenate(keys, axis=0)
    keys_high, keys_low = halves(keys)
    key_grad = (
        matmul(slots_t[0], keys_high) + matmul(slots_t[0], keys_low) + matmul(slots_t[1], keys_high)
    )
    grad_ref[42] = key_grad.astype(bfloat)
    grad_ref[43] = jnp.zeros_like(grad_ref[43])
    slot_grad = (
        matmul(value_weight, maps_high)
        + matmul(value_weight, maps_low)
        + contract_cols(keyvec_ref[...], keys_high)
        + contract_cols(keyvec_ref[...], keys_low)
    )
    turned = slot_grad.T
    pairs, rows = slot_ref.shape[1], slot_ref.shape[3]
    size = slot_share((PATCH + 1) * each, 2 * pairs)
    for group in range(groups):
        pieces = [
            turned[p * SLOT_ROWS + group * each : p * SLOT_ROWS + (group + 1) * each][
                :, piece * WIDTH : (piece + 1) * WIDTH
            ]
            for piece in range(3)
            for p in range(PATCH + 1)
        ]
        used = 3 * (PATCH + 1) * each
        pieces.append(jnp.zeros((2 * pairs * size + rows - used, WIDTH), flt))
        flat = jnp.concatenate(pieces, axis=0)
        for block in range(2 * pairs):
            part = flat[block * size : block * size + rows]
            slot_ref[group, block // 2, block % 2] = part.astype(bfloat)
    grad_high, grad_low = halves(key_grad)
    key_turned = square_ref[0].astype(flt).T.astype(bfloat)
    asked = matmul(key_turned, grad_high) + matmul(key_turned, grad_low)
    lane = lax.broadcasted_iota(jnp.int32, (depth, WIDTH), 1)
    head_of = lax.broadcasted_iota(jnp.int32, (depth, WIDTH), 0) // HDIM
    columns = jnp.where(
        lane == 0, jnp.sum(jnp.where(lane == head_of, asked, 0.0), axis=1, keepdims=True), 0.0
    )
    columns = columns + jnp.where(lane == 11, cols_ref[:, 11:12], 0.0)
    for which in range(10):
        columns = columns + jnp.where(
            lane == which + 1, jnp.sum(column_acc[which], axis=1, keepdims=True), 0.0
        )
    vec_ref[...] = columns.T[:VEC_ROWS]


def slot_share(rows, count):
    return -(-3 * rows // count)


def block_step(count, groups, own, each, segment, fields, slots, mask, square, qkv, mlp, cols, cot):
    length = cot.shape[0]
    bfloat, flt = jnp.bfloat16, jnp.float32
    rows = (PATCH + 1) * SLOT_ROWS
    tiles = length // TILE
    block_rows = -(-own // 16) * 16
    field_rows = -(-PATCH * each // 16) * 16
    team_size = HEADS if count * block_rows <= D else HEADS // 2
    vmem = pl.BlockSpec(memory_space=pltpu.VMEM)
    shapes = [
        ((D, D), bfloat),
        ((3 * D, D), bfloat),
        ((D, D), bfloat),
        ((4 * D, D), bfloat),
        ((4 * D, D), bfloat),
        ((2, D, rows), bfloat),
        ((HEADS, 2 * HDIM, rows), bfloat),
        ((HEADS, rows, 2 * HDIM), bfloat),
        ((rows, WIDTH), flt),
        ((HEADS, SLOT_ROWS, length), flt),
        ((D, length), bfloat),
        ((D, length), flt),
        ((8, length), flt),
        ((D, length), bfloat),
        ((HEADS, AUGMENT, length), bfloat),
        ((HEADS, length, AUGMENT), bfloat),
        ((D, length), bfloat),
        ((HEADS, length, HDIM), bfloat),
        ((HEADS, AUGMENT, length), bfloat),
        ((tiles, team_size, TILE, TILE), flt),
        ((HEADS, AUGMENT, TILE), flt),
        ((8, length), flt),
        ((D, length), bfloat),
        ((D, length), bfloat),
        ((4 * D, length), bfloat),
        ((4 * D, length), bfloat),
        ((D, length), bfloat),
        ((D, length), flt),
        ((D, length), bfloat),
        ((D, length), bfloat),
        ((8, length), flt),
        ((3 * D, length), flt),
        ((D, rows), flt),
        ((HEADS, PATCH + 1, SLOT_ROWS, WIDTH), flt),
        ((10, D, WIDTH), flt),
        ((D, WIDTH), bfloat),
    ]
    return pl.pallas_call(
        functools.partial(block_kernel, groups * count * length, groups, each),
        out_shape=(
            jax.ShapeDtypeStruct((length, D), bfloat),
            jax.ShapeDtypeStruct((44, D, WIDTH), bfloat),
            jax.ShapeDtypeStruct((groups, count // 2, 2, block_rows, WIDTH), bfloat),
            jax.ShapeDtypeStruct((VEC_ROWS, D), flt),
            jax.ShapeDtypeStruct((groups, field_rows, length), bfloat),
        ),
        in_specs=[pl.BlockSpec(memory_space=pltpu.SMEM)] + [vmem] * 9,
        out_specs=(vmem,) * 5,
        scratch_shapes=[pltpu.VMEM(shape, dtype) for shape, dtype in shapes]
        + [pltpu.SMEM((tiles, 2), jnp.int32)],
        compiler_params=pltpu.CompilerParams(vmem_limit_bytes=62 << 20),
    )(segment, fields, slots, mask, square, qkv, mlp, cols, segment, cot)


CHUNKS = 4
CHUNK = 12
ORDER = (3, 0, 1, 2)
WIDTH = 128
VEC_ROWS = 16
MESH = pl.DeviceIdType.MESH


def flip(index, mask, bits):
    total = 0
    for bit in range(bits):
        own = (index // 2**bit) % 2
        total = total + (1 - own if (mask >> bit) & 1 else own) * 2**bit
    return total


def rounds_of(bits, backward):
    order = list(range(bits))
    return order[::-1] if backward else order


def mask_of(order, level, entry):
    mask = 0
    for place, bit in enumerate(order[level:]):
        if (entry >> (len(order) - level - 1 - place)) & 1:
            mask |= 1 << bit
    return mask


def greet(dp, here, masks, bits, groups):
    barrier = pltpu.get_barrier_semaphore()
    for mask in masks:
        pl.semaphore_signal(
            barrier, inc=1, device_id={"dp": flip(dp, mask, bits)}, device_id_type=MESH
        )
    for step in range(1, groups):
        pl.semaphore_signal(
            barrier, inc=1, device_id={"vars": (here + step) % groups}, device_id_type=MESH
        )
    pl.semaphore_wait(barrier, len(masks) + groups - 1)


class Copies:
    def __init__(self, send_sem, recv_sem):
        self.send_sem, self.recv_sem = send_sem, recv_sem
        self.started = []

    def start(self, source, target, device):
        place = len(self.started)
        copy = pltpu.make_async_remote_copy(
            src_ref=source,
            dst_ref=target,
            send_sem=self.send_sem.at[place],
            recv_sem=self.recv_sem.at[place],
            device_id=device,
            device_id_type=MESH,
        )
        copy.start()
        self.started.append(copy)
        return copy

    def finish(self):
        for copy in self.started:
            copy.wait_send()


class Spread:
    def __init__(self, copies, refs, dp, bits, order):
        self.copies, self.refs, self.dp, self.bits = copies, refs, dp, bits
        self.order = order
        self.arriving = {}

    def send(self, mask, first):
        block = flip(self.dp, mask, self.bits)
        for level in range(first, len(self.order)):
            bit = self.order[level]
            partner = {"dp": flip(self.dp, 1 << bit, self.bits)}
            for ref in self.refs:
                copy = self.copies.start(ref(block), ref(block), partner)
                self.arriving.setdefault(level, []).append((mask | (1 << bit), copy))

    def begin(self):
        self.send(0, 0)

    def advance(self, level):
        for place, (mask, copy) in enumerate(self.arriving[level]):
            copy.wait_recv()
            if place % len(self.refs) == len(self.refs) - 1:
                self.send(mask, level + 1)


def reduce_kernel(
    count,
    groups,
    g_ref,
    s_ref,
    vec_ref,
    field_ref,
    total,
    slot_ref,
    vec_all,
    field_out,
    recv0,
    acc,
    send_x,
    recv_x,
    zsend,
    zrecv,
    zkeep,
    ysend,
    yrecv,
    send_sem,
    recv_sem,
):
    bits = count.bit_length() - 1
    lower = bits - 1
    dp, here = lax.axis_index("dp"), lax.axis_index("vars")
    core, pair = dp % 2, dp // 2
    greet(dp, here, [1 << bit for bit in range(bits)], bits, groups)
    copies = Copies(send_sem, recv_sem)
    half = CHUNK // 2
    share = CHUNK // groups
    other = {"dp": dp + 1 - 2 * core}

    def grads_at(piece):
        if piece < 2 * CHUNKS - 2:
            return piece * half, half
        size = half - groups // 2
        return (2 * CHUNKS - 2) * half + (piece % 2) * size, size

    vec_copies = [
        copies.start(vec_ref, vec_all.at[dp, here], {"vars": (here + step) % groups})
        for step in range(1, groups)
    ]
    vec_all[dp, here] = vec_ref[...]
    level0 = {}
    for chunk in ORDER:
        for side in range(2):
            piece = 2 * chunk + side
            base, size = grads_at(piece)
            level0[piece] = [
                copies.start(
                    g_ref.at[pl.ds(base, size), :, 1 - core],
                    recv0.at[piece, pl.ds(0, size)],
                    other,
                )
            ]
            if size < half:
                level0[piece].append(
                    copies.start(
                        s_ref.at[pl.ds(side * (half - size), half - size), :, 1 - core],
                        recv0.at[piece, pl.ds(size, half - size)],
                        other,
                    )
                )
    field_copies = [
        copies.start(
            field_ref.at[(here + step) % groups],
            field_out.at[here],
            {"vars": (here + step) % groups},
        )
        for step in range(1, groups)
    ]
    field_out[here] = field_ref[here]
    forth = list(range(1, bits)) + [0]
    vecs = Spread(copies, [lambda block: vec_all.at[block]], dp, bits, forth)
    slots = Spread(copies, [lambda block: slot_ref.at[block]], dp, bits, forth)

    def vec_begin():
        for copy in vec_copies:
            copy.wait_recv()
        vecs.begin()

    crossing = {}

    def send_level(piece, level):
        order = rounds_of(lower, piece % 2)
        entries = 2 ** (lower - 1 - level)
        low = 2**lower - 2 ** (lower - level)
        partner = {"dp": 2 * flip(pair, 1 << order[level], lower) + core}
        crossing[piece, level] = copies.start(
            send_x.at[piece, pl.ds(low, entries)],
            recv_x.at[piece, pl.ds(low, entries)],
            partner,
        )

    def first(piece):
        order = rounds_of(lower, piece % 2)
        for copy in level0[piece]:
            copy.wait_recv()
        base, size = grads_at(piece)
        kept = 2 ** (lower - 1)
        for entry in range(2**lower):
            block = flip(pair, mask_of(order, 0, entry), lower)
            value = g_ref[pl.ds(base, size), block, core].astype(jnp.float32)
            value = value + recv0[piece, pl.ds(0, size), block].astype(jnp.float32)
            if size < half:
                rest = half - size
                slots = s_ref[pl.ds((piece % 2) * rest, rest), block, core].astype(jnp.float32)
                slots = slots + recv0[piece, pl.ds(size, rest), block].astype(jnp.float32)
                value = jnp.concatenate([value[:2], slots[:1], value[2:], slots[1:]], axis=0)
            if entry < kept:
                acc[piece, entry] = value
            else:
                send_x[piece, entry - kept] = value.astype(jnp.bfloat16)
        send_level(piece, 0)

    def later(piece, level):
        crossing[piece, level].wait_recv()
        entries = 2 ** (lower - 1 - level)
        low = 2**lower - 2 ** (lower - level)
        kept = entries // 2
        for entry in range(entries):
            value = acc[piece, entry] + recv_x[piece, low + entry].astype(jnp.float32)
            if entries > 1 and entry >= kept:
                send_x[piece, low + entries + entry - kept] = value.astype(jnp.bfloat16)
            else:
                acc[piece, entry] = value
        if level + 1 < lower:
            send_level(piece, level + 1)

    near = {"vars": here + 1 - 2 * (here % 2)}
    far = {"vars": (here + 2) % groups}
    low, top = here % 2, here // 2
    across, over, around, forward = {}, {}, {}, {}

    def send_near(piece):
        zsend[piece] = acc[piece, 0, pl.ds(share * (1 - low), share)].astype(jnp.bfloat16)
        across[piece] = copies.start(zsend.at[piece], zrecv.at[piece], near)

    def sum_near(piece):
        across[piece].wait_recv()
        own = acc[piece, 0, pl.ds(share * low, share)]
        zkeep[piece] = own + zrecv[piece].astype(jnp.float32)

    def send_far(chunk):
        for side in range(2):
            sum_near(2 * chunk + side)
        ysend[chunk] = zkeep[2 * chunk + 1 - top].astype(jnp.bfloat16)
        over[chunk] = copies.start(ysend.at[chunk], yrecv.at[chunk], far)

    def quarter(chunk, which):
        count_back = share - 1 if chunk == CHUNKS - 1 else share
        return total.at[chunk, which, pl.ds(0, count_back)]

    def sum_far(chunk):
        over[chunk].wait_recv()
        value = zkeep[2 * chunk + top] + yrecv[chunk].astype(jnp.float32)
        total[chunk, here] = value.astype(jnp.bfloat16)
        if chunk == CHUNKS - 1:
            slot_ref[dp] = value[share - 1]
        around[chunk] = [
            copies.start(quarter(chunk, here), quarter(chunk, here), to) for to in (far, near)
        ]

    def pass_on(chunk):
        around[chunk][0].wait_recv()
        other_quarter = quarter(chunk, (here + 2) % groups)
        forward[chunk] = copies.start(other_quarter, other_quarter, near)

    def finish(chunk):
        around[chunk][1].wait_recv()
        forward[chunk].wait_recv()

    def pieces(act):
        def both(chunk):
            act(2 * chunk)
            act(2 * chunk + 1)

        return both

    stages = [pieces(first)]
    stages += [pieces(lambda piece, level=level: later(piece, level)) for level in range(lower)]
    stages += [pieces(send_near), send_far, sum_far, pass_on, finish]
    extra = {1: [vec_begin], len(stages) - 3: [slots.begin]}
    for level in range(bits):
        tick = min(3 + 2 * level, CHUNKS + len(stages) - 2)
        extra.setdefault(tick, []).append(functools.partial(vecs.advance, level))
        tick = min(len(stages) - 1 + level, CHUNKS + len(stages) - 2)
        extra.setdefault(tick, []).append(functools.partial(slots.advance, level))
    for tick in range(CHUNKS + len(stages) - 1):
        for stage in reversed(range(len(stages))):
            place = tick - stage
            if 0 <= place < CHUNKS:
                stages[stage](ORDER[place])
        for act in extra.get(tick, ()):
            act()
    for copy in field_copies:
        copy.wait_recv()
    copies.finish()


def reduce_all(count, groups, grads, slots, vec, field):
    bits = count.bit_length() - 1
    lower = bits - 1
    rows = grads.shape[3]
    half = CHUNK // 2
    pieces = 2 * CHUNKS
    share = CHUNK // groups
    copies = 2 * (groups - 1) + pieces * (bits + 1) + 4 * CHUNKS + 2 + 2 * (count - 1)
    bfloat = jnp.bfloat16
    vmem = pl.BlockSpec(memory_space=pltpu.VMEM)
    return pl.pallas_call(
        functools.partial(reduce_kernel, count, groups),
        out_shape=(
            jax.ShapeDtypeStruct((CHUNKS, groups, share, rows, WIDTH), bfloat),
            jax.ShapeDtypeStruct((count, rows, WIDTH), jnp.float32),
            jax.ShapeDtypeStruct((count, groups) + vec.shape, jnp.float32),
            jax.ShapeDtypeStruct(field.shape, field.dtype),
        ),
        in_specs=[vmem] * 4,
        out_specs=(vmem,) * 4,
        scratch_shapes=[
            pltpu.VMEM((pieces, half, count // 2, rows, WIDTH), bfloat),
            pltpu.VMEM((pieces, count // 4, half, rows, WIDTH), jnp.float32),
            pltpu.VMEM((pieces, count // 2 - 1, half, rows, WIDTH), bfloat),
            pltpu.VMEM((pieces, count // 2 - 1, half, rows, WIDTH), bfloat),
            pltpu.VMEM((pieces, share, rows, WIDTH), bfloat),
            pltpu.VMEM((pieces, share, rows, WIDTH), bfloat),
            pltpu.VMEM((pieces, share, rows, WIDTH), jnp.float32),
            pltpu.VMEM((CHUNKS, share, rows, WIDTH), bfloat),
            pltpu.VMEM((CHUNKS, share, rows, WIDTH), bfloat),
            pltpu.SemaphoreType.DMA((copies,)),
            pltpu.SemaphoreType.DMA((copies,)),
        ],
        compiler_params=pltpu.CompilerParams(
            collective_id=0, has_side_effects=True, vmem_limit_bytes=60 << 20
        ),
    )(grads, slots, vec, field)


def pack_rows(blocks, count, rows):
    own = blocks.shape[1] // count
    blocks = blocks.reshape(blocks.shape[0], count // 2, 2, own, WIDTH)
    return jnp.pad(blocks, ((0, 0), (0, 0), (0, 0), (0, rows - own), (0, 0)))


def renew_into(outs, refs, at, gradient, step_rate):
    new = renew(*(ref[at] for ref in refs), gradient, step_rate)
    for out, value in zip(outs, new):
        out[at] = value


def update_kernel(groups, sum_ref, slot_ref, vec_ref, *refs):
    flt = jnp.float32
    slot_in, square_in, wide_in, mlp_in, vector_in = (refs[3 * i : 3 * i + 3] for i in range(5))
    refs = refs[15:]
    slot_out, square_out, wide_out, mlp_out, vector_out = (
        refs[4 * i : 4 * i + 4] for i in range(5)
    )
    own = wide_in[0].shape[0]
    bfloat = jnp.bfloat16
    last = CHUNKS - 1

    def block(place):
        if place < last * CHUNK:
            chunk, rest = divmod(place, CHUNK)
            share = CHUNK // groups
        else:
            chunk, rest, share = last, place - last * CHUNK, CHUNK // groups - 1
        return sum_ref[chunk, rest // share, rest % share, :own]

    for place in range(12):
        part = (slice(None), slice(place * WIDTH, (place + 1) * WIDTH))
        for half in range(2):
            grads = block(12 * half + place).astype(flt)
            renew_into(mlp_out, mlp_in, (half,) + part, grads, RATE)
    for place in range(9):
        part = (slice(None), slice(place * WIDTH, (place + 1) * WIDTH))
        renew_into(wide_out, wide_in, part, block(24 + place).astype(flt), RATE)
    for which, base in ((3, 33), (2, 36), (1, 39)):
        for place in range(3):
            part = (which, slice(None), slice(place * WIDTH, (place + 1) * WIDTH))
            renew_into(square_out, square_in, part, block(base + place).astype(flt), RATE)
    asked = vector_in[0][0:1]
    lane = lax.broadcasted_iota(jnp.int32, (WIDTH, D), 1) // HDIM
    head = lax.broadcasted_iota(jnp.int32, (WIDTH, D), 0)
    asked_high, asked_low = halves(jnp.where(lane == head, asked, 0.0))
    keys = block(42)
    renew_into(
        square_out, square_in, (0,), matmul(keys, asked_high) + matmul(keys, asked_low), RATE
    )
    devices = vec_ref.shape[0]
    pick = lax.broadcasted_iota(jnp.int32, (D, own), 0) == lax.axis_index(
        "dp"
    ) * own + lax.broadcasted_iota(jnp.int32, (D, own), 1)
    conditions = matmul(vec_ref[:, 11, :].astype(bfloat), jnp.where(pick, 1.0, 0.0).astype(bfloat))
    conditions = conditions.T.astype(bfloat)
    for row in range(6):
        high, low = halves(vec_ref[:, 5 + row, :])
        part = (slice(None), slice((3 + row) * D, (4 + row) * D))
        grads = matmul(conditions, high) + matmul(conditions, low)
        renew_into(wide_out, wide_in, part, grads, RATE)
    total = vec_ref[0]
    for device in range(1, devices):
        total = total + vec_ref[device]
    renew_into(vector_out, vector_in, (slice(None),), total[:11], RATE)
    each = slot_in[0].shape[1]
    blocks = slot_ref.shape[0]
    size = slot_share((PATCH + 1) * each, blocks)
    flat = jnp.concatenate([slot_ref[b, :size] for b in range(blocks)], axis=0)
    for p in range(PATCH + 1):
        pieces = [
            flat[(piece * (PATCH + 1) + p) * each : (piece * (PATCH + 1) + p + 1) * each]
            for piece in range(3)
        ]
        renew_into(slot_out, slot_in, (p,), jnp.concatenate(pieces, axis=1), EMBED_RATE)


def update_all(groups, sums, slot_blocks, vec_all, parameters):
    vmem = pl.BlockSpec(memory_space=pltpu.VMEM)
    shapes = [jax.ShapeDtypeStruct(a.shape, a.dtype) for a in parameters[::3] for _ in range(4)]
    return pl.pallas_call(
        functools.partial(update_kernel, groups),
        out_shape=tuple(shapes),
        in_specs=[vmem] * (3 + len(parameters)),
        out_specs=(vmem,) * len(shapes),
        compiler_params=pltpu.CompilerParams(vmem_limit_bytes=60 << 20),
    )(sums, slot_blocks, vec_all, *parameters)


def gather_kernel(
    count,
    groups,
    field_ref,
    slot_ref,
    ident_ref,
    cond_ref,
    square_ref,
    wide_ref,
    mlp_ref,
    vec_ref,
    patch_out,
    slots_out,
    mask_out,
    cols_out,
    square_out,
    qkv_out,
    mlp_out,
    field_all,
    slot_all,
    ident_all,
    cond_all,
    part,
    part_in,
    send_sem,
    recv_sem,
):
    bfloat, flt = jnp.bfloat16, jnp.float32
    bits = count.bit_length() - 1
    dp, here = lax.axis_index("dp"), lax.axis_index("vars")
    own, rows = square_ref.shape[1], square_out.shape[2]
    if own < rows:
        square_out[:, dp] = jnp.zeros_like(square_out[:, dp])
        qkv_out[dp] = jnp.zeros_like(qkv_out[dp])
        mlp_out[:, dp] = jnp.zeros_like(mlp_out[:, dp])
    square_out[:, dp, :own] = square_ref[...].astype(bfloat)
    qkv_out[dp, :own] = wide_ref[:, : 3 * D].astype(bfloat)
    mlp_out[:, dp, :own] = mlp_ref[...].astype(bfloat)
    cond_all[dp] = cond_ref[...]
    greet(dp, here, range(1, count), bits, groups)
    copies = Copies(send_sem, recv_sem)
    most = PATCH // 2 + 1
    forth = list(range(1, bits)) + [0]
    back = list(range(1, bits))[::-1] + [0]
    ones = Spread(
        copies,
        [lambda block: square_out.at[:, block], lambda block: qkv_out.at[block]],
        dp,
        bits,
        forth,
    )
    twos = Spread(copies, [lambda block: mlp_out.at[:, block]], dp, bits, back)
    conds = [
        copies.start(cond_ref, cond_all.at[dp], {"dp": (dp + step) % count})
        for step in range(1, count)
    ]
    core = dp % 2
    arrivals, slot_copies = [], []
    sent = pl.ds(core * (PATCH + 1 - most), most)
    for step in range(1, groups):
        to = {"vars": (here + step) % groups}
        arrivals.append(copies.start(ident_ref, ident_all.at[here], to))
        slot_copies.append(copies.start(slot_ref.at[sent], slot_all.at[here, sent], to))
    ones.begin()
    twos.begin()
    for step in range(1, groups):
        to = (here + step) % groups
        arrivals.append(copies.start(field_ref.at[to], field_all.at[here], {"vars": to}))
    field_all[here] = field_ref[here]
    slot_all[here] = slot_ref[...]
    ident_all[here] = ident_ref[...]
    for copy in conds:
        copy.wait_recv()
    cond = cond_all[:, 0, :].astype(bfloat)
    pick = lax.broadcasted_iota(jnp.int32, (D, own), 0) == dp * own + lax.broadcasted_iota(
        jnp.int32, (D, own), 1
    )
    cond_rows = matmul(cond, jnp.where(pick, 1.0, 0.0).astype(bfloat)).astype(bfloat)
    shares = matmul(cond_rows, wide_ref[:, 3 * D :].astype(bfloat))
    strips = shares.shape[1] // WIDTH
    for block in range(count):
        for strip in range(strips):
            part[block, strip : strip + 1] = shares[
                block : block + 1, strip * WIDTH : (strip + 1) * WIDTH
            ]
    part_copies = [
        copies.start(part.at[(dp + step) % count], part_in.at[step - 1], {"dp": (dp + step) % count})
        for step in range(1, count)
    ]
    ones.advance(0)
    twos.advance(0)
    fewer = PATCH + 1 - most
    given = pl.ds(core * most, fewer)
    for step, copy in enumerate(slot_copies, 1):
        copy.wait_recv()
        block = slot_all.at[(here - step + groups) % groups, given]
        arrivals.append(copies.start(block, block, {"dp": dp + 1 - 2 * core}))
    for level in range(1, bits):
        ones.advance(level)
        twos.advance(level)
    for copy in part_copies:
        copy.wait_recv()
    mine = part[dp]
    for step in range(1, count):
        mine = mine + part_in[step - 1]
    wide_parts = [
        jnp.concatenate([mine[3 * row + strip : 3 * row + strip + 1] for strip in range(3)], axis=1)
        for row in range(6)
    ]
    modulation = jnp.concatenate(wide_parts, axis=0) + vec_ref[5:11]
    columns = jnp.concatenate(
        [
            vec_ref[1:5],
            modulation,
            vec_ref[0:1],
            cond_ref[0:1],
            jnp.zeros((WIDTH - 12, D), flt),
        ],
        axis=0,
    )
    cols_out[...] = columns.T
    for copy in arrivals:
        copy.wait_recv()
    each = slot_ref.shape[1]
    spare = SLOT_ROWS - groups * each
    for p in range(PATCH):
        pieces = [
            field_all[source, p * each : (p + 1) * each].astype(flt) for source in range(groups)
        ]
        pieces.append(jnp.zeros((spare, field_ref.shape[2]), flt))
        patch_out[p] = jnp.concatenate(pieces, axis=0).astype(bfloat)
    for p in range(PATCH + 1):
        pieces = [slot_all[source, p] for source in range(groups)]
        pieces.append(jnp.zeros((spare, D), flt))
        slots_out[p * SLOT_ROWS : (p + 1) * SLOT_ROWS] = jnp.concatenate(pieces, axis=0)
    pieces = [ident_all[source, :each] for source in range(groups)]
    pieces.append(jnp.full((spare, WIDTH), float(NVARS), flt))
    mask_out[...] = jnp.where(jnp.concatenate(pieces, axis=0) < NVARS, 0.0, FAR)
    copies.finish()


def gather_all(count, groups, field, slots, ident, cond, square, wide, mlp, vectors):
    bits = count.bit_length() - 1
    own = square.shape[1]
    rows = -(-own // 16) * 16
    bfloat, flt = jnp.bfloat16, jnp.float32
    copies = 4 * (groups - 1) + 5 * (count - 1)
    length = field.shape[2]
    strips = (wide.shape[1] - 3 * D) // WIDTH
    vmem = pl.BlockSpec(memory_space=pltpu.VMEM)
    outs = [
        ((PATCH, SLOT_ROWS, length), bfloat),
        (((PATCH + 1) * SLOT_ROWS, D), flt),
        ((SLOT_ROWS, WIDTH), flt),
        ((D, WIDTH), flt),
        ((4, count, rows, D), bfloat),
        ((count, rows, 3 * D), bfloat),
        ((2, count, rows, 4 * D), bfloat),
    ]
    return pl.pallas_call(
        functools.partial(gather_kernel, count, groups),
        out_shape=tuple(jax.ShapeDtypeStruct(shape, dtype) for shape, dtype in outs),
        in_specs=[vmem] * 8,
        out_specs=(vmem,) * len(outs),
        scratch_shapes=[
            pltpu.VMEM((groups,) + field.shape[1:], bfloat),
            pltpu.VMEM((groups,) + slots.shape, flt),
            pltpu.VMEM((groups,) + ident.shape, flt),
            pltpu.VMEM((count, 8, D), flt),
            pltpu.VMEM((count, strips, WIDTH), flt),
            pltpu.VMEM((count - 1, strips, WIDTH), flt),
            pltpu.SemaphoreType.DMA((copies,)),
            pltpu.SemaphoreType.DMA((copies,)),
        ],
        compiler_params=pltpu.CompilerParams(
            collective_id=1, has_side_effects=True, vmem_limit_bytes=60 << 20
        ),
    )(field, slots, ident, cond, square, wide, mlp, vectors)


def on_device(
    fields,
    var_ids,
    segments,
    condition,
    cotangent,
    slot_weights,
    slot_momentum,
    slot_average,
    square,
    square_momentum,
    square_average,
    wide,
    wide_momentum,
    wide_average,
    mlp,
    mlp_momentum,
    mlp_average,
    vectors,
    vectors_momentum,
    vectors_average,
):
    bfloat = jnp.bfloat16
    length = fields.shape[4]
    count, groups = lax.axis_size("dp"), lax.axis_size("vars")
    own = square.shape[1]
    rows = -(-own // 16) * 16
    cond_low = jax.nn.silu(condition[0].astype(jnp.float32)).astype(bfloat).astype(jnp.float32)
    field = jnp.transpose(fields[:, 0], (1, 2, 0, 3)).reshape(groups, -1, length)
    field = jnp.pad(field, ((0, 0), (0, -field.shape[1] % 16), (0, 0)))
    ident = jnp.broadcast_to(var_ids.astype(jnp.float32)[:, None], (slot_weights.shape[0], WIDTH))
    gathered = gather_all(
        count,
        groups,
        field,
        jnp.transpose(slot_weights, (1, 0, 2)),
        ident,
        jnp.broadcast_to(cond_low, (8, D)),
        square,
        wide,
        mlp,
        vectors,
    )
    patches, slot_rows, mask, columns = gathered[:4]
    square_full, qkv_full, mlp_full = (a[..., :own, :] for a in gathered[4:])
    block_out, grads, slots_packed, vec, field = block_step(
        count,
        groups,
        own,
        slot_weights.shape[0],
        segments[0],
        patches,
        slot_rows,
        mask,
        square_full.reshape(4, D, D),
        qkv_full.reshape(D, 3 * D),
        mlp_full.reshape(2, D, 4 * D),
        columns,
        cotangent[0, 0],
    )
    sums, slot_blocks, vec_all, field_back = reduce_all(
        count, groups, pack_rows(grads, count, rows), slots_packed, vec, field
    )
    updated = update_all(
        groups,
        sums,
        slot_blocks,
        vec_all.reshape(-1, VEC_ROWS, D),
        (
            *(jnp.transpose(a, (1, 0, 2)) for a in (slot_weights, slot_momentum, slot_average)),
            square,
            square_momentum,
            square_average,
            wide,
            wide_momentum,
            wide_average,
            mlp,
            mlp_momentum,
            mlp_average,
            vectors,
            vectors_momentum,
            vectors_average,
        ),
    )
    each = slot_weights.shape[0]
    field_back = field_back[:, : PATCH * each].reshape(groups, PATCH, each, length)
    field_grad = jnp.transpose(field_back, (2, 0, 1, 3)).astype(jnp.float32)[:, None]
    slot_new = tuple(jnp.transpose(a, (1, 0, 2)) for a in updated[:4])
    return (block_out[None, None], field_grad) + slot_new + tuple(updated[4:])


def solution(mesh):
    placed = (
        P("vars", "dp", None, None, None),
        P("vars"),
        P("dp", "vars", None),
        P("dp", "vars", None),
        P("dp", "vars", None, None),
        P("vars", None, None),
        P("vars", None, None),
        P("vars", None, None),
        P(None, "dp", None),
        P(None, "dp", None),
        P(None, "dp", None),
        P("dp", None),
        P("dp", None),
        P("dp", None),
        P(None, "dp", None),
        P(None, "dp", None),
        P(None, "dp", None),
        P(),
        P(),
        P(),
    )
    return jax.shard_map(
        on_device,
        mesh=mesh,
        in_specs=placed,
        out_specs=(
            P("dp", "vars", None, None),
            P("vars", "dp", None, None, None),
            P("vars", None, None),
            P("vars", None, None),
            P("vars", None, None),
            P("vars", None, None),
            P(None, "dp", None),
            P(None, "dp", None),
            P(None, "dp", None),
            P(None, "dp", None),
            P("dp", None),
            P("dp", None),
            P("dp", None),
            P("dp", None),
            P(None, "dp", None),
            P(None, "dp", None),
            P(None, "dp", None),
            P(None, "dp", None),
            P(),
            P(),
            P(),
            P(),
        ),
        check_vma=False,
    )
```

```python
import functools
import math

import jax
import jax.numpy as jnp
from jax import lax
from jax.experimental import pallas as pl
from jax.experimental.pallas import tpu as pltpu
from jax.sharding import PartitionSpec as P

D = 384
HEADS = 6
HDIM = 64
PATCH = 4
NVARS = 69


NEGATIVE = -1e30
EPSILON = 1e-06
GELU_ROOT = math.sqrt(2.0 / math.pi)
GELU_CUBE = 0.044715
WIDTH = 128
VEC_ROWS = 16
MOMENTUM = 0.9
RATE = 0.05
EMBED_RATE = 0.5
AVERAGE_DECAY = 0.9
HIGHEST = lax.Precision.HIGHEST


def contract_cols(left, right):
    return lax.dot_general(
        left, right, (((1,), (1,)), ((), ())), preferred_element_type=jnp.float32
    )


def renew(weight, momentum, average, gradient, step_rate):
    new_momentum = MOMENTUM * momentum + gradient
    new_weight = weight - step_rate * (gradient + MOMENTUM * new_momentum)
    new_average = AVERAGE_DECAY * average + (1.0 - AVERAGE_DECAY) * new_weight
    return (gradient, new_weight, new_momentum, new_average)


TILE = 256
SLOT_ROWS = 80
AUGMENT = 80
FAR = -1e30


def matmul(left, right):
    return lax.dot_general(
        left, right, (((1,), (0,)), ((), ())), preferred_element_type=jnp.float32
    )


def halves(values):
    high = values.astype(jnp.bfloat16)
    return high, (values - high.astype(jnp.float32)).astype(jnp.bfloat16)


def fold(values):
    total = values[:, :WIDTH]
    for start in range(WIDTH, values.shape[1], WIDTH):
        total = total + values[:, start : start + WIDTH]
    return total


def block_kernel(
    tokens_all,
    groups,
    slots_each,
    ids_ref,
    fields_ref,
    slots_ref,
    mask_ref,
    square_ref,
    qkv_ref,
    mlp_hbm,
    cols_ref,
    segment_ref,
    cot_hbm,
    out_hbm,
    grad_hbm,
    slot_ref,
    vec_ref,
    field_ref,
    out_t,
    qkv_t,
    proj_t,
    up_t,
    down_t,
    slots_t,
    value_map,
    value_cols,
    score_map,
    probs,
    pooled,
    start,
    inverse,
    input_one,
    query,
    key,
    key_t,
    value,
    value_t,
    raw,
    mixed,
    log_sum,
    attended,
    input_two,
    active,
    grad_up,
    grad_branch,
    grad_mid,
    grad_att,
    grad_out,
    inner,
    grad_triple,
    map_acc,
    key_acc,
    column_acc,
    keyvec_ref,
    mlp_ref,
    cot_ref,
    out_rows,
    grad_rows,
    spans_ref,
    in_sem,
    out_sem,
):
    bfloat, flt = jnp.bfloat16, jnp.float32
    loads = [
        pltpu.make_async_copy(mlp_hbm, mlp_ref, in_sem.at[0]),
        pltpu.make_async_copy(cot_hbm, cot_ref, in_sem.at[1]),
    ]
    for load in loads:
        load.start()
    length = cot_ref.shape[0]
    tiles = length // TILE
    depth = D
    each = slots_each
    team_size = raw.shape[1]
    spread = 2 if team_size == HEADS else 1
    scale = HDIM ** (-0.5)

    def lanes(i):
        return pl.ds(pl.multiple_of(i * TILE, TILE), TILE)

    def column(which):
        return cols_ref[:, which : which + 1]

    out_t[...] = square_ref[2].astype(flt).T.astype(bfloat)
    proj_t[...] = square_ref[3].astype(flt).T.astype(bfloat)
    for block in range(3):
        part = slice(block * depth, (block + 1) * depth)
        qkv_t[part] = qkv_ref[:, part].astype(flt).T.astype(bfloat)
    asked = cols_ref[:, 10:11]
    lane = lax.broadcasted_iota(jnp.int32, (depth, WIDTH), 1)
    head_of = lax.broadcasted_iota(jnp.int32, (depth, WIDTH), 0) // HDIM
    asked_high, asked_low = halves(jnp.where(lane == head_of, asked, 0.0))
    keyvec_ref[...] = (
        matmul(square_ref[0], asked_high) + matmul(square_ref[0], asked_low)
    ).astype(bfloat)
    firsts = [ids_ref[0, i * TILE] for i in range(tiles)]
    lasts = [ids_ref[0, (i + 1) * TILE - 1] for i in range(tiles)]
    for i in range(tiles):
        spans_ref[i, 0] = sum((lasts[j] < firsts[i]).astype(jnp.int32) for j in range(tiles))
        spans_ref[i, 1] = sum((firsts[j] <= lasts[i]).astype(jnp.int32) for j in range(tiles))
    slots = slots_ref[...]
    slots_high, slots_low = halves(slots)
    value_weight = square_ref[1]
    value_rows = matmul(slots_high, value_weight) + matmul(slots_low, value_weight)
    score_map[...] = matmul(slots_high, keyvec_ref[...]) + matmul(slots_low, keyvec_ref[...])
    turned_high, turned_low = halves(slots.T)
    slots_t[0] = turned_high
    slots_t[1] = turned_low
    value_turned = value_rows.T
    rows_high, rows_low = halves(value_turned)
    for head in range(HEADS):
        part = slice(head * HDIM, (head + 1) * HDIM)
        value_map[head, :HDIM] = rows_high[part]
        value_map[head, HDIM:] = rows_low[part]
        both = jnp.concatenate([value_turned[part], value_turned[part]], axis=0).T
        high = both.astype(bfloat)
        low = (both - high.astype(flt)).astype(bfloat)
        lane = lax.broadcasted_iota(jnp.int32, both.shape, 1)
        value_cols[head] = jnp.where(lane < HDIM, high.astype(flt), low.astype(flt)).astype(bfloat)
    column_acc[...] = jnp.zeros_like(column_acc)
    map_acc[...] = jnp.zeros_like(map_acc)
    key_acc[...] = jnp.zeros_like(key_acc)
    grad_triple[...] = jnp.zeros_like(grad_triple)

    packed = field_ref.shape[1]
    target = lax.broadcasted_iota(jnp.int32, (packed, packed), 0)
    origin = lax.broadcasted_iota(jnp.int32, (packed, packed), 1)
    place = (target % PATCH) * each + target // PATCH
    arrange = jnp.where((origin == place) & (target < PATCH * each), 1.0, 0.0).astype(bfloat)

    def fields_at(i):
        return [fields_ref[p, :, lanes(i)].astype(flt) for p in range(PATCH)]

    def score_col(p, head):
        return score_map[p * SLOT_ROWS : (p + 1) * SLOT_ROWS, head : head + 1]

    def mixture(prob, fields):
        return jnp.concatenate([prob * f for f in fields] + [prob], axis=0).astype(bfloat)

    def normalize_cols(values):
        center = values - jnp.mean(values, axis=0, keepdims=True)
        inv = lax.rsqrt(jnp.mean(center * center, axis=0, keepdims=True) + EPSILON)
        return center * inv, inv

    def normalize_cols_back(grad, normed, inv):
        first = jnp.mean(grad, axis=0, keepdims=True)
        second = jnp.mean(grad * normed, axis=0, keepdims=True)
        return inv * (grad - first - normed * second)

    @pl.loop(0, tiles, unroll=spread)
    def _(i):
        at = lanes(i)
        fields = fields_at(i)
        for head in range(HEADS):
            score = score_col(PATCH, head) + mask_ref[:, 0:1]
            for p in range(PATCH):
                score = score + score_col(p, head) * fields[p]
            score = score * scale
            weight = jnp.exp(score - jnp.max(score, axis=0, keepdims=True))
            prob = weight / jnp.sum(weight, axis=0, keepdims=True)
            probs[head, :, at] = prob
            both = matmul(value_map[head], mixture(prob, fields))
            part = slice(head * HDIM, (head + 1) * HDIM)
            total = both[:HDIM] + both[HDIM:] + cols_ref[part, 0:1]
            pooled[part, at] = total.astype(bfloat)
        begin = matmul(out_t[...], pooled[:, at]) + column(1)
        start[:, at] = begin
        normed, inv = normalize_cols(begin)
        inverse[0:1, at] = inv
        low = (normed * (1.0 + column(5)) + column(4)).astype(bfloat)
        input_one[:, at] = low
        segment = segment_ref[:, at]
        ident = lax.broadcasted_iota(jnp.int32, (AUGMENT - HDIM, TILE), 0)
        hot = jnp.where(ident == segment, 1.0, 0.0)
        cold = jnp.where((ident != segment) & (ident < 4), FAR, 0.0)
        triples = [
            matmul(qkv_t[block * depth : (block + 1) * depth], low).astype(bfloat)
            for block in range(3)
        ]
        key_t[:, at] = triples[1]
        for head in range(HEADS):
            part = slice(head * HDIM, (head + 1) * HDIM)
            queries = triples[0][part].astype(flt) * scale
            query[head, :, at] = jnp.concatenate([queries, hot], axis=0).astype(bfloat)
            long = jnp.concatenate([triples[1][part].astype(flt), cold], axis=0)
            key[head, at] = long.T.astype(bfloat)
            values = triples[2][part]
            value[head, at] = values.astype(flt).T.astype(bfloat)
            value_t[head, :HDIM, at] = values
            value_t[head, HDIM:, at] = jnp.ones((AUGMENT - HDIM, TILE), bfloat)

    @pl.loop(0, tiles)
    def _(i):
        at = lanes(i)
        low, high = spans_ref[i, 0], spans_ref[i, 1]

        mixed[...] = jnp.zeros_like(mixed)
        for base in range(0, HEADS, team_size):
            team = range(base, base + team_size)

            def scores(j, tops, team=team, base=base):
                new = []
                for head in team:
                    logits = matmul(key[head, lanes(j)], query[head, :, at])
                    raw[j, head - base] = logits
                    top = jnp.max(logits, axis=0, keepdims=True)
                    new.append(jnp.maximum(tops[head - base], top))
                return tuple(new)

            none = tuple(jnp.full((1, TILE), FAR, flt) for _ in team)
            tops = lax.fori_loop(low, high, scores, none)

            def blend(j, totals, team=team, base=base, tops=tops):
                new = []
                for head in team:
                    weight = jnp.exp(raw[j, head - base] - tops[head - base])
                    new.append(totals[head - base] + jnp.sum(weight, axis=0, keepdims=True))
                    mixed[head] += matmul(value_t[head, :, lanes(j)], weight.astype(bfloat))
                return tuple(new)

            zero = tuple(jnp.zeros((1, TILE), flt) for _ in team)
            totals = lax.fori_loop(low, high, blend, zero)
            for head in team:
                part = slice(head * HDIM, (head + 1) * HDIM)
                whole = mixed[head, :HDIM] / mixed[head, HDIM : HDIM + 1]
                upper, rest = halves(whole)
                attended[part, at] = upper
                grad_out[part, at] = rest
                log_sum[head : head + 1, at] = tops[head - base] + jnp.log(totals[head - base])

    rate = 1.0 / math.sqrt(tokens_all)
    for load in loads:
        load.wait()
    for block in range(4):
        part = slice(block * depth, (block + 1) * depth)
        up_t[part] = mlp_ref[0, :, part].astype(flt).T.astype(bfloat)
        down_t[part] = mlp_ref[1, :, part].astype(flt).T.astype(bfloat)

    @pl.loop(0, tiles)
    def _(i):
        at = lanes(i)
        att = attended[:, at]
        att_branch = matmul(proj_t[...], att) + column(2)
        mid = start[:, at] + column(6) * att_branch
        normed, inv = normalize_cols(mid)
        low = (normed * (1.0 + column(8)) + column(7)).astype(bfloat)
        input_two[:, at] = low
        out = column(3) + jnp.zeros((depth, TILE), flt)
        for block in range(HEADS):
            part = slice(block * TILE, (block + 1) * TILE)
            up = matmul(up_t[part], low)
            square = up * up
            curve = jnp.tanh(up * (GELU_ROOT + (GELU_ROOT * GELU_CUBE) * square))
            half = 0.5 + 0.5 * curve
            act = (up * half).astype(bfloat)
            active[part, at] = act
            slope = half + (0.5 * up) * (1.0 - curve * curve) * (
                GELU_ROOT + (3.0 * GELU_ROOT * GELU_CUBE) * square
            )
            raw[block // team_size, block % team_size] = slope
        out = out + matmul(mlp_ref[1], active[:, at])
        result = mid + column(9) * out
        rows = pl.ds(pl.multiple_of(i * TILE, TILE), TILE)
        out_rows[rows] = result.T.astype(bfloat)
        grad = cot_ref[rows].astype(flt).T * rate
        column_acc[9] += fold(grad * out)
        low_grad = (grad * column(9)).astype(bfloat)
        grad_branch[:, at] = low_grad
        column_acc[3] += fold(low_grad.astype(flt))
        grad_in = jnp.zeros((depth, TILE), flt)
        for block in range(HEADS):
            part = slice(block * TILE, (block + 1) * TILE)
            ups = (matmul(down_t[part], low_grad) * raw[block // team_size, block % team_size]).astype(bfloat)
            grad_up[part, at] = ups
            grad_in = grad_in + matmul(mlp_ref[0, :, part], ups)
        column_acc[8] += fold(grad_in * normed)
        column_acc[7] += fold(grad_in)
        grad = grad + normalize_cols_back(grad_in * (1.0 + column(8)), normed, inv)
        grad_mid[:, at] = grad
        column_acc[6] += fold(grad * att_branch)
        low_grad = (grad * column(6)).astype(bfloat)
        grad_att[:, at] = low_grad
        column_acc[2] += fold(low_grad.astype(flt))
        grads = matmul(square_ref[3], low_grad)
        low_grad = grads.astype(bfloat)
        whole = att.astype(flt) + grad_out[:, at].astype(flt)
        product = low_grad.astype(flt) * whole
        grad_out[:, at] = low_grad
        for head in range(HEADS):
            part = slice(head * HDIM, (head + 1) * HDIM)
            inner[head : head + 1, at] = jnp.sum(product[part], axis=0, keepdims=True)

    def weight_grad(left, right, rows, base):
        for block in range(0, rows, TILE):
            size = min(TILE, rows - block)
            grads = contract_cols(left[...], right[block : block + size])
            for piece in range(size // WIDTH):
                place = base + block // WIDTH + piece
                grad_rows[place] = grads[:, piece * WIDTH : (piece + 1) * WIDTH].astype(bfloat)

    weight_grad(input_two, grad_up, 4 * depth, 0)
    weight_grad(grad_branch, active, 4 * depth, 12)
    weight_grad(attended, grad_att, depth, 33)
    stores = [pltpu.make_async_copy(out_rows, out_hbm, out_sem.at[0])]

    def store_grads(first, past):
        part = pl.ds(first, past - first)
        stores.append(
            pltpu.make_async_copy(grad_rows.at[part], grad_hbm.at[part], out_sem.at[len(stores)])
        )
        stores[-1].start()

    stores[0].start()
    store_grads(0, 24)
    store_grads(33, 36)

    @pl.loop(0, tiles)
    def _(i):
        at = lanes(i)

        @pl.loop(spans_ref[i, 0], spans_ref[i, 1])
        def _(j):
            to = lanes(j)
            parts = [slice(head * HDIM, (head + 1) * HDIM) for head in range(HEADS)]
            logits = [matmul(key[head, to], query[head, :, at]) for head in range(HEADS)]
            backs = [matmul(value[head, to], grad_out[parts[head], at]) for head in range(HEADS)]
            weights = [jnp.exp(logits[h] - log_sum[h : h + 1, at]) for h in range(HEADS)]
            grad_raw = [
                (weights[h] * (backs[h] - inner[h : h + 1, at])).astype(bfloat)
                for h in range(HEADS)
            ]
            weights = [weight.astype(bfloat) for weight in weights]
            for head, part in enumerate(parts):
                grad_triple[part, at] += matmul(key_t[part, to], grad_raw[head])
            for head in range(HEADS):
                part = slice(depth + head * HDIM, depth + (head + 1) * HDIM)
                grad_triple[part, to] += contract_cols(query[head, :HDIM, at], grad_raw[head])
            for head in range(HEADS):
                part = slice(2 * depth + head * HDIM, 2 * depth + (head + 1) * HDIM)
                grad_triple[part, to] += contract_cols(grad_out[parts[head], at], weights[head])

    @pl.loop(0, tiles, unroll=spread)
    def _(i):
        at = lanes(i)
        grad_in = jnp.zeros((depth, TILE), flt)
        for block in range(3):
            part = slice(block * depth, (block + 1) * depth)
            grads = grad_triple[part, at]
            if block == 0:
                grads = grads * scale
            grads = grads.astype(bfloat)
            active[part, at] = grads
        grad_in = matmul(qkv_ref[...], active[: 3 * depth, at])
        inv = inverse[0:1, at]
        begin = start[:, at]
        normed = (begin - jnp.mean(begin, axis=0, keepdims=True)) * inv
        column_acc[5] += fold(grad_in * normed)
        column_acc[4] += fold(grad_in)
        grad = grad_mid[:, at] + normalize_cols_back(grad_in * (1.0 + column(5)), normed, inv)
        low_grad = grad.astype(bfloat)
        attended[:, at] = low_grad
        column_acc[1] += fold(low_grad.astype(flt))
        grads = matmul(square_ref[2], low_grad).astype(bfloat)
        column_acc[0] += fold(grads.astype(flt))
        fields = fields_at(i)
        field_grads = [jnp.zeros((SLOT_ROWS, TILE), flt) for _ in range(PATCH)]
        for head in range(HEADS):
            part = slice(head * HDIM, (head + 1) * HDIM)
            own = grads[part]
            prob = probs[head, :, at]
            cross = matmul(value_cols[head], jnp.concatenate([own, own], axis=0))
            pieces = [cross[p * SLOT_ROWS : (p + 1) * SLOT_ROWS] for p in range(PATCH + 1)]
            along = pieces[PATCH]
            for p in range(PATCH):
                along = along + pieces[p] * fields[p]
            center = jnp.sum(prob * along, axis=0, keepdims=True)
            grad_score = (prob * (along - center) * scale).astype(bfloat).astype(flt)
            for p in range(PATCH):
                field_grads[p] = (
                    field_grads[p] + prob * pieces[p] + grad_score * score_col(p, head)
                )
                key_acc[head, p] += fold(fields[p] * grad_score)
            key_acc[head, PATCH] += fold(grad_score)
            map_acc[part] += contract_cols(own, mixture(prob, fields))
        for group in range(groups):
            pieces = [grad[group * each : (group + 1) * each] for grad in field_grads]
            pieces.append(jnp.zeros((field_ref.shape[1] - PATCH * each, TILE), flt))
            field_ref[group, :, at] = matmul(
                arrange, jnp.concatenate(pieces, axis=0).astype(bfloat)
            ).astype(bfloat)

    weight_grad(input_one, active, 3 * depth, 24)
    store_grads(24, 33)
    weight_grad(pooled, attended, depth, 36)
    maps_high, maps_low = halves(map_acc[...])
    value_grad = (
        contract_cols(slots_t[0], maps_high)
        + contract_cols(slots_t[0], maps_low)
        + contract_cols(slots_t[1], maps_high)
    )
    for piece in range(3):
        part = slice(piece * WIDTH, (piece + 1) * WIDTH)
        grad_rows[39 + piece] = value_grad[:, part].astype(bfloat)
    lane = lax.broadcasted_iota(jnp.int32, (SLOT_ROWS, WIDTH), 1)
    keys = []
    for p in range(PATCH + 1):
        rows = jnp.zeros((SLOT_ROWS, WIDTH), flt)
        for head in range(HEADS):
            rows = rows + jnp.where(
                lane == head, jnp.sum(key_acc[head, p], axis=1, keepdims=True), 0.0
            )
        keys.append(rows)
    keys = jnp.concatenate(keys, axis=0)
    keys_high, keys_low = halves(keys)
    key_grad = (
        matmul(slots_t[0], keys_high) + matmul(slots_t[0], keys_low) + matmul(slots_t[1], keys_high)
    )
    grad_rows[42] = key_grad.astype(bfloat)
    grad_rows[43] = jnp.zeros_like(grad_rows[43])
    store_grads(36, 44)
    slot_grad = (
        matmul(value_weight, maps_high)
        + matmul(value_weight, maps_low)
        + contract_cols(keyvec_ref[...], keys_high)
        + contract_cols(keyvec_ref[...], keys_low)
    )
    turned = slot_grad.T
    pairs, rows = slot_ref.shape[1], slot_ref.shape[3]
    size = slot_share((PATCH + 1) * each, 2 * pairs)
    for group in range(groups):
        pieces = [
            turned[p * SLOT_ROWS + group * each : p * SLOT_ROWS + (group + 1) * each][
                :, piece * WIDTH : (piece + 1) * WIDTH
            ]
            for piece in range(3)
            for p in range(PATCH + 1)
        ]
        used = 3 * (PATCH + 1) * each
        pieces.append(jnp.zeros((2 * pairs * size + rows - used, WIDTH), flt))
        flat = jnp.concatenate(pieces, axis=0)
        for block in range(2 * pairs):
            part = flat[block * size : block * size + rows]
            slot_ref[group, block // 2, block % 2] = part.astype(bfloat)
    grad_high, grad_low = halves(key_grad)
    key_turned = square_ref[0].astype(flt).T.astype(bfloat)
    asked = matmul(key_turned, grad_high) + matmul(key_turned, grad_low)
    lane = lax.broadcasted_iota(jnp.int32, (depth, WIDTH), 1)
    head_of = lax.broadcasted_iota(jnp.int32, (depth, WIDTH), 0) // HDIM
    columns = jnp.where(
        lane == 0, jnp.sum(jnp.where(lane == head_of, asked, 0.0), axis=1, keepdims=True), 0.0
    )
    columns = columns + jnp.where(lane == 11, cols_ref[:, 11:12], 0.0)
    for which in range(10):
        columns = columns + jnp.where(
            lane == which + 1, jnp.sum(column_acc[which], axis=1, keepdims=True), 0.0
        )
    vec_ref[...] = columns.T[:VEC_ROWS]
    for store in stores:
        store.wait()


def slot_share(rows, count):
    return -(-3 * rows // count)


def block_step(count, groups, own, each, segment, fields, slots, mask, square, qkv, mlp, cols, cot):
    length = cot.shape[0]
    bfloat, flt = jnp.bfloat16, jnp.float32
    rows = (PATCH + 1) * SLOT_ROWS
    tiles = length // TILE
    block_rows = -(-own // 16) * 16
    field_rows = -(-PATCH * each // 16) * 16
    team_size = HEADS if count * block_rows <= D else HEADS // 2
    vmem = pl.BlockSpec(memory_space=pltpu.VMEM)
    hbm = pl.BlockSpec(memory_space=pl.ANY)
    shapes = [
        ((D, D), bfloat),
        ((3 * D, D), bfloat),
        ((D, D), bfloat),
        ((4 * D, D), bfloat),
        ((4 * D, D), bfloat),
        ((2, D, rows), bfloat),
        ((HEADS, 2 * HDIM, rows), bfloat),
        ((HEADS, rows, 2 * HDIM), bfloat),
        ((rows, WIDTH), flt),
        ((HEADS, SLOT_ROWS, length), flt),
        ((D, length), bfloat),
        ((D, length), flt),
        ((8, length), flt),
        ((D, length), bfloat),
        ((HEADS, AUGMENT, length), bfloat),
        ((HEADS, length, AUGMENT), bfloat),
        ((D, length), bfloat),
        ((HEADS, length, HDIM), bfloat),
        ((HEADS, AUGMENT, length), bfloat),
        ((tiles, team_size, TILE, TILE), flt),
        ((HEADS, AUGMENT, TILE), flt),
        ((8, length), flt),
        ((D, length), bfloat),
        ((D, length), bfloat),
        ((4 * D, length), bfloat),
        ((4 * D, length), bfloat),
        ((D, length), bfloat),
        ((D, length), flt),
        ((D, length), bfloat),
        ((D, length), bfloat),
        ((8, length), flt),
        ((3 * D, length), flt),
        ((D, rows), flt),
        ((HEADS, PATCH + 1, SLOT_ROWS, WIDTH), flt),
        ((10, D, WIDTH), flt),
        ((D, WIDTH), bfloat),
        ((2, D, 4 * D), bfloat),
        ((length, D), bfloat),
        ((length, D), bfloat),
        ((44, D, WIDTH), bfloat),
    ]
    return pl.pallas_call(
        functools.partial(block_kernel, groups * count * length, groups, each),
        out_shape=(
            jax.ShapeDtypeStruct((length, D), bfloat),
            jax.ShapeDtypeStruct((44, D, WIDTH), bfloat),
            jax.ShapeDtypeStruct((groups, count // 2, 2, block_rows, WIDTH), bfloat),
            jax.ShapeDtypeStruct((VEC_ROWS, D), flt),
            jax.ShapeDtypeStruct((groups, field_rows, length), bfloat),
        ),
        in_specs=[pl.BlockSpec(memory_space=pltpu.SMEM)]
        + [vmem] * 5
        + [hbm, vmem, vmem, hbm],
        out_specs=(hbm, hbm, vmem, vmem, vmem),
        scratch_shapes=[pltpu.VMEM(shape, dtype) for shape, dtype in shapes]
        + [
            pltpu.SMEM((tiles, 2), jnp.int32),
            pltpu.SemaphoreType.DMA((2,)),
            pltpu.SemaphoreType.DMA((5,)),
        ],
        compiler_params=pltpu.CompilerParams(vmem_limit_bytes=62 << 20),
    )(segment, fields, slots, mask, square, qkv, mlp, cols, segment, cot)


CHUNKS = 4
CHUNK = 12
ORDER = (3, 0, 1, 2)
WIDTH = 128
VEC_ROWS = 16
MESH = pl.DeviceIdType.MESH


def flip(index, mask, bits):
    total = 0
    for bit in range(bits):
        own = (index // 2**bit) % 2
        total = total + (1 - own if (mask >> bit) & 1 else own) * 2**bit
    return total


def rounds_of(bits, backward):
    order = list(range(bits))
    return order[::-1] if backward else order


def mask_of(order, level, entry):
    mask = 0
    for place, bit in enumerate(order[level:]):
        if (entry >> (len(order) - level - 1 - place)) & 1:
            mask |= 1 << bit
    return mask


def greet(dp, here, masks, bits, groups):
    barrier = pltpu.get_barrier_semaphore()
    for mask in masks:
        pl.semaphore_signal(
            barrier, inc=1, device_id={"dp": flip(dp, mask, bits)}, device_id_type=MESH
        )
    for step in range(1, groups):
        pl.semaphore_signal(
            barrier, inc=1, device_id={"vars": (here + step) % groups}, device_id_type=MESH
        )
    pl.semaphore_wait(barrier, len(masks) + groups - 1)


class Copies:
    def __init__(self, send_sem, recv_sem):
        self.send_sem, self.recv_sem = send_sem, recv_sem
        self.started = []

    def start(self, source, target, device):
        place = len(self.started)
        copy = pltpu.make_async_remote_copy(
            src_ref=source,
            dst_ref=target,
            send_sem=self.send_sem.at[place],
            recv_sem=self.recv_sem.at[place],
            device_id=device,
            device_id_type=MESH,
        )
        copy.start()
        self.started.append(copy)
        return copy

    def finish(self):
        for copy in self.started:
            copy.wait_send()


class Spread:
    def __init__(self, copies, refs, dp, bits, order, own=None):
        self.copies, self.refs, self.dp, self.bits = copies, refs, dp, bits
        self.own = own
        self.order = order
        self.arriving = {}

    def send(self, mask, first):
        block = flip(self.dp, mask, self.bits)
        for level in range(first, len(self.order)):
            bit = self.order[level]
            partner = {"dp": flip(self.dp, 1 << bit, self.bits)}
            for which, ref in enumerate(self.refs):
                source = self.own[which] if self.own and not mask else ref(block)
                copy = self.copies.start(source, ref(block), partner)
                self.arriving.setdefault(level, []).append((mask | (1 << bit), copy))

    def begin(self):
        self.send(0, 0)

    def advance(self, level):
        for place, (mask, copy) in enumerate(self.arriving[level]):
            copy.wait_recv()
            if place % len(self.refs) == len(self.refs) - 1:
                self.send(mask, level + 1)


def reduce_kernel(
    count,
    groups,
    g_ref,
    s_ref,
    vec_ref,
    field_ref,
    total,
    slot_ref,
    vec_all,
    field_out,
    recv0,
    acc,
    send_x,
    recv_x,
    zsend,
    zrecv,
    zkeep,
    ysend,
    yrecv,
    lsend,
    lrecv,
    g_own,
    own_sem,
    send_sem,
    recv_sem,
):
    bits = count.bit_length() - 1
    lower = bits - 1
    dp, here = lax.axis_index("dp"), lax.axis_index("vars")
    core, pair = dp % 2, dp // 2
    own_copy = pltpu.make_async_copy(g_ref.at[:, :, core], g_own, own_sem.at[0])
    own_copy.start()
    greet(dp, here, [1 << bit for bit in range(bits)], bits, groups)
    copies = Copies(send_sem, recv_sem)
    half = CHUNK // 2
    share = CHUNK // groups
    other = {"dp": dp + 1 - 2 * core}

    def grads_at(piece):
        if piece < 2 * CHUNKS - 2:
            return piece * half, half
        size = half - groups // 2
        return (2 * CHUNKS - 2) * half + (piece % 2) * size, size

    vec_copies = [
        copies.start(vec_ref, vec_all.at[dp, here], {"vars": (here + step) % groups})
        for step in range(1, groups)
    ]
    vec_all[dp, here] = vec_ref[...]
    level0 = {}
    for chunk in ORDER:
        for side in range(2):
            piece = 2 * chunk + side
            base, size = grads_at(piece)
            level0[piece] = [
                copies.start(
                    g_ref.at[pl.ds(base, size), :, 1 - core],
                    recv0.at[piece, pl.ds(0, size)],
                    other,
                )
            ]
            if size < half:
                level0[piece].append(
                    copies.start(
                        s_ref.at[pl.ds(side * (half - size), half - size), :, 1 - core],
                        recv0.at[piece, pl.ds(size, half - size)],
                        other,
                    )
                )
    field_copies = [
        copies.start(
            field_ref.at[(here + step) % groups],
            field_out.at[here],
            {"vars": (here + step) % groups},
        )
        for step in range(1, groups)
    ]
    field_out[here] = field_ref[here]
    forth = list(range(1, bits)) + [0]
    vecs = Spread(copies, [lambda block: vec_all.at[block]], dp, bits, forth)
    slots = Spread(copies, [lambda block: slot_ref.at[block]], dp, bits, forth)

    def vec_begin():
        for copy in vec_copies:
            copy.wait_recv()
        vecs.begin()

    crossing = {}
    own_copy.wait()

    def send_level(piece, level):
        order = rounds_of(lower, piece % 2)
        entries = 2 ** (lower - 1 - level)
        low = 2**lower - 2 ** (lower - level)
        partner = {"dp": 2 * flip(pair, 1 << order[level], lower) + core}
        crossing[piece, level] = copies.start(
            send_x.at[piece, pl.ds(low, entries)],
            recv_x.at[piece, pl.ds(low, entries)],
            partner,
        )

    def first(piece):
        order = rounds_of(lower, piece % 2)
        for copy in level0[piece]:
            copy.wait_recv()
        base, size = grads_at(piece)
        kept = 2 ** (lower - 1)
        for entry in range(2**lower):
            block = flip(pair, mask_of(order, 0, entry), lower)
            value = g_own[pl.ds(base, size), block].astype(jnp.float32)
            value = value + recv0[piece, pl.ds(0, size), block].astype(jnp.float32)
            if size < half:
                rest = half - size
                slots = s_ref[pl.ds((piece % 2) * rest, rest), block, core].astype(jnp.float32)
                slots = slots + recv0[piece, pl.ds(size, rest), block].astype(jnp.float32)
                value = jnp.concatenate([value[:2], slots[:1], value[2:], slots[1:]], axis=0)
            if entry < kept:
                acc[piece, entry] = value
            else:
                send_x[piece, entry - kept] = value.astype(jnp.bfloat16)
        send_level(piece, 0)

    def later(piece, level):
        crossing[piece, level].wait_recv()
        entries = 2 ** (lower - 1 - level)
        low = 2**lower - 2 ** (lower - level)
        kept = entries // 2
        for entry in range(entries):
            value = acc[piece, entry] + recv_x[piece, low + entry].astype(jnp.float32)
            if entries > 1 and entry >= kept:
                send_x[piece, low + entries + entry - kept] = value.astype(jnp.bfloat16)
            else:
                acc[piece, entry] = value
        if level + 1 < lower:
            send_level(piece, level + 1)

    near = {"vars": here + 1 - 2 * (here % 2)}
    far = {"vars": (here + 2) % groups}
    low, top = here % 2, here // 2
    across, over, around, forward = {}, {}, {}, {}

    final = ORDER[-1]

    def send_near(piece):
        if piece // 2 == final:
            return
        zsend[piece] = acc[piece, 0, pl.ds(share * (1 - low), share)].astype(jnp.bfloat16)
        across[piece] = copies.start(zsend.at[piece], zrecv.at[piece], near)

    def sum_near(piece):
        across[piece].wait_recv()
        own = acc[piece, 0, pl.ds(share * low, share)]
        zkeep[piece] = own + zrecv[piece].astype(jnp.float32)

    def send_far(chunk):
        if chunk == final:
            for side in range(2):
                for half_side in range(2):
                    part = acc[2 * chunk + side, 0, pl.ds(share * half_side, share)]
                    lsend[2 * side + half_side] = part.astype(jnp.bfloat16)
            over[chunk] = [
                copies.start(
                    lsend.at[(here + step) % groups],
                    lrecv.at[step - 1],
                    {"vars": (here + step) % groups},
                )
                for step in range(1, groups)
            ]
            return
        for side in range(2):
            sum_near(2 * chunk + side)
        ysend[chunk] = zkeep[2 * chunk + 1 - top].astype(jnp.bfloat16)
        over[chunk] = copies.start(ysend.at[chunk], yrecv.at[chunk], far)

    def quarter(chunk, which):
        count_back = share - 1 if chunk == CHUNKS - 1 else share
        return total.at[chunk, which, pl.ds(0, count_back)]

    def sum_far(chunk):
        if chunk == final:
            value = acc[2 * chunk + top, 0, pl.ds(share * low, share)]
            for step, copy in enumerate(over[chunk]):
                copy.wait_recv()
                value = value + lrecv[step].astype(jnp.float32)
            total[chunk, here] = value.astype(jnp.bfloat16)
            around[chunk] = [
                copies.start(
                    quarter(chunk, here), quarter(chunk, here), {"vars": (here + step) % groups}
                )
                for step in range(1, groups)
            ]
            return
        over[chunk].wait_recv()
        value = zkeep[2 * chunk + top] + yrecv[chunk].astype(jnp.float32)
        total[chunk, here] = value.astype(jnp.bfloat16)
        if chunk == CHUNKS - 1:
            slot_ref[dp] = value[share - 1]
        around[chunk] = [
            copies.start(quarter(chunk, here), quarter(chunk, here), to) for to in (far, near)
        ]

    def pass_on(chunk):
        if chunk == final:
            return
        around[chunk][0].wait_recv()
        other_quarter = quarter(chunk, (here + 2) % groups)
        forward[chunk] = copies.start(other_quarter, other_quarter, near)

    def finish(chunk):
        if chunk == final:
            for copy in around[chunk]:
                copy.wait_recv()
            return
        around[chunk][1].wait_recv()
        forward[chunk].wait_recv()

    def pieces(act):
        def both(chunk):
            act(2 * chunk)
            act(2 * chunk + 1)

        return both

    stages = [pieces(first)]
    stages += [pieces(lambda piece, level=level: later(piece, level)) for level in range(lower)]
    stages += [pieces(send_near), send_far, sum_far, pass_on, finish]
    extra = {1: [vec_begin], len(stages) - 3: [slots.begin]}
    for level in range(bits):
        tick = min(4 + 2 * level, CHUNKS + len(stages) - 2)
        extra.setdefault(tick, []).append(functools.partial(vecs.advance, level))
        tick = min(len(stages) - 1 + level, CHUNKS + len(stages) - 2)
        extra.setdefault(tick, []).append(functools.partial(slots.advance, level))
    for tick in range(CHUNKS + len(stages) - 1):
        for stage in range(len(stages)):
            place = tick - stage
            if 0 <= place < CHUNKS:
                stages[stage](ORDER[place])
        for act in extra.get(tick, ()):
            act()
    for copy in field_copies:
        copy.wait_recv()
    copies.finish()


def reduce_all(count, groups, grads, slots, vec, field):
    bits = count.bit_length() - 1
    lower = bits - 1
    rows = grads.shape[3]
    half = CHUNK // 2
    pieces = 2 * CHUNKS
    share = CHUNK // groups
    copies = 4 * (groups - 1) + (pieces - 2) * (bits + 1) + 2 * bits
    copies += 4 * (CHUNKS - 1) + 2 + 2 * (count - 1)
    bfloat = jnp.bfloat16
    vmem = pl.BlockSpec(memory_space=pltpu.VMEM)
    return pl.pallas_call(
        functools.partial(reduce_kernel, count, groups),
        out_shape=(
            jax.ShapeDtypeStruct((CHUNKS, groups, share, rows, WIDTH), bfloat),
            jax.ShapeDtypeStruct((count, rows, WIDTH), jnp.float32),
            jax.ShapeDtypeStruct((count, groups) + vec.shape, jnp.float32),
            jax.ShapeDtypeStruct(field.shape, field.dtype),
        ),
        in_specs=[pl.BlockSpec(memory_space=pl.ANY)] + [vmem] * 3,
        out_specs=(vmem,) * 4,
        scratch_shapes=[
            pltpu.VMEM((pieces, half, count // 2, rows, WIDTH), bfloat),
            pltpu.VMEM((pieces, count // 4, half, rows, WIDTH), jnp.float32),
            pltpu.VMEM((pieces, count // 2 - 1, half, rows, WIDTH), bfloat),
            pltpu.VMEM((pieces, count // 2 - 1, half, rows, WIDTH), bfloat),
            pltpu.VMEM((pieces, share, rows, WIDTH), bfloat),
            pltpu.VMEM((pieces, share, rows, WIDTH), bfloat),
            pltpu.VMEM((pieces, share, rows, WIDTH), jnp.float32),
            pltpu.VMEM((CHUNKS, share, rows, WIDTH), bfloat),
            pltpu.VMEM((CHUNKS, share, rows, WIDTH), bfloat),
            pltpu.VMEM((groups, share, rows, WIDTH), bfloat),
            pltpu.VMEM((groups - 1, share, rows, WIDTH), bfloat),
            pltpu.VMEM((CHUNKS * CHUNK - groups, count // 2, rows, WIDTH), bfloat),
            pltpu.SemaphoreType.DMA((1,)),
            pltpu.SemaphoreType.DMA((copies,)),
            pltpu.SemaphoreType.DMA((copies,)),
        ],
        compiler_params=pltpu.CompilerParams(
            collective_id=0, has_side_effects=True, vmem_limit_bytes=60 << 20
        ),
    )(grads, slots, vec, field)


def pack_rows(blocks, count, rows):
    own = blocks.shape[1] // count
    blocks = blocks.reshape(blocks.shape[0], count // 2, 2, own, WIDTH)
    return jnp.pad(blocks, ((0, 0), (0, 0), (0, 0), (0, rows - own), (0, 0)))


def renew_into(outs, refs, at, gradient, step_rate):
    new = renew(*(ref[at] for ref in refs), gradient, step_rate)
    for out, value in zip(outs, new):
        out[at] = value


def update_kernel(groups, sum_ref, slot_ref, vec_ref, back_ref, *refs):
    flt = jnp.float32
    slot_in, square_in, wide_in, mlp_in, vector_in = (refs[3 * i : 3 * i + 3] for i in range(5))
    refs = refs[15:]
    field_out = refs[-1]
    slot_out, square_out, wide_out, mlp_out, vector_out = (
        refs[4 * i : 4 * i + 4] for i in range(5)
    )
    own = wide_in[0].shape[0]
    for group in range(groups):
        rows = back_ref[group].astype(flt)
        for slot in range(field_out.shape[0]):
            field_out[slot, group] = rows[slot * PATCH : (slot + 1) * PATCH]
    bfloat = jnp.bfloat16
    last = CHUNKS - 1

    def block(place):
        if place < last * CHUNK:
            chunk, rest = divmod(place, CHUNK)
            share = CHUNK // groups
        else:
            chunk, rest, share = last, place - last * CHUNK, CHUNK // groups - 1
        return sum_ref[chunk, rest // share, rest % share, :own]

    for place in range(12):
        part = (slice(None), slice(place * WIDTH, (place + 1) * WIDTH))
        for half in range(2):
            grads = block(12 * half + place).astype(flt)
            renew_into(mlp_out, mlp_in, (half,) + part, grads, RATE)
    for place in range(9):
        part = (slice(None), slice(place * WIDTH, (place + 1) * WIDTH))
        renew_into(wide_out, wide_in, part, block(24 + place).astype(flt), RATE)
    for which, base in ((3, 33), (2, 36), (1, 39)):
        for place in range(3):
            part = (which, slice(None), slice(place * WIDTH, (place + 1) * WIDTH))
            renew_into(square_out, square_in, part, block(base + place).astype(flt), RATE)
    asked = vector_in[0][0:1]
    lane = lax.broadcasted_iota(jnp.int32, (WIDTH, D), 1) // HDIM
    head = lax.broadcasted_iota(jnp.int32, (WIDTH, D), 0)
    asked_high, asked_low = halves(jnp.where(lane == head, asked, 0.0))
    keys = block(42)
    renew_into(
        square_out, square_in, (0,), matmul(keys, asked_high) + matmul(keys, asked_low), RATE
    )
    devices = vec_ref.shape[0]
    pick = lax.broadcasted_iota(jnp.int32, (D, own), 0) == lax.axis_index(
        "dp"
    ) * own + lax.broadcasted_iota(jnp.int32, (D, own), 1)
    conditions = matmul(vec_ref[:, 11, :].astype(bfloat), jnp.where(pick, 1.0, 0.0).astype(bfloat))
    conditions = conditions.T.astype(bfloat)
    for row in range(6):
        high, low = halves(vec_ref[:, 5 + row, :])
        part = (slice(None), slice((3 + row) * D, (4 + row) * D))
        grads = matmul(conditions, high) + matmul(conditions, low)
        renew_into(wide_out, wide_in, part, grads, RATE)
    total = vec_ref[0]
    for device in range(1, devices):
        total = total + vec_ref[device]
    renew_into(vector_out, vector_in, (slice(None),), total[:11], RATE)
    each = slot_in[0].shape[1]
    blocks = slot_ref.shape[0]
    size = slot_share((PATCH + 1) * each, blocks)
    flat = jnp.concatenate([slot_ref[b, :size] for b in range(blocks)], axis=0)
    for p in range(PATCH + 1):
        pieces = [
            flat[(piece * (PATCH + 1) + p) * each : (piece * (PATCH + 1) + p + 1) * each]
            for piece in range(3)
        ]
        renew_into(slot_out, slot_in, (p,), jnp.concatenate(pieces, axis=1), EMBED_RATE)


def update_all(groups, sums, slot_blocks, vec_all, field_back, parameters):
    vmem = pl.BlockSpec(memory_space=pltpu.VMEM)
    shapes = [jax.ShapeDtypeStruct(a.shape, a.dtype) for a in parameters[::3] for _ in range(4)]
    field_shape = (parameters[0].shape[1], groups, PATCH, field_back.shape[2])
    shapes.append(jax.ShapeDtypeStruct(field_shape, jnp.float32))
    return pl.pallas_call(
        functools.partial(update_kernel, groups),
        out_shape=tuple(shapes),
        in_specs=[vmem] * (4 + len(parameters)),
        out_specs=(vmem,) * len(shapes),
        compiler_params=pltpu.CompilerParams(vmem_limit_bytes=60 << 20),
    )(sums, slot_blocks, vec_all, field_back, *parameters)


def gather_kernel(
    count,
    groups,
    ids_ref,
    field_ref,
    slot_ref,
    cond_in,
    square_ref,
    wide_ref,
    mlp_ref,
    vec_ref,
    patch_out,
    slots_out,
    mask_out,
    cols_out,
    square_out,
    qkv_out,
    mlp_out,
    field_all,
    slot_src,
    slot_all,
    cond_ref,
    cond_all,
    part,
    part_in,
    square_own,
    qkv_own,
    mlp_own,
    own_sem,
    send_sem,
    recv_sem,
):
    bfloat, flt = jnp.bfloat16, jnp.float32
    bits = count.bit_length() - 1
    dp, here = lax.axis_index("dp"), lax.axis_index("vars")
    own, rows = square_ref.shape[1], square_out.shape[2]
    if own < rows:
        for ref in (square_own, qkv_own, mlp_own):
            ref[...] = jnp.zeros_like(ref)
    square_own[:, :own] = square_ref[...].astype(bfloat)
    qkv_own[:own] = wide_ref[:, : 3 * D].astype(bfloat)
    mlp_own[:, :own] = mlp_ref[...].astype(bfloat)
    kept = [
        pltpu.make_async_copy(square_own, square_out.at[:, dp], own_sem.at[0]),
        pltpu.make_async_copy(qkv_own, qkv_out.at[dp], own_sem.at[1]),
        pltpu.make_async_copy(mlp_own, mlp_out.at[:, dp], own_sem.at[2]),
    ]
    for copy in kept:
        copy.start()
    raw = cond_in[...].astype(flt)
    cond = (raw * jax.nn.sigmoid(raw)).astype(bfloat).astype(flt)
    cond_ref[...] = jnp.broadcast_to(cond, cond_ref.shape)
    cond_all[dp] = cond_ref[...]
    each = slot_ref.shape[1]
    per = slot_src.shape[1]
    pieces = 3 * (PATCH + 1)
    for piece in range(count * per):
        block, at = piece // per, piece % per
        if piece < pieces:
            lane = piece % 3 * WIDTH
            slot_src[block, at] = slot_ref[piece // 3, :, lane : lane + WIDTH]
        else:
            slot_src[block, at] = jnp.zeros((each, WIDTH), flt)
    for row in range(each):
        ident = jnp.full((1, WIDTH), ids_ref[0, row], jnp.int32).astype(flt)
        slot_src[pieces // per, pieces % per, row : row + 1] = ident
    greet(dp, here, range(1, count), bits, groups)
    copies = Copies(send_sem, recv_sem)
    forth = list(range(1, bits)) + [0]
    back = list(range(1, bits))[::-1] + [0]
    ones = Spread(
        copies,
        [lambda block: square_out.at[:, block], lambda block: qkv_out.at[block]],
        dp,
        bits,
        forth,
        [square_own, qkv_own],
    )
    twos = Spread(copies, [lambda block: mlp_out.at[:, block]], dp, bits, back, [mlp_own])
    conds = [
        copies.start(cond_ref, cond_all.at[dp], {"dp": (dp + step) % count})
        for step in range(1, count)
    ]
    arrivals = []
    slot_copies = [
        copies.start(
            slot_src.at[dp], slot_all.at[dp, here], {"vars": (here + step) % groups}
        )
        for step in range(1, groups)
    ]
    trees = [
        Spread(copies, [lambda block, at=at: slot_all.at[block, :, at]], dp, bits, order)
        for at, order in zip(range(per), (forth, back))
    ]
    ones.begin()
    twos.begin()
    for step in range(1, groups):
        to = (here + step) % groups
        arrivals.append(copies.start(field_ref.at[to], field_all.at[here], {"vars": to}))
    field_all[here] = field_ref[here]
    slot_all[dp, here] = slot_src[dp]
    for copy in conds:
        copy.wait_recv()
    cond = cond_all[:, 0, :].astype(bfloat)
    pick = lax.broadcasted_iota(jnp.int32, (D, own), 0) == dp * own + lax.broadcasted_iota(
        jnp.int32, (D, own), 1
    )
    cond_rows = matmul(cond, jnp.where(pick, 1.0, 0.0).astype(bfloat)).astype(bfloat)
    shares = matmul(cond_rows, wide_ref[:, 3 * D :].astype(bfloat))
    strips = shares.shape[1] // WIDTH
    for block in range(count):
        for strip in range(strips):
            part[block, strip : strip + 1] = shares[
                block : block + 1, strip * WIDTH : (strip + 1) * WIDTH
            ]
    part_copies = [
        copies.start(part.at[(dp + step) % count], part_in.at[step - 1], {"dp": (dp + step) % count})
        for step in range(1, count)
    ]
    for copy in slot_copies:
        copy.wait_recv()
    for tree in trees:
        tree.begin()
    for stream in (ones, twos, *trees):
        stream.advance(0)
    for copy in part_copies:
        copy.wait_recv()
    mine = part[dp]
    for step in range(1, count):
        mine = mine + part_in[step - 1]
    wide_parts = [
        jnp.concatenate([mine[3 * row + strip : 3 * row + strip + 1] for strip in range(3)], axis=1)
        for row in range(6)
    ]
    modulation = jnp.concatenate(wide_parts, axis=0) + vec_ref[5:11]
    columns = jnp.concatenate(
        [
            vec_ref[1:5],
            modulation,
            vec_ref[0:1],
            cond_ref[0:1],
            jnp.zeros((WIDTH - 12, D), flt),
        ],
        axis=0,
    )
    cols_out[...] = columns.T
    for level in range(1, bits - 1):
        for stream in (*trees, ones, twos):
            stream.advance(level)
    for tree in trees:
        tree.advance(bits - 1)
    spare = SLOT_ROWS - groups * each
    def slot_piece(piece, fill):
        rows = [slot_all[piece // per, source, piece % per] for source in range(groups)]
        rows.append(jnp.full((spare, WIDTH), fill, flt))
        return jnp.concatenate(rows, axis=0)

    for piece in range(pieces):
        base, lane = piece // 3 * SLOT_ROWS, piece % 3 * WIDTH
        slots_out[base : base + SLOT_ROWS, lane : lane + WIDTH] = slot_piece(piece, 0.0)
    mask_out[...] = jnp.where(slot_piece(pieces, float(NVARS)) < NVARS, 0.0, FAR)
    for copy in arrivals:
        copy.wait_recv()
    for p in range(PATCH):
        rows = [
            field_all[source, p * each : (p + 1) * each].astype(flt) for source in range(groups)
        ]
        rows.append(jnp.zeros((spare, field_ref.shape[2]), flt))
        patch_out[p] = jnp.concatenate(rows, axis=0).astype(bfloat)
    for stream in (ones, twos):
        stream.advance(bits - 1)
    for copy in kept:
        copy.wait()
    copies.finish()


def gather_all(count, groups, ids, field, slots, cond, square, wide, mlp, vectors):
    bits = count.bit_length() - 1
    own = square.shape[1]
    rows = -(-own // 16) * 16
    bfloat, flt = jnp.bfloat16, jnp.float32
    per = -(-(3 * (PATCH + 1) + 1) // count)
    copies = 2 * (groups - 1) + (5 + min(per, 2)) * (count - 1)
    length = field.shape[2]
    strips = (wide.shape[1] - 3 * D) // WIDTH
    vmem = pl.BlockSpec(memory_space=pltpu.VMEM)
    outs = [
        ((PATCH, SLOT_ROWS, length), bfloat),
        (((PATCH + 1) * SLOT_ROWS, D), flt),
        ((SLOT_ROWS, WIDTH), flt),
        ((D, WIDTH), flt),
        ((4, count, rows, D), bfloat),
        ((count, rows, 3 * D), bfloat),
        ((2, count, rows, 4 * D), bfloat),
    ]
    return pl.pallas_call(
        functools.partial(gather_kernel, count, groups),
        out_shape=tuple(jax.ShapeDtypeStruct(shape, dtype) for shape, dtype in outs),
        in_specs=[pl.BlockSpec(memory_space=pltpu.SMEM)] + [vmem] * 7,
        out_specs=(vmem,) * 4 + (pl.BlockSpec(memory_space=pl.ANY),) * 3,
        scratch_shapes=[
            pltpu.VMEM((groups,) + field.shape[1:], bfloat),
            pltpu.VMEM((count, per, slots.shape[1], WIDTH), flt),
            pltpu.VMEM((count, groups, per, slots.shape[1], WIDTH), flt),
            pltpu.VMEM((8, D), flt),
            pltpu.VMEM((count, 8, D), flt),
            pltpu.VMEM((count, strips, WIDTH), flt),
            pltpu.VMEM((count - 1, strips, WIDTH), flt),
            pltpu.VMEM((4, rows, D), bfloat),
            pltpu.VMEM((rows, 3 * D), bfloat),
            pltpu.VMEM((2, rows, 4 * D), bfloat),
            pltpu.SemaphoreType.DMA((3,)),
            pltpu.SemaphoreType.DMA((copies,)),
            pltpu.SemaphoreType.DMA((copies,)),
        ],
        compiler_params=pltpu.CompilerParams(
            collective_id=1, has_side_effects=True, vmem_limit_bytes=60 << 20
        ),
    )(ids, field, slots, cond, square, wide, mlp, vectors)


def on_device(
    fields,
    var_ids,
    segments,
    condition,
    cotangent,
    slot_weights,
    slot_momentum,
    slot_average,
    square,
    square_momentum,
    square_average,
    wide,
    wide_momentum,
    wide_average,
    mlp,
    mlp_momentum,
    mlp_average,
    vectors,
    vectors_momentum,
    vectors_average,
):
    bfloat = jnp.bfloat16
    length = fields.shape[4]
    count, groups = lax.axis_size("dp"), lax.axis_size("vars")
    own = square.shape[1]
    rows = -(-own // 16) * 16
    field = jnp.transpose(fields[:, 0], (1, 2, 0, 3)).reshape(groups, -1, length)
    field = jnp.pad(field, ((0, 0), (0, -field.shape[1] % 16), (0, 0)))
    gathered = gather_all(
        count,
        groups,
        var_ids[None],
        field,
        jnp.transpose(slot_weights, (1, 0, 2)),
        condition[0],
        square,
        wide,
        mlp,
        vectors,
    )
    patches, slot_rows, mask, columns = gathered[:4]
    square_full, qkv_full, mlp_full = (a[..., :own, :] for a in gathered[4:])
    block_out, grads, slots_packed, vec, field = block_step(
        count,
        groups,
        own,
        slot_weights.shape[0],
        segments[0],
        patches,
        slot_rows,
        mask,
        square_full.reshape(4, D, D),
        qkv_full.reshape(D, 3 * D),
        mlp_full.reshape(2, D, 4 * D),
        columns,
        cotangent[0, 0],
    )
    sums, slot_blocks, vec_all, field_back = reduce_all(
        count, groups, pack_rows(grads, count, rows), slots_packed, vec, field
    )
    updated = update_all(
        groups,
        sums,
        slot_blocks,
        vec_all.reshape(-1, VEC_ROWS, D),
        field_back,
        (
            *(jnp.transpose(a, (1, 0, 2)) for a in (slot_weights, slot_momentum, slot_average)),
            square,
            square_momentum,
            square_average,
            wide,
            wide_momentum,
            wide_average,
            mlp,
            mlp_momentum,
            mlp_average,
            vectors,
            vectors_momentum,
            vectors_average,
        ),
    )
    field_grad = updated[-1][:, None]
    slot_new = tuple(jnp.transpose(a, (1, 0, 2)) for a in updated[:4])
    return (block_out[None, None], field_grad) + slot_new + tuple(updated[4:-1])


def solution(mesh):
    placed = (
        P("vars", "dp", None, None, None),
        P("vars"),
        P("dp", "vars", None),
        P("dp", "vars", None),
        P("dp", "vars", None, None),
        P("vars", None, None),
        P("vars", None, None),
        P("vars", None, None),
        P(None, "dp", None),
        P(None, "dp", None),
        P(None, "dp", None),
        P("dp", None),
        P("dp", None),
        P("dp", None),
        P(None, "dp", None),
        P(None, "dp", None),
        P(None, "dp", None),
        P(),
        P(),
        P(),
    )
    return jax.shard_map(
        on_device,
        mesh=mesh,
        in_specs=placed,
        out_specs=(
            P("dp", "vars", None, None),
            P("vars", "dp", None, None, None),
            P("vars", None, None),
            P("vars", None, None),
            P("vars", None, None),
            P("vars", None, None),
            P(None, "dp", None),
            P(None, "dp", None),
            P(None, "dp", None),
            P(None, "dp", None),
            P("dp", None),
            P("dp", None),
            P("dp", None),
            P("dp", None),
            P(None, "dp", None),
            P(None, "dp", None),
            P(None, "dp", None),
            P(None, "dp", None),
            P(),
            P(),
            P(),
            P(),
        ),
        check_vma=False,
    )
```

```python
import functools
import math

import jax
import jax.numpy as jnp
from jax import lax
from jax.experimental import pallas as pl
from jax.experimental.pallas import tpu as pltpu
from jax.sharding import PartitionSpec as P

D = 384
HEADS = 6
HDIM = 64
PATCH = 4
NVARS = 69


NEGATIVE = -1e30
EPSILON = 1e-06
GELU_ROOT = math.sqrt(2.0 / math.pi)
GELU_CUBE = 0.044715
WIDTH = 128
VEC_ROWS = 16
MOMENTUM = 0.9
RATE = 0.05
EMBED_RATE = 0.5
AVERAGE_DECAY = 0.9
HIGHEST = lax.Precision.HIGHEST


def contract_cols(left, right):
    return lax.dot_general(
        left, right, (((1,), (1,)), ((), ())), preferred_element_type=jnp.float32
    )


def renew(weight, momentum, average, gradient, step_rate):
    new_momentum = MOMENTUM * momentum + gradient
    new_weight = weight - step_rate * (gradient + MOMENTUM * new_momentum)
    new_average = AVERAGE_DECAY * average + (1.0 - AVERAGE_DECAY) * new_weight
    return (gradient, new_weight, new_momentum, new_average)


TILE = 256
SLOT_ROWS = 80
AUGMENT = 80
FAR = -1e30


def matmul(left, right):
    return lax.dot_general(
        left, right, (((1,), (0,)), ((), ())), preferred_element_type=jnp.float32
    )


def halves(values):
    high = values.astype(jnp.bfloat16)
    return high, (values - high.astype(jnp.float32)).astype(jnp.bfloat16)


def fold(values):
    total = values[:, :WIDTH]
    for start in range(WIDTH, values.shape[1], WIDTH):
        total = total + values[:, start : start + WIDTH]
    return total


def block_kernel(
    tokens_all,
    groups,
    slots_each,
    ids_ref,
    fields_ref,
    slots_ref,
    mask_ref,
    square_ref,
    qkv_ref,
    mlp_hbm,
    cols_ref,
    segment_ref,
    cot_hbm,
    out_hbm,
    grad_hbm,
    slot_ref,
    vec_ref,
    field_ref,
    out_t,
    qkv_t,
    proj_t,
    up_t,
    down_t,
    slots_t,
    value_map,
    value_cols,
    score_map,
    probs,
    pooled,
    start,
    inverse,
    input_one,
    query,
    key,
    key_t,
    value,
    value_t,
    raw,
    mixed,
    log_sum,
    attended,
    input_two,
    active,
    grad_up,
    grad_branch,
    grad_mid,
    grad_att,
    grad_out,
    inner,
    grad_triple,
    map_acc,
    key_acc,
    column_acc,
    keyvec_ref,
    mlp_ref,
    cot_ref,
    out_rows,
    grad_rows,
    spans_ref,
    in_sem,
    out_sem,
):
    bfloat, flt = jnp.bfloat16, jnp.float32
    loads = [
        pltpu.make_async_copy(mlp_hbm, mlp_ref, in_sem.at[0]),
        pltpu.make_async_copy(cot_hbm, cot_ref, in_sem.at[1]),
    ]
    for load in loads:
        load.start()
    length = cot_ref.shape[0]
    tiles = length // TILE
    depth = D
    each = slots_each
    team_size = raw.shape[1]
    spread = 2 if team_size == HEADS else 1
    scale = HDIM ** (-0.5)

    def lanes(i):
        return pl.ds(pl.multiple_of(i * TILE, TILE), TILE)

    def column(which):
        return cols_ref[:, which : which + 1]

    out_t[...] = square_ref[2].astype(flt).T.astype(bfloat)
    proj_t[...] = square_ref[3].astype(flt).T.astype(bfloat)
    for block in range(3):
        part = slice(block * depth, (block + 1) * depth)
        qkv_t[part] = qkv_ref[:, part].astype(flt).T.astype(bfloat)
    asked = cols_ref[:, 10:11]
    lane = lax.broadcasted_iota(jnp.int32, (depth, WIDTH), 1)
    head_of = lax.broadcasted_iota(jnp.int32, (depth, WIDTH), 0) // HDIM
    asked_high, asked_low = halves(jnp.where(lane == head_of, asked, 0.0))
    keyvec_ref[...] = (
        matmul(square_ref[0], asked_high) + matmul(square_ref[0], asked_low)
    ).astype(bfloat)
    firsts = [ids_ref[0, i * TILE] for i in range(tiles)]
    lasts = [ids_ref[0, (i + 1) * TILE - 1] for i in range(tiles)]
    for i in range(tiles):
        spans_ref[i, 0] = sum((lasts[j] < firsts[i]).astype(jnp.int32) for j in range(tiles))
        spans_ref[i, 1] = sum((firsts[j] <= lasts[i]).astype(jnp.int32) for j in range(tiles))
    slots = slots_ref[...]
    slots_high, slots_low = halves(slots)
    value_weight = square_ref[1]
    value_rows = matmul(slots_high, value_weight) + matmul(slots_low, value_weight)
    score_map[...] = matmul(slots_high, keyvec_ref[...]) + matmul(slots_low, keyvec_ref[...])
    turned_high, turned_low = halves(slots.T)
    slots_t[0] = turned_high
    slots_t[1] = turned_low
    value_turned = value_rows.T
    rows_high, rows_low = halves(value_turned)
    for head in range(HEADS):
        part = slice(head * HDIM, (head + 1) * HDIM)
        value_map[head, :HDIM] = rows_high[part]
        value_map[head, HDIM:] = rows_low[part]
        both = jnp.concatenate([value_turned[part], value_turned[part]], axis=0).T
        high = both.astype(bfloat)
        low = (both - high.astype(flt)).astype(bfloat)
        lane = lax.broadcasted_iota(jnp.int32, both.shape, 1)
        value_cols[head] = jnp.where(lane < HDIM, high.astype(flt), low.astype(flt)).astype(bfloat)
    column_acc[...] = jnp.zeros_like(column_acc)
    map_acc[...] = jnp.zeros_like(map_acc)
    key_acc[...] = jnp.zeros_like(key_acc)
    grad_triple[...] = jnp.zeros_like(grad_triple)

    packed = field_ref.shape[1]
    target = lax.broadcasted_iota(jnp.int32, (packed, packed), 0)
    origin = lax.broadcasted_iota(jnp.int32, (packed, packed), 1)
    place = (target % PATCH) * each + target // PATCH
    arrange = jnp.where((origin == place) & (target < PATCH * each), 1.0, 0.0).astype(bfloat)

    def fields_at(i):
        return [fields_ref[p, :, lanes(i)].astype(flt) for p in range(PATCH)]

    def score_col(p, head):
        return score_map[p * SLOT_ROWS : (p + 1) * SLOT_ROWS, head : head + 1]

    def mixture(prob, fields):
        return jnp.concatenate([prob * f for f in fields] + [prob], axis=0).astype(bfloat)

    def normalize_cols(values):
        center = values - jnp.mean(values, axis=0, keepdims=True)
        inv = lax.rsqrt(jnp.mean(center * center, axis=0, keepdims=True) + EPSILON)
        return center * inv, inv

    def normalize_cols_back(grad, normed, inv):
        first = jnp.mean(grad, axis=0, keepdims=True)
        second = jnp.mean(grad * normed, axis=0, keepdims=True)
        return inv * (grad - first - normed * second)

    @pl.loop(0, tiles, unroll=spread)
    def _(i):
        at = lanes(i)
        fields = fields_at(i)
        for head in range(HEADS):
            score = score_col(PATCH, head) + mask_ref[:, 0:1]
            for p in range(PATCH):
                score = score + score_col(p, head) * fields[p]
            score = score * scale
            weight = jnp.exp(score - jnp.max(score, axis=0, keepdims=True))
            prob = weight / jnp.sum(weight, axis=0, keepdims=True)
            probs[head, :, at] = prob
            both = matmul(value_map[head], mixture(prob, fields))
            part = slice(head * HDIM, (head + 1) * HDIM)
            total = both[:HDIM] + both[HDIM:] + cols_ref[part, 0:1]
            pooled[part, at] = total.astype(bfloat)
        begin = matmul(out_t[...], pooled[:, at]) + column(1)
        start[:, at] = begin
        normed, inv = normalize_cols(begin)
        inverse[0:1, at] = inv
        low = (normed * (1.0 + column(5)) + column(4)).astype(bfloat)
        input_one[:, at] = low
        segment = segment_ref[:, at]
        ident = lax.broadcasted_iota(jnp.int32, (AUGMENT - HDIM, TILE), 0)
        hot = jnp.where(ident == segment, 1.0, 0.0)
        cold = jnp.where((ident != segment) & (ident < 4), FAR, 0.0)
        triples = [
            matmul(qkv_t[block * depth : (block + 1) * depth], low).astype(bfloat)
            for block in range(3)
        ]
        key_t[:, at] = triples[1]
        for head in range(HEADS):
            part = slice(head * HDIM, (head + 1) * HDIM)
            queries = triples[0][part].astype(flt) * scale
            query[head, :, at] = jnp.concatenate([queries, hot], axis=0).astype(bfloat)
            long = jnp.concatenate([triples[1][part].astype(flt), cold], axis=0)
            key[head, at] = long.T.astype(bfloat)
            values = triples[2][part]
            value[head, at] = values.astype(flt).T.astype(bfloat)
            value_t[head, :HDIM, at] = values
            value_t[head, HDIM:, at] = jnp.ones((AUGMENT - HDIM, TILE), bfloat)

    @pl.loop(0, tiles)
    def _(i):
        at = lanes(i)
        low, high = spans_ref[i, 0], spans_ref[i, 1]

        mixed[...] = jnp.zeros_like(mixed)
        for base in range(0, HEADS, team_size):
            team = range(base, base + team_size)

            def scores(j, tops, team=team, base=base):
                new = []
                for head in team:
                    logits = matmul(key[head, lanes(j)], query[head, :, at])
                    raw[j, head - base] = logits
                    top = jnp.max(logits, axis=0, keepdims=True)
                    new.append(jnp.maximum(tops[head - base], top))
                return tuple(new)

            none = tuple(jnp.full((1, TILE), FAR, flt) for _ in team)
            tops = lax.fori_loop(low, high, scores, none)

            def blend(j, totals, team=team, base=base, tops=tops):
                new = []
                for head in team:
                    weight = jnp.exp(raw[j, head - base] - tops[head - base])
                    new.append(totals[head - base] + jnp.sum(weight, axis=0, keepdims=True))
                    mixed[head] += matmul(value_t[head, :, lanes(j)], weight.astype(bfloat))
                return tuple(new)

            zero = tuple(jnp.zeros((1, TILE), flt) for _ in team)
            totals = lax.fori_loop(low, high, blend, zero)
            for head in team:
                part = slice(head * HDIM, (head + 1) * HDIM)
                whole = mixed[head, :HDIM] / mixed[head, HDIM : HDIM + 1]
                upper, rest = halves(whole)
                attended[part, at] = upper
                grad_out[part, at] = rest
                log_sum[head : head + 1, at] = tops[head - base] + jnp.log(totals[head - base])

    rate = 1.0 / math.sqrt(tokens_all)
    for load in loads:
        load.wait()
    for block in range(4):
        part = slice(block * depth, (block + 1) * depth)
        up_t[part] = mlp_ref[0, :, part].astype(flt).T.astype(bfloat)
        down_t[part] = mlp_ref[1, :, part].astype(flt).T.astype(bfloat)

    @pl.loop(0, tiles)
    def _(i):
        at = lanes(i)
        att = attended[:, at]
        att_branch = matmul(proj_t[...], att) + column(2)
        mid = start[:, at] + column(6) * att_branch
        normed, inv = normalize_cols(mid)
        low = (normed * (1.0 + column(8)) + column(7)).astype(bfloat)
        input_two[:, at] = low
        out = column(3) + jnp.zeros((depth, TILE), flt)
        for block in range(HEADS):
            part = slice(block * TILE, (block + 1) * TILE)
            up = matmul(up_t[part], low)
            square = up * up
            curve = jnp.tanh(up * (GELU_ROOT + (GELU_ROOT * GELU_CUBE) * square))
            half = 0.5 + 0.5 * curve
            act = (up * half).astype(bfloat)
            active[part, at] = act
            slope = half + (0.5 * up) * (1.0 - curve * curve) * (
                GELU_ROOT + (3.0 * GELU_ROOT * GELU_CUBE) * square
            )
            raw[block // team_size, block % team_size] = slope
        out = out + matmul(mlp_ref[1], active[:, at])
        result = mid + column(9) * out
        rows = pl.ds(pl.multiple_of(i * TILE, TILE), TILE)
        out_rows[rows] = result.T.astype(bfloat)
        grad = cot_ref[rows].astype(flt).T * rate
        column_acc[9] += fold(grad * out)
        low_grad = (grad * column(9)).astype(bfloat)
        grad_branch[:, at] = low_grad
        column_acc[3] += fold(low_grad.astype(flt))
        grad_in = jnp.zeros((depth, TILE), flt)
        for base in range(0, HEADS, 3):
            blocks = range(base, base + 3)
            backs = [matmul(down_t[b * TILE : (b + 1) * TILE], low_grad) for b in blocks]
            lows = []
            for block, back in zip(blocks, backs):
                ups = (back * raw[block // team_size, block % team_size]).astype(bfloat)
                grad_up[block * TILE : (block + 1) * TILE, at] = ups
                lows.append(ups)
            for block, ups in zip(blocks, lows):
                part = slice(block * TILE, (block + 1) * TILE)
                grad_in = grad_in + matmul(mlp_ref[0, :, part], ups)
        column_acc[8] += fold(grad_in * normed)
        column_acc[7] += fold(grad_in)
        grad = grad + normalize_cols_back(grad_in * (1.0 + column(8)), normed, inv)
        grad_mid[:, at] = grad
        column_acc[6] += fold(grad * att_branch)
        low_grad = (grad * column(6)).astype(bfloat)
        grad_att[:, at] = low_grad
        column_acc[2] += fold(low_grad.astype(flt))
        grads = matmul(square_ref[3], low_grad)
        low_grad = grads.astype(bfloat)
        whole = att.astype(flt) + grad_out[:, at].astype(flt)
        product = low_grad.astype(flt) * whole
        grad_out[:, at] = low_grad
        for head in range(HEADS):
            part = slice(head * HDIM, (head + 1) * HDIM)
            inner[head : head + 1, at] = jnp.sum(product[part], axis=0, keepdims=True)

    def weight_grad(left, right, rows, base):
        for block in range(0, rows, TILE):
            size = min(TILE, rows - block)
            grads = contract_cols(left[...], right[block : block + size])
            for piece in range(size // WIDTH):
                place = base + block // WIDTH + piece
                grad_rows[place] = grads[:, piece * WIDTH : (piece + 1) * WIDTH].astype(bfloat)

    weight_grad(input_two, grad_up, 4 * depth, 0)
    weight_grad(grad_branch, active, 4 * depth, 12)
    weight_grad(attended, grad_att, depth, 33)
    stores = [pltpu.make_async_copy(out_rows, out_hbm, out_sem.at[0])]

    def store_grads(first, past):
        part = pl.ds(first, past - first)
        stores.append(
            pltpu.make_async_copy(grad_rows.at[part], grad_hbm.at[part], out_sem.at[len(stores)])
        )
        stores[-1].start()

    stores[0].start()
    store_grads(0, 24)
    store_grads(33, 36)

    @pl.loop(0, tiles)
    def _(i):
        at = lanes(i)

        @pl.loop(spans_ref[i, 0], spans_ref[i, 1])
        def _(j):
            to = lanes(j)
            parts = [slice(head * HDIM, (head + 1) * HDIM) for head in range(HEADS)]
            logits = [matmul(key[head, to], query[head, :, at]) for head in range(HEADS)]
            backs = [matmul(value[head, to], grad_out[parts[head], at]) for head in range(HEADS)]
            weights = [jnp.exp(logits[h] - log_sum[h : h + 1, at]) for h in range(HEADS)]
            grad_raw = [
                (weights[h] * (backs[h] - inner[h : h + 1, at])).astype(bfloat)
                for h in range(HEADS)
            ]
            weights = [weight.astype(bfloat) for weight in weights]
            for head, part in enumerate(parts):
                grad_triple[part, at] += matmul(key_t[part, to], grad_raw[head])
            for head in range(HEADS):
                part = slice(depth + head * HDIM, depth + (head + 1) * HDIM)
                grad_triple[part, to] += contract_cols(query[head, :HDIM, at], grad_raw[head])
            for head in range(HEADS):
                part = slice(2 * depth + head * HDIM, 2 * depth + (head + 1) * HDIM)
                grad_triple[part, to] += contract_cols(grad_out[parts[head], at], weights[head])

    @pl.loop(0, tiles, unroll=spread)
    def _(i):
        at = lanes(i)
        grad_in = jnp.zeros((depth, TILE), flt)
        for block in range(3):
            part = slice(block * depth, (block + 1) * depth)
            grads = grad_triple[part, at]
            if block == 0:
                grads = grads * scale
            grads = grads.astype(bfloat)
            active[part, at] = grads
        grad_in = matmul(qkv_ref[...], active[: 3 * depth, at])
        inv = inverse[0:1, at]
        begin = start[:, at]
        normed = (begin - jnp.mean(begin, axis=0, keepdims=True)) * inv
        column_acc[5] += fold(grad_in * normed)
        column_acc[4] += fold(grad_in)
        grad = grad_mid[:, at] + normalize_cols_back(grad_in * (1.0 + column(5)), normed, inv)
        low_grad = grad.astype(bfloat)
        attended[:, at] = low_grad
        column_acc[1] += fold(low_grad.astype(flt))
        grads = matmul(square_ref[2], low_grad).astype(bfloat)
        column_acc[0] += fold(grads.astype(flt))
        fields = fields_at(i)
        field_grads = [jnp.zeros((SLOT_ROWS, TILE), flt) for _ in range(PATCH)]
        for head in range(HEADS):
            part = slice(head * HDIM, (head + 1) * HDIM)
            own = grads[part]
            prob = probs[head, :, at]
            cross = matmul(value_cols[head], jnp.concatenate([own, own], axis=0))
            pieces = [cross[p * SLOT_ROWS : (p + 1) * SLOT_ROWS] for p in range(PATCH + 1)]
            along = pieces[PATCH]
            for p in range(PATCH):
                along = along + pieces[p] * fields[p]
            center = jnp.sum(prob * along, axis=0, keepdims=True)
            grad_score = (prob * (along - center) * scale).astype(bfloat).astype(flt)
            for p in range(PATCH):
                field_grads[p] = (
                    field_grads[p] + prob * pieces[p] + grad_score * score_col(p, head)
                )
                key_acc[head, p] += fold(fields[p] * grad_score)
            key_acc[head, PATCH] += fold(grad_score)
            map_acc[part] += contract_cols(own, mixture(prob, fields))
        for group in range(groups):
            pieces = [grad[group * each : (group + 1) * each] for grad in field_grads]
            pieces.append(jnp.zeros((field_ref.shape[1] - PATCH * each, TILE), flt))
            field_ref[group, :, at] = matmul(
                arrange, jnp.concatenate(pieces, axis=0).astype(bfloat)
            ).astype(bfloat)

    weight_grad(input_one, active, 3 * depth, 24)
    store_grads(24, 33)
    weight_grad(pooled, attended, depth, 36)
    maps_high, maps_low = halves(map_acc[...])
    value_grad = (
        contract_cols(slots_t[0], maps_high)
        + contract_cols(slots_t[0], maps_low)
        + contract_cols(slots_t[1], maps_high)
    )
    for piece in range(3):
        part = slice(piece * WIDTH, (piece + 1) * WIDTH)
        grad_rows[39 + piece] = value_grad[:, part].astype(bfloat)
    lane = lax.broadcasted_iota(jnp.int32, (SLOT_ROWS, WIDTH), 1)
    keys = []
    for p in range(PATCH + 1):
        rows = jnp.zeros((SLOT_ROWS, WIDTH), flt)
        for head in range(HEADS):
            rows = rows + jnp.where(
                lane == head, jnp.sum(key_acc[head, p], axis=1, keepdims=True), 0.0
            )
        keys.append(rows)
    keys = jnp.concatenate(keys, axis=0)
    keys_high, keys_low = halves(keys)
    key_grad = (
        matmul(slots_t[0], keys_high) + matmul(slots_t[0], keys_low) + matmul(slots_t[1], keys_high)
    )
    grad_rows[42] = key_grad.astype(bfloat)
    grad_rows[43] = jnp.zeros_like(grad_rows[43])
    store_grads(36, 44)
    slot_grad = (
        matmul(value_weight, maps_high)
        + matmul(value_weight, maps_low)
        + contract_cols(keyvec_ref[...], keys_high)
        + contract_cols(keyvec_ref[...], keys_low)
    )
    turned = slot_grad.T
    pairs, rows = slot_ref.shape[1], slot_ref.shape[3]
    size = slot_share((PATCH + 1) * each, 2 * pairs)
    for group in range(groups):
        pieces = [
            turned[p * SLOT_ROWS + group * each : p * SLOT_ROWS + (group + 1) * each][
                :, piece * WIDTH : (piece + 1) * WIDTH
            ]
            for piece in range(3)
            for p in range(PATCH + 1)
        ]
        used = 3 * (PATCH + 1) * each
        pieces.append(jnp.zeros((2 * pairs * size + rows - used, WIDTH), flt))
        flat = jnp.concatenate(pieces, axis=0)
        for block in range(2 * pairs):
            part = flat[block * size : block * size + rows]
            slot_ref[group, block // 2, block % 2] = part.astype(bfloat)
    grad_high, grad_low = halves(key_grad)
    key_turned = square_ref[0].astype(flt).T.astype(bfloat)
    asked = matmul(key_turned, grad_high) + matmul(key_turned, grad_low)
    lane = lax.broadcasted_iota(jnp.int32, (depth, WIDTH), 1)
    head_of = lax.broadcasted_iota(jnp.int32, (depth, WIDTH), 0) // HDIM
    columns = jnp.where(
        lane == 0, jnp.sum(jnp.where(lane == head_of, asked, 0.0), axis=1, keepdims=True), 0.0
    )
    columns = columns + jnp.where(lane == 11, cols_ref[:, 11:12], 0.0)
    for which in range(10):
        columns = columns + jnp.where(
            lane == which + 1, jnp.sum(column_acc[which], axis=1, keepdims=True), 0.0
        )
    vec_ref[...] = columns.T[:VEC_ROWS]
    for store in stores:
        store.wait()


def slot_share(rows, count):
    return -(-3 * rows // count)


def block_step(count, groups, own, each, segment, fields, slots, mask, square, qkv, mlp, cols, cot):
    length = cot.shape[0]
    bfloat, flt = jnp.bfloat16, jnp.float32
    rows = (PATCH + 1) * SLOT_ROWS
    tiles = length // TILE
    block_rows = -(-own // 16) * 16
    field_rows = -(-PATCH * each // 16) * 16
    team_size = HEADS if count * block_rows <= D else HEADS // 2
    vmem = pl.BlockSpec(memory_space=pltpu.VMEM)
    hbm = pl.BlockSpec(memory_space=pl.ANY)
    shapes = [
        ((D, D), bfloat),
        ((3 * D, D), bfloat),
        ((D, D), bfloat),
        ((4 * D, D), bfloat),
        ((4 * D, D), bfloat),
        ((2, D, rows), bfloat),
        ((HEADS, 2 * HDIM, rows), bfloat),
        ((HEADS, rows, 2 * HDIM), bfloat),
        ((rows, WIDTH), flt),
        ((HEADS, SLOT_ROWS, length), flt),
        ((D, length), bfloat),
        ((D, length), flt),
        ((8, length), flt),
        ((D, length), bfloat),
        ((HEADS, AUGMENT, length), bfloat),
        ((HEADS, length, AUGMENT), bfloat),
        ((D, length), bfloat),
        ((HEADS, length, HDIM), bfloat),
        ((HEADS, AUGMENT, length), bfloat),
        ((tiles, team_size, TILE, TILE), flt),
        ((HEADS, AUGMENT, TILE), flt),
        ((8, length), flt),
        ((D, length), bfloat),
        ((D, length), bfloat),
        ((4 * D, length), bfloat),
        ((4 * D, length), bfloat),
        ((D, length), bfloat),
        ((D, length), flt),
        ((D, length), bfloat),
        ((D, length), bfloat),
        ((8, length), flt),
        ((3 * D, length), flt),
        ((D, rows), flt),
        ((HEADS, PATCH + 1, SLOT_ROWS, WIDTH), flt),
        ((10, D, WIDTH), flt),
        ((D, WIDTH), bfloat),
        ((2, D, 4 * D), bfloat),
        ((length, D), bfloat),
        ((length, D), bfloat),
        ((44, D, WIDTH), bfloat),
    ]
    return pl.pallas_call(
        functools.partial(block_kernel, groups * count * length, groups, each),
        out_shape=(
            jax.ShapeDtypeStruct((length, D), bfloat),
            jax.ShapeDtypeStruct((44, D, WIDTH), bfloat),
            jax.ShapeDtypeStruct((groups, count // 2, 2, block_rows, WIDTH), bfloat),
            jax.ShapeDtypeStruct((VEC_ROWS, D), flt),
            jax.ShapeDtypeStruct((groups, field_rows, length), bfloat),
        ),
        in_specs=[pl.BlockSpec(memory_space=pltpu.SMEM)]
        + [vmem] * 5
        + [hbm, vmem, vmem, hbm],
        out_specs=(hbm, hbm, vmem, vmem, vmem),
        scratch_shapes=[pltpu.VMEM(shape, dtype) for shape, dtype in shapes]
        + [
            pltpu.SMEM((tiles, 2), jnp.int32),
            pltpu.SemaphoreType.DMA((2,)),
            pltpu.SemaphoreType.DMA((5,)),
        ],
        compiler_params=pltpu.CompilerParams(vmem_limit_bytes=62 << 20),
    )(segment, fields, slots, mask, square, qkv, mlp, cols, segment, cot)


CHUNKS = 4
CHUNK = 12
ORDER = (3, 0, 1, 2)
WIDTH = 128
VEC_ROWS = 16
MESH = pl.DeviceIdType.MESH


def flip(index, mask, bits):
    total = 0
    for bit in range(bits):
        own = (index // 2**bit) % 2
        total = total + (1 - own if (mask >> bit) & 1 else own) * 2**bit
    return total


def rounds_of(bits, backward):
    order = list(range(bits))
    return order[::-1] if backward else order


def mask_of(order, level, entry):
    mask = 0
    for place, bit in enumerate(order[level:]):
        if (entry >> (len(order) - level - 1 - place)) & 1:
            mask |= 1 << bit
    return mask


def greet(dp, here, masks, bits, groups):
    barrier = pltpu.get_barrier_semaphore()
    for mask in masks:
        pl.semaphore_signal(
            barrier, inc=1, device_id={"dp": flip(dp, mask, bits)}, device_id_type=MESH
        )
    for step in range(1, groups):
        pl.semaphore_signal(
            barrier, inc=1, device_id={"vars": (here + step) % groups}, device_id_type=MESH
        )
    pl.semaphore_wait(barrier, len(masks) + groups - 1)


class Copies:
    def __init__(self, send_sem, recv_sem):
        self.send_sem, self.recv_sem = send_sem, recv_sem
        self.started = []

    def start(self, source, target, device):
        place = len(self.started)
        copy = pltpu.make_async_remote_copy(
            src_ref=source,
            dst_ref=target,
            send_sem=self.send_sem.at[place],
            recv_sem=self.recv_sem.at[place],
            device_id=device,
            device_id_type=MESH,
        )
        copy.start()
        self.started.append(copy)
        return copy

    def finish(self):
        for copy in self.started:
            copy.wait_send()


class Spread:
    def __init__(self, copies, refs, dp, bits, order, own=None):
        self.copies, self.refs, self.dp, self.bits = copies, refs, dp, bits
        self.own = own
        self.order = order
        self.arriving = {}

    def send(self, mask, first):
        block = flip(self.dp, mask, self.bits)
        for level in range(first, len(self.order)):
            bit = self.order[level]
            partner = {"dp": flip(self.dp, 1 << bit, self.bits)}
            for which, ref in enumerate(self.refs):
                source = self.own[which] if self.own and not mask else ref(block)
                copy = self.copies.start(source, ref(block), partner)
                self.arriving.setdefault(level, []).append((mask | (1 << bit), copy))

    def begin(self):
        self.send(0, 0)

    def advance(self, level):
        for place, (mask, copy) in enumerate(self.arriving[level]):
            copy.wait_recv()
            if place % len(self.refs) == len(self.refs) - 1:
                self.send(mask, level + 1)


def reduce_kernel(
    count,
    groups,
    g_ref,
    s_ref,
    vec_ref,
    field_ref,
    total,
    slot_ref,
    ada_ref,
    sums_ref,
    field_out,
    recv0,
    acc,
    send_x,
    recv_x,
    zsend,
    zrecv,
    zkeep,
    ysend,
    yrecv,
    lsend,
    lrecv,
    vec_all,
    g_own,
    own_sem,
    send_sem,
    recv_sem,
):
    bits = count.bit_length() - 1
    lower = bits - 1
    dp, here = lax.axis_index("dp"), lax.axis_index("vars")
    core, pair = dp % 2, dp // 2
    own_copy = pltpu.make_async_copy(g_ref.at[:, :, core], g_own, own_sem.at[0])
    own_copy.start()
    greet(dp, here, [1 << bit for bit in range(bits)], bits, groups)
    copies = Copies(send_sem, recv_sem)
    half = CHUNK // 2
    share = CHUNK // groups
    other = {"dp": dp + 1 - 2 * core}

    def grads_at(piece):
        if piece < 2 * CHUNKS - 2:
            return piece * half, half
        size = half - groups // 2
        return (2 * CHUNKS - 2) * half + (piece % 2) * size, size

    vec_copies = [
        copies.start(vec_ref, vec_all.at[dp, here], {"vars": (here + step) % groups})
        for step in range(1, groups)
    ]
    vec_all[dp, here] = vec_ref[...]
    level0 = {}
    for chunk in ORDER:
        for side in range(2):
            piece = 2 * chunk + side
            base, size = grads_at(piece)
            level0[piece] = [
                copies.start(
                    g_ref.at[pl.ds(base, size), :, 1 - core],
                    recv0.at[piece, pl.ds(0, size)],
                    other,
                )
            ]
            if size < half:
                level0[piece].append(
                    copies.start(
                        s_ref.at[pl.ds(side * (half - size), half - size), :, 1 - core],
                        recv0.at[piece, pl.ds(size, half - size)],
                        other,
                    )
                )
    field_copies = [
        copies.start(
            field_ref.at[(here + step) % groups],
            field_out.at[here],
            {"vars": (here + step) % groups},
        )
        for step in range(1, groups)
    ]
    field_out[here] = field_ref[here]
    forth = list(range(1, bits)) + [0]
    vecs = Spread(copies, [lambda block: vec_all.at[block]], dp, bits, forth)
    slots = Spread(copies, [lambda block: slot_ref.at[block]], dp, bits, forth)

    def vec_finish():
        own = ada_ref.shape[0]
        sums = vec_all[0, 0]
        for device in range(1, count * groups):
            sums = sums + vec_all[device // groups, device % groups]
        sums_ref[...] = sums
        device_rows = vec_all[...].reshape(count * groups, VEC_ROWS, D)
        pick = lax.broadcasted_iota(jnp.int32, (D, own), 0) == dp * own + lax.broadcasted_iota(
            jnp.int32, (D, own), 1
        )
        pick = jnp.where(pick, 1.0, 0.0).astype(jnp.bfloat16)
        conditions = matmul(device_rows[:, 11, :].astype(jnp.bfloat16), pick)
        conditions = conditions.T.astype(jnp.bfloat16)
        for row in range(6):
            upper, rest = halves(device_rows[:, 5 + row, :])
            grads = matmul(conditions, upper) + matmul(conditions, rest)
            ada_ref[:, row * D : (row + 1) * D] = grads

    def vec_begin():
        for copy in vec_copies:
            copy.wait_recv()
        vecs.begin()

    crossing = {}
    own_copy.wait()

    def send_level(piece, level):
        order = rounds_of(lower, piece % 2)
        entries = 2 ** (lower - 1 - level)
        low = 2**lower - 2 ** (lower - level)
        partner = {"dp": 2 * flip(pair, 1 << order[level], lower) + core}
        crossing[piece, level] = copies.start(
            send_x.at[piece, pl.ds(low, entries)],
            recv_x.at[piece, pl.ds(low, entries)],
            partner,
        )

    def first(piece):
        order = rounds_of(lower, piece % 2)
        for copy in level0[piece]:
            copy.wait_recv()
        base, size = grads_at(piece)
        kept = 2 ** (lower - 1)
        for entry in range(2**lower):
            block = flip(pair, mask_of(order, 0, entry), lower)
            value = g_own[pl.ds(base, size), block].astype(jnp.float32)
            value = value + recv0[piece, pl.ds(0, size), block].astype(jnp.float32)
            if size < half:
                rest = half - size
                slots = s_ref[pl.ds((piece % 2) * rest, rest), block, core].astype(jnp.float32)
                slots = slots + recv0[piece, pl.ds(size, rest), block].astype(jnp.float32)
                value = jnp.concatenate([value[:2], slots[:1], value[2:], slots[1:]], axis=0)
            if entry < kept:
                acc[piece, entry] = value
            else:
                send_x[piece, entry - kept] = value.astype(jnp.bfloat16)
        send_level(piece, 0)

    def later(piece, level):
        crossing[piece, level].wait_recv()
        entries = 2 ** (lower - 1 - level)
        low = 2**lower - 2 ** (lower - level)
        kept = entries // 2
        for entry in range(entries):
            value = acc[piece, entry] + recv_x[piece, low + entry].astype(jnp.float32)
            if entries > 1 and entry >= kept:
                send_x[piece, low + entries + entry - kept] = value.astype(jnp.bfloat16)
            else:
                acc[piece, entry] = value
        if level + 1 < lower:
            send_level(piece, level + 1)

    near = {"vars": here + 1 - 2 * (here % 2)}
    far = {"vars": (here + 2) % groups}
    low, top = here % 2, here // 2
    across, over, around, forward = {}, {}, {}, {}

    final = ORDER[-1]

    def send_near(piece):
        if piece // 2 == final:
            return
        zsend[piece] = acc[piece, 0, pl.ds(share * (1 - low), share)].astype(jnp.bfloat16)
        across[piece] = copies.start(zsend.at[piece], zrecv.at[piece], near)

    def sum_near(piece):
        across[piece].wait_recv()
        own = acc[piece, 0, pl.ds(share * low, share)]
        zkeep[piece] = own + zrecv[piece].astype(jnp.float32)

    def send_far(chunk):
        if chunk == final:
            for side in range(2):
                for half_side in range(2):
                    part = acc[2 * chunk + side, 0, pl.ds(share * half_side, share)]
                    lsend[2 * side + half_side] = part.astype(jnp.bfloat16)
            over[chunk] = [
                copies.start(
                    lsend.at[(here + step) % groups],
                    lrecv.at[step - 1],
                    {"vars": (here + step) % groups},
                )
                for step in range(1, groups)
            ]
            return
        for side in range(2):
            sum_near(2 * chunk + side)
        ysend[chunk] = zkeep[2 * chunk + 1 - top].astype(jnp.bfloat16)
        over[chunk] = copies.start(ysend.at[chunk], yrecv.at[chunk], far)

    def quarter(chunk, which):
        count_back = share - 1 if chunk == CHUNKS - 1 else share
        return total.at[chunk, which, pl.ds(0, count_back)]

    def sum_far(chunk):
        if chunk == final:
            value = acc[2 * chunk + top, 0, pl.ds(share * low, share)]
            for step, copy in enumerate(over[chunk]):
                copy.wait_recv()
                value = value + lrecv[step].astype(jnp.float32)
            total[chunk, here] = value.astype(jnp.bfloat16)
            around[chunk] = [
                copies.start(
                    quarter(chunk, here), quarter(chunk, here), {"vars": (here + step) % groups}
                )
                for step in range(1, groups)
            ]
            return
        over[chunk].wait_recv()
        value = zkeep[2 * chunk + top] + yrecv[chunk].astype(jnp.float32)
        total[chunk, here] = value.astype(jnp.bfloat16)
        if chunk == CHUNKS - 1:
            slot_ref[dp] = value[share - 1]
        around[chunk] = [
            copies.start(quarter(chunk, here), quarter(chunk, here), to) for to in (far, near)
        ]

    def pass_on(chunk):
        if chunk == final:
            return
        around[chunk][0].wait_recv()
        other_quarter = quarter(chunk, (here + 2) % groups)
        forward[chunk] = copies.start(other_quarter, other_quarter, near)

    def finish(chunk):
        if chunk == final:
            for copy in around[chunk]:
                copy.wait_recv()
            return
        around[chunk][1].wait_recv()
        forward[chunk].wait_recv()

    def pieces(act):
        def both(chunk):
            act(2 * chunk)
            act(2 * chunk + 1)

        return both

    stages = [pieces(first)]
    stages += [pieces(lambda piece, level=level: later(piece, level)) for level in range(lower)]
    stages += [pieces(send_near), send_far, sum_far, pass_on, finish]
    extra = {1: [vec_begin], len(stages) - 3: [slots.begin]}
    for level in range(bits):
        tick = min(4 + 2 * level, CHUNKS + len(stages) - 2)
        extra.setdefault(tick, []).append(functools.partial(vecs.advance, level))
        tick = min(len(stages) - 1 + level, CHUNKS + len(stages) - 2)
        extra.setdefault(tick, []).append(functools.partial(slots.advance, level))
    extra.setdefault(min(4 + 2 * bits - 2, CHUNKS + len(stages) - 2), []).append(vec_finish)
    for tick in range(CHUNKS + len(stages) - 1):
        for stage in range(len(stages)):
            place = tick - stage
            if 0 <= place < CHUNKS:
                stages[stage](ORDER[place])
        for act in extra.get(tick, ()):
            act()
    for copy in field_copies:
        copy.wait_recv()
    copies.finish()


def reduce_all(count, groups, grads, slots, vec, field):
    bits = count.bit_length() - 1
    lower = bits - 1
    rows = grads.shape[3]
    half = CHUNK // 2
    pieces = 2 * CHUNKS
    share = CHUNK // groups
    copies = 4 * (groups - 1) + (pieces - 2) * (bits + 1) + 2 * bits
    copies += 4 * (CHUNKS - 1) + 2 + 2 * (count - 1)
    bfloat = jnp.bfloat16
    vmem = pl.BlockSpec(memory_space=pltpu.VMEM)
    return pl.pallas_call(
        functools.partial(reduce_kernel, count, groups),
        out_shape=(
            jax.ShapeDtypeStruct((CHUNKS, groups, share, rows, WIDTH), bfloat),
            jax.ShapeDtypeStruct((count, rows, WIDTH), jnp.float32),
            jax.ShapeDtypeStruct((D // count, 6 * D), jnp.float32),
            jax.ShapeDtypeStruct(vec.shape, jnp.float32),
            jax.ShapeDtypeStruct(field.shape, field.dtype),
        ),
        in_specs=[pl.BlockSpec(memory_space=pl.ANY)] + [vmem] * 3,
        out_specs=(vmem,) * 5,
        scratch_shapes=[
            pltpu.VMEM((pieces, half, count // 2, rows, WIDTH), bfloat),
            pltpu.VMEM((pieces, count // 4, half, rows, WIDTH), jnp.float32),
            pltpu.VMEM((pieces, count // 2 - 1, half, rows, WIDTH), bfloat),
            pltpu.VMEM((pieces, count // 2 - 1, half, rows, WIDTH), bfloat),
            pltpu.VMEM((pieces, share, rows, WIDTH), bfloat),
            pltpu.VMEM((pieces, share, rows, WIDTH), bfloat),
            pltpu.VMEM((pieces, share, rows, WIDTH), jnp.float32),
            pltpu.VMEM((CHUNKS, share, rows, WIDTH), bfloat),
            pltpu.VMEM((CHUNKS, share, rows, WIDTH), bfloat),
            pltpu.VMEM((groups, share, rows, WIDTH), bfloat),
            pltpu.VMEM((groups - 1, share, rows, WIDTH), bfloat),
            pltpu.VMEM((count, groups) + vec.shape, jnp.float32),
            pltpu.VMEM((CHUNKS * CHUNK - groups, count // 2, rows, WIDTH), bfloat),
            pltpu.SemaphoreType.DMA((1,)),
            pltpu.SemaphoreType.DMA((copies,)),
            pltpu.SemaphoreType.DMA((copies,)),
        ],
        compiler_params=pltpu.CompilerParams(
            collective_id=0, has_side_effects=True, vmem_limit_bytes=60 << 20
        ),
    )(grads, slots, vec, field)


def pack_rows(blocks, count, rows):
    own = blocks.shape[1] // count
    blocks = blocks.reshape(blocks.shape[0], count // 2, 2, own, WIDTH)
    return jnp.pad(blocks, ((0, 0), (0, 0), (0, 0), (0, rows - own), (0, 0)))


def renew_into(outs, refs, at, gradient, step_rate):
    new = renew(*(ref[at] for ref in refs), gradient, step_rate)
    for out, value in zip(outs, new):
        out[at] = value


def update_kernel(groups, sum_ref, slot_ref, ada_ref, vec_ref, back_ref, *refs):
    flt = jnp.float32
    slot_in, square_in, wide_in, mlp_in, vector_in = (refs[3 * i : 3 * i + 3] for i in range(5))
    refs = refs[15:]
    field_out = refs[-1]
    slot_out, square_out, wide_out, mlp_out, vector_out = (
        refs[4 * i : 4 * i + 4] for i in range(5)
    )
    own = wide_in[0].shape[0]
    for group in range(groups):
        rows = back_ref[group].astype(flt)
        for slot in range(field_out.shape[0]):
            field_out[slot, group] = rows[slot * PATCH : (slot + 1) * PATCH]
    bfloat = jnp.bfloat16
    last = CHUNKS - 1

    def block(place):
        if place < last * CHUNK:
            chunk, rest = divmod(place, CHUNK)
            share = CHUNK // groups
        else:
            chunk, rest, share = last, place - last * CHUNK, CHUNK // groups - 1
        return sum_ref[chunk, rest // share, rest % share, :own]

    for place in range(12):
        part = (slice(None), slice(place * WIDTH, (place + 1) * WIDTH))
        for half in range(2):
            grads = block(12 * half + place).astype(flt)
            renew_into(mlp_out, mlp_in, (half,) + part, grads, RATE)
    for place in range(9):
        part = (slice(None), slice(place * WIDTH, (place + 1) * WIDTH))
        renew_into(wide_out, wide_in, part, block(24 + place).astype(flt), RATE)
    for which, base in ((3, 33), (2, 36), (1, 39)):
        for place in range(3):
            part = (which, slice(None), slice(place * WIDTH, (place + 1) * WIDTH))
            renew_into(square_out, square_in, part, block(base + place).astype(flt), RATE)
    asked = vector_in[0][0:1]
    lane = lax.broadcasted_iota(jnp.int32, (WIDTH, D), 1) // HDIM
    head = lax.broadcasted_iota(jnp.int32, (WIDTH, D), 0)
    asked_high, asked_low = halves(jnp.where(lane == head, asked, 0.0))
    keys = block(42)
    renew_into(
        square_out, square_in, (0,), matmul(keys, asked_high) + matmul(keys, asked_low), RATE
    )
    part = (slice(None), slice(3 * D, 9 * D))
    renew_into(wide_out, wide_in, part, ada_ref[...], RATE)
    renew_into(vector_out, vector_in, (slice(None),), vec_ref[:11], RATE)
    each = slot_in[0].shape[1]
    blocks = slot_ref.shape[0]
    size = slot_share((PATCH + 1) * each, blocks)
    flat = jnp.concatenate([slot_ref[b, :size] for b in range(blocks)], axis=0)
    for p in range(PATCH + 1):
        pieces = [
            flat[(piece * (PATCH + 1) + p) * each : (piece * (PATCH + 1) + p + 1) * each]
            for piece in range(3)
        ]
        renew_into(slot_out, slot_in, (p,), jnp.concatenate(pieces, axis=1), EMBED_RATE)


def update_all(groups, sums, slot_blocks, ada, vec_sums, field_back, parameters):
    vmem = pl.BlockSpec(memory_space=pltpu.VMEM)
    shapes = [jax.ShapeDtypeStruct(a.shape, a.dtype) for a in parameters[::3] for _ in range(4)]
    field_shape = (parameters[0].shape[1], groups, PATCH, field_back.shape[2])
    shapes.append(jax.ShapeDtypeStruct(field_shape, jnp.float32))
    return pl.pallas_call(
        functools.partial(update_kernel, groups),
        out_shape=tuple(shapes),
        in_specs=[vmem] * (5 + len(parameters)),
        out_specs=(vmem,) * len(shapes),
        compiler_params=pltpu.CompilerParams(vmem_limit_bytes=60 << 20),
    )(sums, slot_blocks, ada, vec_sums, field_back, *parameters)


def gather_kernel(
    count,
    groups,
    ids_ref,
    field_ref,
    slot_ref,
    cond_in,
    square_ref,
    wide_ref,
    mlp_ref,
    vec_ref,
    patch_out,
    slots_out,
    mask_out,
    cols_out,
    square_out,
    qkv_out,
    mlp_out,
    field_src,
    field_all,
    slot_src,
    slot_all,
    cond_ref,
    cond_all,
    part,
    part_in,
    square_own,
    qkv_own,
    mlp_own,
    own_sem,
    send_sem,
    recv_sem,
):
    bfloat, flt = jnp.bfloat16, jnp.float32
    bits = count.bit_length() - 1
    dp, here = lax.axis_index("dp"), lax.axis_index("vars")
    own, rows = square_ref.shape[1], square_out.shape[2]
    if own < rows:
        for ref in (square_own, qkv_own, mlp_own):
            ref[...] = jnp.zeros_like(ref)
    square_own[:, :own] = square_ref[...].astype(bfloat)
    qkv_own[:own] = wide_ref[:, : 3 * D].astype(bfloat)
    mlp_own[:, :own] = mlp_ref[...].astype(bfloat)
    kept = [
        pltpu.make_async_copy(square_own, square_out.at[:, dp], own_sem.at[0]),
        pltpu.make_async_copy(qkv_own, qkv_out.at[dp], own_sem.at[1]),
        pltpu.make_async_copy(mlp_own, mlp_out.at[:, dp], own_sem.at[2]),
    ]
    for copy in kept:
        copy.start()
    used, packed = field_ref.shape[1], field_src.shape[1]
    for group in range(groups):
        pieces = [field_ref[group].astype(flt)]
        if packed > used:
            pieces.append(jnp.zeros((packed - used, field_ref.shape[2]), flt))
        field_src[group] = jnp.concatenate(pieces, axis=0).astype(bfloat)
    raw = cond_in[...].astype(flt)
    cond = (raw * jax.nn.sigmoid(raw)).astype(bfloat).astype(flt)
    cond_ref[...] = jnp.broadcast_to(cond, cond_ref.shape)
    cond_all[dp] = cond_ref[...]
    each = slot_ref.shape[1]
    per = slot_src.shape[1]
    pieces = 3 * (PATCH + 1)
    for piece in range(count * per):
        block, at = piece // per, piece % per
        if piece < pieces:
            lane = piece % 3 * WIDTH
            slot_src[block, at] = slot_ref[piece // 3, :, lane : lane + WIDTH]
        else:
            slot_src[block, at] = jnp.zeros((each, WIDTH), flt)
    for row in range(each):
        ident = jnp.full((1, WIDTH), ids_ref[0, row], jnp.int32).astype(flt)
        slot_src[pieces // per, pieces % per, row : row + 1] = ident
    greet(dp, here, range(1, count), bits, groups)
    copies = Copies(send_sem, recv_sem)
    forth = list(range(1, bits)) + [0]
    back = list(range(1, bits))[::-1] + [0]
    ones = Spread(
        copies,
        [lambda block: square_out.at[:, block], lambda block: qkv_out.at[block]],
        dp,
        bits,
        forth,
        [square_own, qkv_own],
    )
    twos = Spread(copies, [lambda block: mlp_out.at[:, block]], dp, bits, back, [mlp_own])
    conds = [
        copies.start(cond_ref, cond_all.at[dp], {"dp": (dp + step) % count})
        for step in range(1, count)
    ]
    arrivals = []
    slot_copies = [
        copies.start(
            slot_src.at[dp], slot_all.at[dp, here], {"vars": (here + step) % groups}
        )
        for step in range(1, groups)
    ]
    trees = [
        Spread(copies, [lambda block, at=at: slot_all.at[block, :, at]], dp, bits, order)
        for at, order in zip(range(per), (forth, back))
    ]
    ones.begin()
    twos.begin()
    for step in range(1, groups):
        to = (here + step) % groups
        arrivals.append(copies.start(field_src.at[to], field_all.at[here], {"vars": to}))
    field_all[here] = field_src[here]
    slot_all[dp, here] = slot_src[dp]
    for copy in conds:
        copy.wait_recv()
    cond = cond_all[:, 0, :].astype(bfloat)
    pick = lax.broadcasted_iota(jnp.int32, (D, own), 0) == dp * own + lax.broadcasted_iota(
        jnp.int32, (D, own), 1
    )
    cond_rows = matmul(cond, jnp.where(pick, 1.0, 0.0).astype(bfloat)).astype(bfloat)
    shares = matmul(cond_rows, wide_ref[:, 3 * D :].astype(bfloat))
    strips = shares.shape[1] // WIDTH
    for block in range(count):
        for strip in range(strips):
            part[block, strip : strip + 1] = shares[
                block : block + 1, strip * WIDTH : (strip + 1) * WIDTH
            ]
    part_copies = [
        copies.start(part.at[(dp + step) % count], part_in.at[step - 1], {"dp": (dp + step) % count})
        for step in range(1, count)
    ]
    for copy in slot_copies:
        copy.wait_recv()
    for tree in trees:
        tree.begin()
    for stream in (ones, twos, *trees):
        stream.advance(0)
    for copy in part_copies:
        copy.wait_recv()
    mine = part[dp]
    for step in range(1, count):
        mine = mine + part_in[step - 1]
    wide_parts = [
        jnp.concatenate([mine[3 * row + strip : 3 * row + strip + 1] for strip in range(3)], axis=1)
        for row in range(6)
    ]
    modulation = jnp.concatenate(wide_parts, axis=0) + vec_ref[5:11]
    columns = jnp.concatenate(
        [
            vec_ref[1:5],
            modulation,
            vec_ref[0:1],
            cond_ref[0:1],
            jnp.zeros((WIDTH - 12, D), flt),
        ],
        axis=0,
    )
    cols_out[...] = columns.T
    for level in range(1, bits - 1):
        for stream in (*trees, ones, twos):
            stream.advance(level)
    for tree in trees:
        tree.advance(bits - 1)
    spare = SLOT_ROWS - groups * each
    def slot_piece(piece, fill):
        rows = [slot_all[piece // per, source, piece % per] for source in range(groups)]
        rows.append(jnp.full((spare, WIDTH), fill, flt))
        return jnp.concatenate(rows, axis=0)

    for piece in range(pieces):
        base, lane = piece // 3 * SLOT_ROWS, piece % 3 * WIDTH
        slots_out[base : base + SLOT_ROWS, lane : lane + WIDTH] = slot_piece(piece, 0.0)
    mask_out[...] = jnp.where(slot_piece(pieces, float(NVARS)) < NVARS, 0.0, FAR)
    for copy in arrivals:
        copy.wait_recv()
    for p in range(PATCH):
        rows = [
            field_all[source, p * each : (p + 1) * each].astype(flt) for source in range(groups)
        ]
        rows.append(jnp.zeros((spare, field_ref.shape[2]), flt))
        patch_out[p] = jnp.concatenate(rows, axis=0).astype(bfloat)
    for stream in (ones, twos):
        stream.advance(bits - 1)
    for copy in kept:
        copy.wait()
    copies.finish()


def gather_all(count, groups, ids, field, slots, cond, square, wide, mlp, vectors):
    bits = count.bit_length() - 1
    own = square.shape[1]
    rows = -(-own // 16) * 16
    bfloat, flt = jnp.bfloat16, jnp.float32
    per = -(-(3 * (PATCH + 1) + 1) // count)
    copies = 2 * (groups - 1) + (5 + min(per, 2)) * (count - 1)
    length = field.shape[2]
    packed = -(-field.shape[1] // 16) * 16
    strips = (wide.shape[1] - 3 * D) // WIDTH
    vmem = pl.BlockSpec(memory_space=pltpu.VMEM)
    outs = [
        ((PATCH, SLOT_ROWS, length), bfloat),
        (((PATCH + 1) * SLOT_ROWS, D), flt),
        ((SLOT_ROWS, WIDTH), flt),
        ((D, WIDTH), flt),
        ((4, count, rows, D), bfloat),
        ((count, rows, 3 * D), bfloat),
        ((2, count, rows, 4 * D), bfloat),
    ]
    return pl.pallas_call(
        functools.partial(gather_kernel, count, groups),
        out_shape=tuple(jax.ShapeDtypeStruct(shape, dtype) for shape, dtype in outs),
        in_specs=[pl.BlockSpec(memory_space=pltpu.SMEM)] + [vmem] * 7,
        out_specs=(vmem,) * 4 + (pl.BlockSpec(memory_space=pl.ANY),) * 3,
        scratch_shapes=[
            pltpu.VMEM((groups, packed, length), bfloat),
            pltpu.VMEM((groups, packed, length), bfloat),
            pltpu.VMEM((count, per, slots.shape[1], WIDTH), flt),
            pltpu.VMEM((count, groups, per, slots.shape[1], WIDTH), flt),
            pltpu.VMEM((8, D), flt),
            pltpu.VMEM((count, 8, D), flt),
            pltpu.VMEM((count, strips, WIDTH), flt),
            pltpu.VMEM((count - 1, strips, WIDTH), flt),
            pltpu.VMEM((4, rows, D), bfloat),
            pltpu.VMEM((rows, 3 * D), bfloat),
            pltpu.VMEM((2, rows, 4 * D), bfloat),
            pltpu.SemaphoreType.DMA((3,)),
            pltpu.SemaphoreType.DMA((copies,)),
            pltpu.SemaphoreType.DMA((copies,)),
        ],
        compiler_params=pltpu.CompilerParams(
            collective_id=1, has_side_effects=True, vmem_limit_bytes=60 << 20
        ),
    )(ids, field, slots, cond, square, wide, mlp, vectors)


def on_device(
    fields,
    var_ids,
    segments,
    condition,
    cotangent,
    slot_weights,
    slot_momentum,
    slot_average,
    square,
    square_momentum,
    square_average,
    wide,
    wide_momentum,
    wide_average,
    mlp,
    mlp_momentum,
    mlp_average,
    vectors,
    vectors_momentum,
    vectors_average,
):
    bfloat = jnp.bfloat16
    length = fields.shape[4]
    count, groups = lax.axis_size("dp"), lax.axis_size("vars")
    own = square.shape[1]
    rows = -(-own // 16) * 16
    field = jnp.transpose(fields[:, 0], (1, 2, 0, 3)).reshape(groups, -1, length)
    gathered = gather_all(
        count,
        groups,
        var_ids[None],
        field,
        jnp.transpose(slot_weights, (1, 0, 2)),
        condition[0],
        square,
        wide,
        mlp,
        vectors,
    )
    patches, slot_rows, mask, columns = gathered[:4]
    square_full, qkv_full, mlp_full = (a[..., :own, :] for a in gathered[4:])
    block_out, grads, slots_packed, vec, field = block_step(
        count,
        groups,
        own,
        slot_weights.shape[0],
        segments[0],
        patches,
        slot_rows,
        mask,
        square_full.reshape(4, D, D),
        qkv_full.reshape(D, 3 * D),
        mlp_full.reshape(2, D, 4 * D),
        columns,
        cotangent[0, 0],
    )
    sums, slot_blocks, ada, vec_sums, field_back = reduce_all(
        count, groups, pack_rows(grads, count, rows), slots_packed, vec, field
    )
    updated = update_all(
        groups,
        sums,
        slot_blocks,
        ada,
        vec_sums,
        field_back,
        (
            *(jnp.transpose(a, (1, 0, 2)) for a in (slot_weights, slot_momentum, slot_average)),
            square,
            square_momentum,
            square_average,
            wide,
            wide_momentum,
            wide_average,
            mlp,
            mlp_momentum,
            mlp_average,
            vectors,
            vectors_momentum,
            vectors_average,
        ),
    )
    field_grad = updated[-1][:, None]
    slot_new = tuple(jnp.transpose(a, (1, 0, 2)) for a in updated[:4])
    return (block_out[None, None], field_grad) + slot_new + tuple(updated[4:-1])


def solution(mesh):
    placed = (
        P("vars", "dp", None, None, None),
        P("vars"),
        P("dp", "vars", None),
        P("dp", "vars", None),
        P("dp", "vars", None, None),
        P("vars", None, None),
        P("vars", None, None),
        P("vars", None, None),
        P(None, "dp", None),
        P(None, "dp", None),
        P(None, "dp", None),
        P("dp", None),
        P("dp", None),
        P("dp", None),
        P(None, "dp", None),
        P(None, "dp", None),
        P(None, "dp", None),
        P(),
        P(),
        P(),
    )
    return jax.shard_map(
        on_device,
        mesh=mesh,
        in_specs=placed,
        out_specs=(
            P("dp", "vars", None, None),
            P("vars", "dp", None, None, None),
            P("vars", None, None),
            P("vars", None, None),
            P("vars", None, None),
            P("vars", None, None),
            P(None, "dp", None),
            P(None, "dp", None),
            P(None, "dp", None),
            P(None, "dp", None),
            P("dp", None),
            P("dp", None),
            P("dp", None),
            P("dp", None),
            P(None, "dp", None),
            P(None, "dp", None),
            P(None, "dp", None),
            P(None, "dp", None),
            P(),
            P(),
            P(),
            P(),
        ),
        check_vma=False,
    )
```

```python
import functools
import math

import jax
import jax.numpy as jnp
from jax import lax
from jax.experimental import pallas as pl
from jax.experimental.pallas import tpu as pltpu
from jax.sharding import PartitionSpec as P

D = 384
HEADS = 6
HDIM = 64
PATCH = 4
NVARS = 69


NEGATIVE = -1e30
EPSILON = 1e-06
GELU_ROOT = math.sqrt(2.0 / math.pi)
GELU_CUBE = 0.044715
WIDTH = 128
VEC_ROWS = 16
MOMENTUM = 0.9
RATE = 0.05
EMBED_RATE = 0.5
AVERAGE_DECAY = 0.9
HIGHEST = lax.Precision.HIGHEST


def contract_cols(left, right):
    return lax.dot_general(
        left, right, (((1,), (1,)), ((), ())), preferred_element_type=jnp.float32
    )


def renew(weight, momentum, average, gradient, step_rate):
    new_momentum = MOMENTUM * momentum + gradient
    new_weight = weight - step_rate * (gradient + MOMENTUM * new_momentum)
    new_average = AVERAGE_DECAY * average + (1.0 - AVERAGE_DECAY) * new_weight
    return (gradient, new_weight, new_momentum, new_average)


TILE = 256
SLOT_ROWS = 80
AUGMENT = 80
FAR = -1e30


def matmul(left, right):
    return lax.dot_general(
        left, right, (((1,), (0,)), ((), ())), preferred_element_type=jnp.float32
    )


def halves(values):
    high = values.astype(jnp.bfloat16)
    return high, (values - high.astype(jnp.float32)).astype(jnp.bfloat16)


def fold(values):
    total = values[:, :WIDTH]
    for start in range(WIDTH, values.shape[1], WIDTH):
        total = total + values[:, start : start + WIDTH]
    return total


def block_kernel(
    tokens_all,
    groups,
    slots_each,
    ids_ref,
    fields_ref,
    slots_ref,
    mask_ref,
    square_ref,
    qkv_ref,
    mlp_hbm,
    cols_ref,
    segment_ref,
    cot_hbm,
    out_hbm,
    grad_hbm,
    slot_ref,
    vec_ref,
    field_ref,
    out_t,
    qkv_t,
    proj_t,
    up_t,
    down_t,
    slots_t,
    value_map,
    value_cols,
    score_map,
    probs,
    pooled,
    start,
    inverse,
    input_one,
    query,
    key,
    key_t,
    value,
    value_t,
    raw,
    mixed,
    log_sum,
    attended,
    input_two,
    active,
    grad_up,
    grad_branch,
    grad_mid,
    grad_att,
    grad_out,
    inner,
    grad_triple,
    map_acc,
    key_acc,
    column_acc,
    keyvec_ref,
    mlp_ref,
    cot_ref,
    out_rows,
    grad_rows,
    spans_ref,
    in_sem,
    out_sem,
):
    bfloat, flt = jnp.bfloat16, jnp.float32
    loads = [
        pltpu.make_async_copy(mlp_hbm, mlp_ref, in_sem.at[0]),
        pltpu.make_async_copy(cot_hbm, cot_ref, in_sem.at[1]),
    ]
    for load in loads:
        load.start()
    length = cot_ref.shape[0]
    tiles = length // TILE
    depth = D
    each = slots_each
    team_size = raw.shape[1]
    spread = 2 if team_size == HEADS else 1
    scale = HDIM ** (-0.5)

    def lanes(i):
        return pl.ds(pl.multiple_of(i * TILE, TILE), TILE)

    def column(which):
        return cols_ref[:, which : which + 1]

    out_t[...] = square_ref[2].astype(flt).T.astype(bfloat)
    proj_t[...] = square_ref[3].astype(flt).T.astype(bfloat)
    for block in range(3):
        part = slice(block * depth, (block + 1) * depth)
        qkv_t[part] = qkv_ref[:, part].astype(flt).T.astype(bfloat)
    asked = cols_ref[:, 10:11]
    lane = lax.broadcasted_iota(jnp.int32, (depth, WIDTH), 1)
    head_of = lax.broadcasted_iota(jnp.int32, (depth, WIDTH), 0) // HDIM
    asked_high, asked_low = halves(jnp.where(lane == head_of, asked, 0.0))
    keyvec_ref[...] = (
        matmul(square_ref[0], asked_high) + matmul(square_ref[0], asked_low)
    ).astype(bfloat)
    firsts = [ids_ref[0, i * TILE] for i in range(tiles)]
    lasts = [ids_ref[0, (i + 1) * TILE - 1] for i in range(tiles)]
    for i in range(tiles):
        spans_ref[i, 0] = sum((lasts[j] < firsts[i]).astype(jnp.int32) for j in range(tiles))
        spans_ref[i, 1] = sum((firsts[j] <= lasts[i]).astype(jnp.int32) for j in range(tiles))
    slots = slots_ref[...]
    slots_high, slots_low = halves(slots)
    value_weight = square_ref[1]
    value_rows = matmul(slots_high, value_weight) + matmul(slots_low, value_weight)
    score_map[...] = matmul(slots_high, keyvec_ref[...]) + matmul(slots_low, keyvec_ref[...])
    turned_high, turned_low = halves(slots.T)
    slots_t[0] = turned_high
    slots_t[1] = turned_low
    value_turned = value_rows.T
    rows_high, rows_low = halves(value_turned)
    for head in range(HEADS):
        part = slice(head * HDIM, (head + 1) * HDIM)
        value_map[head, :HDIM] = rows_high[part]
        value_map[head, HDIM:] = rows_low[part]
        both = jnp.concatenate([value_turned[part], value_turned[part]], axis=0).T
        high = both.astype(bfloat)
        low = (both - high.astype(flt)).astype(bfloat)
        lane = lax.broadcasted_iota(jnp.int32, both.shape, 1)
        value_cols[head] = jnp.where(lane < HDIM, high.astype(flt), low.astype(flt)).astype(bfloat)
    column_acc[...] = jnp.zeros_like(column_acc)
    map_acc[...] = jnp.zeros_like(map_acc)
    key_acc[...] = jnp.zeros_like(key_acc)
    grad_triple[...] = jnp.zeros_like(grad_triple)

    packed = field_ref.shape[1]
    target = lax.broadcasted_iota(jnp.int32, (packed, packed), 0)
    origin = lax.broadcasted_iota(jnp.int32, (packed, packed), 1)
    place = (target % PATCH) * each + target // PATCH
    arrange = jnp.where((origin == place) & (target < PATCH * each), 1.0, 0.0).astype(bfloat)

    def fields_at(i):
        return [fields_ref[p, :, lanes(i)].astype(flt) for p in range(PATCH)]

    def score_col(p, head):
        return score_map[p * SLOT_ROWS : (p + 1) * SLOT_ROWS, head : head + 1]

    def mixture(prob, fields):
        return jnp.concatenate([prob * f for f in fields] + [prob], axis=0).astype(bfloat)

    def normalize_cols(values):
        center = values - jnp.mean(values, axis=0, keepdims=True)
        inv = lax.rsqrt(jnp.mean(center * center, axis=0, keepdims=True) + EPSILON)
        return center * inv, inv

    def normalize_cols_back(grad, normed, inv):
        first = jnp.mean(grad, axis=0, keepdims=True)
        second = jnp.mean(grad * normed, axis=0, keepdims=True)
        return inv * (grad - first - normed * second)

    @pl.loop(0, tiles, unroll=spread)
    def _(i):
        at = lanes(i)
        fields = fields_at(i)
        for head in range(HEADS):
            score = score_col(PATCH, head) + mask_ref[:, 0:1]
            for p in range(PATCH):
                score = score + score_col(p, head) * fields[p]
            score = score * scale
            weight = jnp.exp(score - jnp.max(score, axis=0, keepdims=True))
            prob = weight * (1.0 / jnp.sum(weight, axis=0, keepdims=True))
            probs[head, :, at] = prob
            both = matmul(value_map[head], mixture(prob, fields))
            part = slice(head * HDIM, (head + 1) * HDIM)
            total = both[:HDIM] + both[HDIM:] + cols_ref[part, 0:1]
            pooled[part, at] = total.astype(bfloat)
        begin = matmul(out_t[...], pooled[:, at]) + column(1)
        start[:, at] = begin
        normed, inv = normalize_cols(begin)
        inverse[0:1, at] = inv
        low = (normed * (1.0 + column(5)) + column(4)).astype(bfloat)
        input_one[:, at] = low
        segment = segment_ref[:, at]
        ident = lax.broadcasted_iota(jnp.int32, (AUGMENT - HDIM, TILE), 0)
        hot = jnp.where(ident == segment, 1.0, 0.0)
        cold = jnp.where((ident != segment) & (ident < 4), FAR, 0.0)
        triples = [
            matmul(qkv_t[block * depth : (block + 1) * depth], low).astype(bfloat)
            for block in range(3)
        ]
        key_t[:, at] = triples[1]
        for head in range(HEADS):
            part = slice(head * HDIM, (head + 1) * HDIM)
            queries = triples[0][part].astype(flt) * scale
            query[head, :, at] = jnp.concatenate([queries, hot], axis=0).astype(bfloat)
            long = jnp.concatenate([triples[1][part].astype(flt), cold], axis=0)
            key[head, at] = long.T.astype(bfloat)
            values = triples[2][part]
            value[head, at] = values.astype(flt).T.astype(bfloat)
            value_t[head, :HDIM, at] = values
            value_t[head, HDIM:, at] = jnp.ones((AUGMENT - HDIM, TILE), bfloat)

    @pl.loop(0, tiles)
    def _(i):
        at = lanes(i)
        low, high = spans_ref[i, 0], spans_ref[i, 1]

        mixed[...] = jnp.zeros_like(mixed)
        for base in range(0, HEADS, team_size):
            team = range(base, base + team_size)

            def scores(j, tops, team=team, base=base):
                new = []
                for head in team:
                    logits = matmul(key[head, lanes(j)], query[head, :, at])
                    raw[j, head - base] = logits
                    top = jnp.max(logits, axis=0, keepdims=True)
                    new.append(jnp.maximum(tops[head - base], top))
                return tuple(new)

            none = tuple(jnp.full((1, TILE), FAR, flt) for _ in team)
            tops = lax.fori_loop(low, high, scores, none)

            def blend(j, totals, team=team, base=base, tops=tops):
                new = []
                for head in team:
                    weight = jnp.exp(raw[j, head - base] - tops[head - base])
                    new.append(totals[head - base] + jnp.sum(weight, axis=0, keepdims=True))
                    mixed[head] += matmul(value_t[head, :, lanes(j)], weight.astype(bfloat))
                return tuple(new)

            zero = tuple(jnp.zeros((1, TILE), flt) for _ in team)
            totals = lax.fori_loop(low, high, blend, zero)
            for head in team:
                part = slice(head * HDIM, (head + 1) * HDIM)
                whole = mixed[head, :HDIM] * (1.0 / mixed[head, HDIM : HDIM + 1])
                upper, rest = halves(whole)
                attended[part, at] = upper
                grad_out[part, at] = rest
                log_sum[head : head + 1, at] = tops[head - base] + jnp.log(totals[head - base])

    rate = 1.0 / math.sqrt(tokens_all)
    for load in loads:
        load.wait()
    for block in range(4):
        part = slice(block * depth, (block + 1) * depth)
        up_t[part] = mlp_ref[0, :, part].astype(flt).T.astype(bfloat)
        down_t[part] = mlp_ref[1, :, part].astype(flt).T.astype(bfloat)

    @pl.loop(0, tiles)
    def _(i):
        at = lanes(i)
        att = attended[:, at]
        att_branch = matmul(proj_t[...], att) + column(2)
        mid = start[:, at] + column(6) * att_branch
        normed, inv = normalize_cols(mid)
        low = (normed * (1.0 + column(8)) + column(7)).astype(bfloat)
        input_two[:, at] = low
        out = column(3) + jnp.zeros((depth, TILE), flt)
        for block in range(HEADS):
            part = slice(block * TILE, (block + 1) * TILE)
            up = matmul(up_t[part], low)
            square = up * up
            curve = jnp.tanh(up * (GELU_ROOT + (GELU_ROOT * GELU_CUBE) * square))
            half = 0.5 + 0.5 * curve
            act = (up * half).astype(bfloat)
            active[part, at] = act
            slope = half + (0.5 * up) * (1.0 - curve * curve) * (
                GELU_ROOT + (3.0 * GELU_ROOT * GELU_CUBE) * square
            )
            raw[block // team_size, block % team_size] = slope
        out = out + matmul(mlp_ref[1], active[:, at])
        result = mid + column(9) * out
        rows = pl.ds(pl.multiple_of(i * TILE, TILE), TILE)
        out_rows[rows] = result.T.astype(bfloat)
        grad = cot_ref[rows].astype(flt).T * rate
        column_acc[9] += fold(grad * out)
        low_grad = (grad * column(9)).astype(bfloat)
        grad_branch[:, at] = low_grad
        column_acc[3] += fold(low_grad.astype(flt))
        grad_in = jnp.zeros((depth, TILE), flt)
        for base in range(0, HEADS, 3):
            blocks = range(base, base + 3)
            backs = [matmul(down_t[b * TILE : (b + 1) * TILE], low_grad) for b in blocks]
            lows = []
            for block, back in zip(blocks, backs):
                ups = (back * raw[block // team_size, block % team_size]).astype(bfloat)
                grad_up[block * TILE : (block + 1) * TILE, at] = ups
                lows.append(ups)
            for block, ups in zip(blocks, lows):
                part = slice(block * TILE, (block + 1) * TILE)
                grad_in = grad_in + matmul(mlp_ref[0, :, part], ups)
        column_acc[8] += fold(grad_in * normed)
        column_acc[7] += fold(grad_in)
        grad = grad + normalize_cols_back(grad_in * (1.0 + column(8)), normed, inv)
        grad_mid[:, at] = grad
        column_acc[6] += fold(grad * att_branch)
        low_grad = (grad * column(6)).astype(bfloat)
        grad_att[:, at] = low_grad
        column_acc[2] += fold(low_grad.astype(flt))
        grads = matmul(square_ref[3], low_grad)
        low_grad = grads.astype(bfloat)
        whole = att.astype(flt) + grad_out[:, at].astype(flt)
        product = low_grad.astype(flt) * whole
        grad_out[:, at] = low_grad
        for head in range(HEADS):
            part = slice(head * HDIM, (head + 1) * HDIM)
            inner[head : head + 1, at] = jnp.sum(product[part], axis=0, keepdims=True)

    def weight_grad(left, right, rows, base):
        for block in range(0, rows, TILE):
            size = min(TILE, rows - block)
            grads = contract_cols(left[...], right[block : block + size])
            for piece in range(size // WIDTH):
                place = base + block // WIDTH + piece
                grad_rows[place] = grads[:, piece * WIDTH : (piece + 1) * WIDTH].astype(bfloat)

    weight_grad(input_two, grad_up, 4 * depth, 0)
    weight_grad(grad_branch, active, 4 * depth, 12)
    weight_grad(attended, grad_att, depth, 33)
    stores = [pltpu.make_async_copy(out_rows, out_hbm, out_sem.at[0])]

    def store_grads(first, past):
        part = pl.ds(first, past - first)
        stores.append(
            pltpu.make_async_copy(grad_rows.at[part], grad_hbm.at[part], out_sem.at[len(stores)])
        )
        stores[-1].start()

    stores[0].start()
    store_grads(0, 24)
    store_grads(33, 36)

    @pl.loop(0, tiles)
    def _(i):
        at = lanes(i)

        @pl.loop(spans_ref[i, 0], spans_ref[i, 1])
        def _(j):
            to = lanes(j)
            parts = [slice(head * HDIM, (head + 1) * HDIM) for head in range(HEADS)]
            logits = [matmul(key[head, to], query[head, :, at]) for head in range(HEADS)]
            backs = [matmul(value[head, to], grad_out[parts[head], at]) for head in range(HEADS)]
            weights = [jnp.exp(logits[h] - log_sum[h : h + 1, at]) for h in range(HEADS)]
            grad_raw = [
                (weights[h] * (backs[h] - inner[h : h + 1, at])).astype(bfloat)
                for h in range(HEADS)
            ]
            weights = [weight.astype(bfloat) for weight in weights]
            for head, part in enumerate(parts):
                grad_triple[part, at] += matmul(key_t[part, to], grad_raw[head])
            for head in range(HEADS):
                part = slice(depth + head * HDIM, depth + (head + 1) * HDIM)
                grad_triple[part, to] += contract_cols(query[head, :HDIM, at], grad_raw[head])
            for head in range(HEADS):
                part = slice(2 * depth + head * HDIM, 2 * depth + (head + 1) * HDIM)
                grad_triple[part, to] += contract_cols(grad_out[parts[head], at], weights[head])

    @pl.loop(0, tiles, unroll=spread)
    def _(i):
        at = lanes(i)
        grad_in = jnp.zeros((depth, TILE), flt)
        for block in range(3):
            part = slice(block * depth, (block + 1) * depth)
            grads = grad_triple[part, at]
            if block == 0:
                grads = grads * scale
            grads = grads.astype(bfloat)
            active[part, at] = grads
        grad_in = matmul(qkv_ref[...], active[: 3 * depth, at])
        inv = inverse[0:1, at]
        begin = start[:, at]
        normed = (begin - jnp.mean(begin, axis=0, keepdims=True)) * inv
        column_acc[5] += fold(grad_in * normed)
        column_acc[4] += fold(grad_in)
        grad = grad_mid[:, at] + normalize_cols_back(grad_in * (1.0 + column(5)), normed, inv)
        low_grad = grad.astype(bfloat)
        attended[:, at] = low_grad
        column_acc[1] += fold(low_grad.astype(flt))
        grads = matmul(square_ref[2], low_grad).astype(bfloat)
        column_acc[0] += fold(grads.astype(flt))
        fields = fields_at(i)
        field_grads = [jnp.zeros((SLOT_ROWS, TILE), flt) for _ in range(PATCH)]
        for head in range(HEADS):
            part = slice(head * HDIM, (head + 1) * HDIM)
            own = grads[part]
            prob = probs[head, :, at]
            cross = matmul(value_cols[head], jnp.concatenate([own, own], axis=0))
            pieces = [cross[p * SLOT_ROWS : (p + 1) * SLOT_ROWS] for p in range(PATCH + 1)]
            along = pieces[PATCH]
            for p in range(PATCH):
                along = along + pieces[p] * fields[p]
            center = jnp.sum(prob * along, axis=0, keepdims=True)
            grad_score = (prob * (along - center) * scale).astype(bfloat).astype(flt)
            for p in range(PATCH):
                field_grads[p] = (
                    field_grads[p] + prob * pieces[p] + grad_score * score_col(p, head)
                )
                key_acc[head, p] += fold(fields[p] * grad_score)
            key_acc[head, PATCH] += fold(grad_score)
            map_acc[part] += contract_cols(own, mixture(prob, fields))
        for group in range(groups):
            pieces = [grad[group * each : (group + 1) * each] for grad in field_grads]
            pieces.append(jnp.zeros((field_ref.shape[1] - PATCH * each, TILE), flt))
            field_ref[group, :, at] = matmul(
                arrange, jnp.concatenate(pieces, axis=0).astype(bfloat)
            ).astype(bfloat)

    weight_grad(input_one, active, 3 * depth, 24)
    store_grads(24, 33)
    weight_grad(pooled, attended, depth, 36)
    maps_high, maps_low = halves(map_acc[...])
    value_grad = (
        contract_cols(slots_t[0], maps_high)
        + contract_cols(slots_t[0], maps_low)
        + contract_cols(slots_t[1], maps_high)
    )
    for piece in range(3):
        part = slice(piece * WIDTH, (piece + 1) * WIDTH)
        grad_rows[39 + piece] = value_grad[:, part].astype(bfloat)
    lane = lax.broadcasted_iota(jnp.int32, (SLOT_ROWS, WIDTH), 1)
    keys = []
    for p in range(PATCH + 1):
        rows = jnp.zeros((SLOT_ROWS, WIDTH), flt)
        for head in range(HEADS):
            rows = rows + jnp.where(
                lane == head, jnp.sum(key_acc[head, p], axis=1, keepdims=True), 0.0
            )
        keys.append(rows)
    keys = jnp.concatenate(keys, axis=0)
    keys_high, keys_low = halves(keys)
    key_grad = (
        matmul(slots_t[0], keys_high) + matmul(slots_t[0], keys_low) + matmul(slots_t[1], keys_high)
    )
    grad_rows[42] = key_grad.astype(bfloat)
    grad_rows[43] = jnp.zeros_like(grad_rows[43])
    store_grads(36, 44)
    slot_grad = (
        matmul(value_weight, maps_high)
        + matmul(value_weight, maps_low)
        + contract_cols(keyvec_ref[...], keys_high)
        + contract_cols(keyvec_ref[...], keys_low)
    )
    turned = slot_grad.T
    pairs, rows = slot_ref.shape[1], slot_ref.shape[3]
    size = slot_share((PATCH + 1) * each, 2 * pairs)
    for group in range(groups):
        pieces = [
            turned[p * SLOT_ROWS + group * each : p * SLOT_ROWS + (group + 1) * each][
                :, piece * WIDTH : (piece + 1) * WIDTH
            ]
            for piece in range(3)
            for p in range(PATCH + 1)
        ]
        used = 3 * (PATCH + 1) * each
        pieces.append(jnp.zeros((2 * pairs * size + rows - used, WIDTH), flt))
        flat = jnp.concatenate(pieces, axis=0)
        for block in range(2 * pairs):
            part = flat[block * size : block * size + rows]
            slot_ref[group, block // 2, block % 2] = part.astype(bfloat)
    grad_high, grad_low = halves(key_grad)
    key_turned = square_ref[0].astype(flt).T.astype(bfloat)
    asked = matmul(key_turned, grad_high) + matmul(key_turned, grad_low)
    lane = lax.broadcasted_iota(jnp.int32, (depth, WIDTH), 1)
    head_of = lax.broadcasted_iota(jnp.int32, (depth, WIDTH), 0) // HDIM
    columns = jnp.where(
        lane == 0, jnp.sum(jnp.where(lane == head_of, asked, 0.0), axis=1, keepdims=True), 0.0
    )
    columns = columns + jnp.where(lane == 11, cols_ref[:, 11:12], 0.0)
    for which in range(10):
        columns = columns + jnp.where(
            lane == which + 1, jnp.sum(column_acc[which], axis=1, keepdims=True), 0.0
        )
    vec_ref[...] = columns.T[:VEC_ROWS]
    for store in stores:
        store.wait()


def slot_share(rows, count):
    return -(-3 * rows // count)


def block_step(count, groups, own, each, segment, fields, slots, mask, square, qkv, mlp, cols, cot):
    length = cot.shape[0]
    bfloat, flt = jnp.bfloat16, jnp.float32
    rows = (PATCH + 1) * SLOT_ROWS
    tiles = length // TILE
    block_rows = -(-own // 16) * 16
    field_rows = -(-PATCH * each // 16) * 16
    team_size = HEADS if count * block_rows <= D else HEADS // 2
    vmem = pl.BlockSpec(memory_space=pltpu.VMEM)
    hbm = pl.BlockSpec(memory_space=pl.ANY)
    shapes = [
        ((D, D), bfloat),
        ((3 * D, D), bfloat),
        ((D, D), bfloat),
        ((4 * D, D), bfloat),
        ((4 * D, D), bfloat),
        ((2, D, rows), bfloat),
        ((HEADS, 2 * HDIM, rows), bfloat),
        ((HEADS, rows, 2 * HDIM), bfloat),
        ((rows, WIDTH), flt),
        ((HEADS, SLOT_ROWS, length), flt),
        ((D, length), bfloat),
        ((D, length), flt),
        ((8, length), flt),
        ((D, length), bfloat),
        ((HEADS, AUGMENT, length), bfloat),
        ((HEADS, length, AUGMENT), bfloat),
        ((D, length), bfloat),
        ((HEADS, length, HDIM), bfloat),
        ((HEADS, AUGMENT, length), bfloat),
        ((tiles, team_size, TILE, TILE), flt),
        ((HEADS, AUGMENT, TILE), flt),
        ((8, length), flt),
        ((D, length), bfloat),
        ((D, length), bfloat),
        ((4 * D, length), bfloat),
        ((4 * D, length), bfloat),
        ((D, length), bfloat),
        ((D, length), flt),
        ((D, length), bfloat),
        ((D, length), bfloat),
        ((8, length), flt),
        ((3 * D, length), flt),
        ((D, rows), flt),
        ((HEADS, PATCH + 1, SLOT_ROWS, WIDTH), flt),
        ((10, D, WIDTH), flt),
        ((D, WIDTH), bfloat),
        ((2, D, 4 * D), bfloat),
        ((length, D), bfloat),
        ((length, D), bfloat),
        ((44, D, WIDTH), bfloat),
    ]
    return pl.pallas_call(
        functools.partial(block_kernel, groups * count * length, groups, each),
        out_shape=(
            jax.ShapeDtypeStruct((length, D), bfloat),
            jax.ShapeDtypeStruct((44, D, WIDTH), bfloat),
            jax.ShapeDtypeStruct((groups, count // 2, 2, block_rows, WIDTH), bfloat),
            jax.ShapeDtypeStruct((VEC_ROWS, D), flt),
            jax.ShapeDtypeStruct((groups, field_rows, length), bfloat),
        ),
        in_specs=[pl.BlockSpec(memory_space=pltpu.SMEM)]
        + [vmem] * 5
        + [hbm, vmem, vmem, hbm],
        out_specs=(hbm, hbm, vmem, vmem, vmem),
        scratch_shapes=[pltpu.VMEM(shape, dtype) for shape, dtype in shapes]
        + [
            pltpu.SMEM((tiles, 2), jnp.int32),
            pltpu.SemaphoreType.DMA((2,)),
            pltpu.SemaphoreType.DMA((5,)),
        ],
        compiler_params=pltpu.CompilerParams(vmem_limit_bytes=62 << 20),
    )(segment, fields, slots, mask, square, qkv, mlp, cols, segment, cot)


CHUNKS = 4
CHUNK = 12
ORDER = (3, 0, 1, 2)
WIDTH = 128
VEC_ROWS = 16
MESH = pl.DeviceIdType.MESH


def flip(index, mask, bits):
    total = 0
    for bit in range(bits):
        own = (index // 2**bit) % 2
        total = total + (1 - own if (mask >> bit) & 1 else own) * 2**bit
    return total


def rounds_of(bits, backward):
    order = list(range(bits))
    return order[::-1] if backward else order


def mask_of(order, level, entry):
    mask = 0
    for place, bit in enumerate(order[level:]):
        if (entry >> (len(order) - level - 1 - place)) & 1:
            mask |= 1 << bit
    return mask


def greet(dp, here, masks, bits, groups):
    barrier = pltpu.get_barrier_semaphore()
    for mask in masks:
        pl.semaphore_signal(
            barrier, inc=1, device_id={"dp": flip(dp, mask, bits)}, device_id_type=MESH
        )
    for step in range(1, groups):
        pl.semaphore_signal(
            barrier, inc=1, device_id={"vars": (here + step) % groups}, device_id_type=MESH
        )
    pl.semaphore_wait(barrier, len(masks) + groups - 1)


class Copies:
    def __init__(self, send_sem, recv_sem):
        self.send_sem, self.recv_sem = send_sem, recv_sem
        self.started = []

    def start(self, source, target, device):
        place = len(self.started)
        copy = pltpu.make_async_remote_copy(
            src_ref=source,
            dst_ref=target,
            send_sem=self.send_sem.at[place],
            recv_sem=self.recv_sem.at[place],
            device_id=device,
            device_id_type=MESH,
        )
        copy.start()
        self.started.append(copy)
        return copy

    def finish(self):
        for copy in self.started:
            copy.wait_send()


class Spread:
    def __init__(self, copies, refs, dp, bits, order, own=None):
        self.copies, self.refs, self.dp, self.bits = copies, refs, dp, bits
        self.own = own
        self.order = order
        self.arriving = {}

    def send(self, mask, first):
        block = flip(self.dp, mask, self.bits)
        for level in range(first, len(self.order)):
            bit = self.order[level]
            partner = {"dp": flip(self.dp, 1 << bit, self.bits)}
            for which, ref in enumerate(self.refs):
                source = self.own[which] if self.own and not mask else ref(block)
                copy = self.copies.start(source, ref(block), partner)
                self.arriving.setdefault(level, []).append((mask | (1 << bit), copy))

    def begin(self):
        self.send(0, 0)

    def advance(self, level):
        for place, (mask, copy) in enumerate(self.arriving[level]):
            copy.wait_recv()
            if place % len(self.refs) == len(self.refs) - 1:
                self.send(mask, level + 1)


def reduce_kernel(
    count,
    groups,
    g_ref,
    s_ref,
    vec_ref,
    field_ref,
    total,
    slot_ref,
    ada_ref,
    sums_ref,
    field_out,
    recv0,
    acc,
    send_x,
    recv_x,
    zsend,
    zrecv,
    zkeep,
    ysend,
    yrecv,
    lsend,
    lrecv,
    vec_all,
    g_own,
    own_sem,
    send_sem,
    recv_sem,
):
    bits = count.bit_length() - 1
    lower = bits - 1
    dp, here = lax.axis_index("dp"), lax.axis_index("vars")
    core, pair = dp % 2, dp // 2
    own_copy = pltpu.make_async_copy(g_ref.at[:, :, core], g_own, own_sem.at[0])
    own_copy.start()
    greet(dp, here, [1 << bit for bit in range(bits)], bits, groups)
    copies = Copies(send_sem, recv_sem)
    half = CHUNK // 2
    share = CHUNK // groups
    other = {"dp": dp + 1 - 2 * core}

    def grads_at(piece):
        if piece < 2 * CHUNKS - 2:
            return piece * half, half
        size = half - groups // 2
        return (2 * CHUNKS - 2) * half + (piece % 2) * size, size

    vec_copies = [
        copies.start(vec_ref, vec_all.at[dp, here], {"vars": (here + step) % groups})
        for step in range(1, groups)
    ]
    vec_all[dp, here] = vec_ref[...]
    level0 = {}
    for chunk in ORDER:
        for side in range(2):
            piece = 2 * chunk + side
            base, size = grads_at(piece)
            level0[piece] = [
                copies.start(
                    g_ref.at[pl.ds(base, size), :, 1 - core],
                    recv0.at[piece, pl.ds(0, size)],
                    other,
                )
            ]
            if size < half:
                level0[piece].append(
                    copies.start(
                        s_ref.at[pl.ds(side * (half - size), half - size), :, 1 - core],
                        recv0.at[piece, pl.ds(size, half - size)],
                        other,
                    )
                )
    field_copies = [
        copies.start(
            field_ref.at[(here + step) % groups],
            field_out.at[here],
            {"vars": (here + step) % groups},
        )
        for step in range(1, groups)
    ]
    field_out[here] = field_ref[here]
    forth = list(range(1, bits)) + [0]
    vecs = Spread(copies, [lambda block: vec_all.at[block]], dp, bits, forth)
    slots = Spread(copies, [lambda block: slot_ref.at[block]], dp, bits, forth)

    def vec_finish():
        own = ada_ref.shape[0]
        sums = vec_all[0, 0]
        for device in range(1, count * groups):
            sums = sums + vec_all[device // groups, device % groups]
        sums_ref[...] = sums
        device_rows = vec_all[...].reshape(count * groups, VEC_ROWS, D)
        pick = lax.broadcasted_iota(jnp.int32, (D, own), 0) == dp * own + lax.broadcasted_iota(
            jnp.int32, (D, own), 1
        )
        pick = jnp.where(pick, 1.0, 0.0).astype(jnp.bfloat16)
        conditions = matmul(device_rows[:, 11, :].astype(jnp.bfloat16), pick)
        conditions = conditions.T.astype(jnp.bfloat16)
        for row in range(6):
            upper, rest = halves(device_rows[:, 5 + row, :])
            grads = matmul(conditions, upper) + matmul(conditions, rest)
            ada_ref[:, row * D : (row + 1) * D] = grads

    def vec_begin():
        for copy in vec_copies:
            copy.wait_recv()
        vecs.begin()

    crossing = {}
    own_copy.wait()

    def send_level(piece, level):
        order = rounds_of(lower, piece % 2)
        entries = 2 ** (lower - 1 - level)
        low = 2**lower - 2 ** (lower - level)
        partner = {"dp": 2 * flip(pair, 1 << order[level], lower) + core}
        crossing[piece, level] = copies.start(
            send_x.at[piece, pl.ds(low, entries)],
            recv_x.at[piece, pl.ds(low, entries)],
            partner,
        )

    def first(piece):
        order = rounds_of(lower, piece % 2)
        for copy in level0[piece]:
            copy.wait_recv()
        base, size = grads_at(piece)
        kept = 2 ** (lower - 1)
        for entry in range(2**lower):
            block = flip(pair, mask_of(order, 0, entry), lower)
            value = g_own[pl.ds(base, size), block].astype(jnp.float32)
            value = value + recv0[piece, pl.ds(0, size), block].astype(jnp.float32)
            if size < half:
                rest = half - size
                slots = s_ref[pl.ds((piece % 2) * rest, rest), block, core].astype(jnp.float32)
                slots = slots + recv0[piece, pl.ds(size, rest), block].astype(jnp.float32)
                value = jnp.concatenate([value[:2], slots[:1], value[2:], slots[1:]], axis=0)
            if entry < kept:
                acc[piece, entry] = value
            else:
                send_x[piece, entry - kept] = value.astype(jnp.bfloat16)
        send_level(piece, 0)

    def later(piece, level):
        crossing[piece, level].wait_recv()
        entries = 2 ** (lower - 1 - level)
        low = 2**lower - 2 ** (lower - level)
        kept = entries // 2
        for entry in range(entries):
            value = acc[piece, entry] + recv_x[piece, low + entry].astype(jnp.float32)
            if entries > 1 and entry >= kept:
                send_x[piece, low + entries + entry - kept] = value.astype(jnp.bfloat16)
            else:
                acc[piece, entry] = value
        if level + 1 < lower:
            send_level(piece, level + 1)

    near = {"vars": here + 1 - 2 * (here % 2)}
    far = {"vars": (here + 2) % groups}
    low, top = here % 2, here // 2
    across, over, around, forward = {}, {}, {}, {}

    final = ORDER[-1]

    def send_near(piece):
        if piece // 2 == final:
            return
        zsend[piece] = acc[piece, 0, pl.ds(share * (1 - low), share)].astype(jnp.bfloat16)
        across[piece] = copies.start(zsend.at[piece], zrecv.at[piece], near)

    def sum_near(piece):
        across[piece].wait_recv()
        own = acc[piece, 0, pl.ds(share * low, share)]
        zkeep[piece] = own + zrecv[piece].astype(jnp.float32)

    def send_far(chunk):
        if chunk == final:
            for side in range(2):
                for half_side in range(2):
                    part = acc[2 * chunk + side, 0, pl.ds(share * half_side, share)]
                    lsend[2 * side + half_side] = part.astype(jnp.bfloat16)
            over[chunk] = [
                copies.start(
                    lsend.at[(here + step) % groups],
                    lrecv.at[step - 1],
                    {"vars": (here + step) % groups},
                )
                for step in range(1, groups)
            ]
            return
        for side in range(2):
            sum_near(2 * chunk + side)
        ysend[chunk] = zkeep[2 * chunk + 1 - top].astype(jnp.bfloat16)
        over[chunk] = copies.start(ysend.at[chunk], yrecv.at[chunk], far)

    def quarter(chunk, which):
        count_back = share - 1 if chunk == CHUNKS - 1 else share
        return total.at[chunk, which, pl.ds(0, count_back)]

    def sum_far(chunk):
        if chunk == final:
            value = acc[2 * chunk + top, 0, pl.ds(share * low, share)]
            for step, copy in enumerate(over[chunk]):
                copy.wait_recv()
                value = value + lrecv[step].astype(jnp.float32)
            total[chunk, here] = value.astype(jnp.bfloat16)
            around[chunk] = [
                copies.start(
                    quarter(chunk, here), quarter(chunk, here), {"vars": (here + step) % groups}
                )
                for step in range(1, groups)
            ]
            return
        over[chunk].wait_recv()
        value = zkeep[2 * chunk + top] + yrecv[chunk].astype(jnp.float32)
        total[chunk, here] = value.astype(jnp.bfloat16)
        if chunk == CHUNKS - 1:
            slot_ref[dp] = value[share - 1]
        around[chunk] = [
            copies.start(quarter(chunk, here), quarter(chunk, here), to) for to in (far, near)
        ]

    def pass_on(chunk):
        if chunk == final:
            return
        around[chunk][0].wait_recv()
        other_quarter = quarter(chunk, (here + 2) % groups)
        forward[chunk] = copies.start(other_quarter, other_quarter, near)

    def finish(chunk):
        if chunk == final:
            for copy in around[chunk]:
                copy.wait_recv()
            return
        around[chunk][1].wait_recv()
        forward[chunk].wait_recv()

    def pieces(act):
        def both(chunk):
            act(2 * chunk)
            act(2 * chunk + 1)

        return both

    stages = [pieces(first)]
    stages += [pieces(lambda piece, level=level: later(piece, level)) for level in range(lower)]
    stages += [pieces(send_near), send_far, sum_far, pass_on, finish]
    extra = {1: [vec_begin], len(stages) - 3: [slots.begin]}
    for level in range(bits):
        tick = min(4 + 2 * level, CHUNKS + len(stages) - 2)
        extra.setdefault(tick, []).append(functools.partial(vecs.advance, level))
        tick = min(len(stages) - 1 + level, CHUNKS + len(stages) - 2)
        extra.setdefault(tick, []).append(functools.partial(slots.advance, level))
    extra.setdefault(min(4 + 2 * bits - 2, CHUNKS + len(stages) - 2), []).append(vec_finish)
    for tick in range(CHUNKS + len(stages) - 1):
        for stage in range(len(stages)):
            place = tick - stage
            if 0 <= place < CHUNKS:
                stages[stage](ORDER[place])
        for act in extra.get(tick, ()):
            act()
    for copy in field_copies:
        copy.wait_recv()
    copies.finish()


def reduce_all(count, groups, grads, slots, vec, field):
    bits = count.bit_length() - 1
    lower = bits - 1
    rows = grads.shape[3]
    half = CHUNK // 2
    pieces = 2 * CHUNKS
    share = CHUNK // groups
    copies = 4 * (groups - 1) + (pieces - 2) * (bits + 1) + 2 * bits
    copies += 4 * (CHUNKS - 1) + 2 + 2 * (count - 1)
    bfloat = jnp.bfloat16
    vmem = pl.BlockSpec(memory_space=pltpu.VMEM)
    return pl.pallas_call(
        functools.partial(reduce_kernel, count, groups),
        out_shape=(
            jax.ShapeDtypeStruct((CHUNKS, groups, share, rows, WIDTH), bfloat),
            jax.ShapeDtypeStruct((count, rows, WIDTH), jnp.float32),
            jax.ShapeDtypeStruct((D // count, 6 * D), jnp.float32),
            jax.ShapeDtypeStruct(vec.shape, jnp.float32),
            jax.ShapeDtypeStruct(field.shape, field.dtype),
        ),
        in_specs=[pl.BlockSpec(memory_space=pl.ANY)] + [vmem] * 3,
        out_specs=(vmem,) * 5,
        scratch_shapes=[
            pltpu.VMEM((pieces, half, count // 2, rows, WIDTH), bfloat),
            pltpu.VMEM((pieces, count // 4, half, rows, WIDTH), jnp.float32),
            pltpu.VMEM((pieces, count // 2 - 1, half, rows, WIDTH), bfloat),
            pltpu.VMEM((pieces, count // 2 - 1, half, rows, WIDTH), bfloat),
            pltpu.VMEM((pieces, share, rows, WIDTH), bfloat),
            pltpu.VMEM((pieces, share, rows, WIDTH), bfloat),
            pltpu.VMEM((pieces, share, rows, WIDTH), jnp.float32),
            pltpu.VMEM((CHUNKS, share, rows, WIDTH), bfloat),
            pltpu.VMEM((CHUNKS, share, rows, WIDTH), bfloat),
            pltpu.VMEM((groups, share, rows, WIDTH), bfloat),
            pltpu.VMEM((groups - 1, share, rows, WIDTH), bfloat),
            pltpu.VMEM((count, groups) + vec.shape, jnp.float32),
            pltpu.VMEM((CHUNKS * CHUNK - groups, count // 2, rows, WIDTH), bfloat),
            pltpu.SemaphoreType.DMA((1,)),
            pltpu.SemaphoreType.DMA((copies,)),
            pltpu.SemaphoreType.DMA((copies,)),
        ],
        compiler_params=pltpu.CompilerParams(
            collective_id=0, has_side_effects=True, vmem_limit_bytes=60 << 20
        ),
    )(grads, slots, vec, field)


def pack_rows(blocks, count, rows):
    own = blocks.shape[1] // count
    blocks = blocks.reshape(blocks.shape[0], count // 2, 2, own, WIDTH)
    return jnp.pad(blocks, ((0, 0), (0, 0), (0, 0), (0, rows - own), (0, 0)))


def renew_into(outs, refs, at, gradient, step_rate):
    new = renew(*(ref[at] for ref in refs), gradient, step_rate)
    for out, value in zip(outs, new):
        out[at] = value


def update_kernel(groups, sum_ref, slot_ref, ada_ref, vec_ref, back_ref, *refs):
    flt = jnp.float32
    slot_in, square_in, wide_in, mlp_in, vector_in = (refs[3 * i : 3 * i + 3] for i in range(5))
    refs = refs[15:]
    field_out = refs[-1]
    slot_out, square_out, wide_out, mlp_out, vector_out = (
        refs[4 * i : 4 * i + 4] for i in range(5)
    )
    own = wide_in[0].shape[0]
    for group in range(groups):
        rows = back_ref[group].astype(flt)
        for slot in range(field_out.shape[0]):
            field_out[slot, group] = rows[slot * PATCH : (slot + 1) * PATCH]
    bfloat = jnp.bfloat16
    last = CHUNKS - 1

    def block(place):
        if place < last * CHUNK:
            chunk, rest = divmod(place, CHUNK)
            share = CHUNK // groups
        else:
            chunk, rest, share = last, place - last * CHUNK, CHUNK // groups - 1
        return sum_ref[chunk, rest // share, rest % share, :own]

    for place in range(12):
        part = (slice(None), slice(place * WIDTH, (place + 1) * WIDTH))
        for half in range(2):
            grads = block(12 * half + place).astype(flt)
            renew_into(mlp_out, mlp_in, (half,) + part, grads, RATE)
    for place in range(9):
        part = (slice(None), slice(place * WIDTH, (place + 1) * WIDTH))
        renew_into(wide_out, wide_in, part, block(24 + place).astype(flt), RATE)
    for which, base in ((3, 33), (2, 36), (1, 39)):
        for place in range(3):
            part = (which, slice(None), slice(place * WIDTH, (place + 1) * WIDTH))
            renew_into(square_out, square_in, part, block(base + place).astype(flt), RATE)
    asked = vector_in[0][0:1]
    lane = lax.broadcasted_iota(jnp.int32, (WIDTH, D), 1) // HDIM
    head = lax.broadcasted_iota(jnp.int32, (WIDTH, D), 0)
    asked_high, asked_low = halves(jnp.where(lane == head, asked, 0.0))
    keys = block(42)
    renew_into(
        square_out, square_in, (0,), matmul(keys, asked_high) + matmul(keys, asked_low), RATE
    )
    part = (slice(None), slice(3 * D, 9 * D))
    renew_into(wide_out, wide_in, part, ada_ref[...], RATE)
    renew_into(vector_out, vector_in, (slice(None),), vec_ref[:11], RATE)
    each = slot_in[0].shape[1]
    blocks = slot_ref.shape[0]
    size = slot_share((PATCH + 1) * each, blocks)
    flat = jnp.concatenate([slot_ref[b, :size] for b in range(blocks)], axis=0)
    for p in range(PATCH + 1):
        pieces = [
            flat[(piece * (PATCH + 1) + p) * each : (piece * (PATCH + 1) + p + 1) * each]
            for piece in range(3)
        ]
        renew_into(slot_out, slot_in, (p,), jnp.concatenate(pieces, axis=1), EMBED_RATE)


def update_all(groups, sums, slot_blocks, ada, vec_sums, field_back, parameters):
    vmem = pl.BlockSpec(memory_space=pltpu.VMEM)
    shapes = [jax.ShapeDtypeStruct(a.shape, a.dtype) for a in parameters[::3] for _ in range(4)]
    field_shape = (parameters[0].shape[1], groups, PATCH, field_back.shape[2])
    shapes.append(jax.ShapeDtypeStruct(field_shape, jnp.float32))
    return pl.pallas_call(
        functools.partial(update_kernel, groups),
        out_shape=tuple(shapes),
        in_specs=[vmem] * (5 + len(parameters)),
        out_specs=(vmem,) * len(shapes),
        compiler_params=pltpu.CompilerParams(vmem_limit_bytes=60 << 20),
    )(sums, slot_blocks, ada, vec_sums, field_back, *parameters)


def gather_kernel(
    count,
    groups,
    ids_ref,
    field_ref,
    slot_ref,
    cond_in,
    square_ref,
    wide_ref,
    mlp_ref,
    vec_ref,
    patch_out,
    slots_out,
    mask_out,
    cols_out,
    square_out,
    qkv_out,
    mlp_out,
    field_src,
    field_all,
    slot_src,
    slot_all,
    cond_ref,
    cond_all,
    part,
    part_in,
    square_own,
    qkv_own,
    mlp_own,
    own_sem,
    send_sem,
    recv_sem,
):
    bfloat, flt = jnp.bfloat16, jnp.float32
    bits = count.bit_length() - 1
    dp, here = lax.axis_index("dp"), lax.axis_index("vars")
    own, rows = square_ref.shape[1], square_out.shape[2]
    if own < rows:
        for ref in (square_own, qkv_own, mlp_own):
            ref[...] = jnp.zeros_like(ref)
    square_own[:, :own] = square_ref[...].astype(bfloat)
    qkv_own[:own] = wide_ref[:, : 3 * D].astype(bfloat)
    mlp_own[:, :own] = mlp_ref[...].astype(bfloat)
    kept = [
        pltpu.make_async_copy(square_own, square_out.at[:, dp], own_sem.at[0]),
        pltpu.make_async_copy(qkv_own, qkv_out.at[dp], own_sem.at[1]),
        pltpu.make_async_copy(mlp_own, mlp_out.at[:, dp], own_sem.at[2]),
    ]
    for copy in kept:
        copy.start()
    used, packed = field_ref.shape[1], field_src.shape[1]
    for group in range(groups):
        pieces = [field_ref[group].astype(flt)]
        if packed > used:
            pieces.append(jnp.zeros((packed - used, field_ref.shape[2]), flt))
        field_src[group] = jnp.concatenate(pieces, axis=0).astype(bfloat)
    raw = cond_in[...].astype(flt)
    cond = (raw * jax.nn.sigmoid(raw)).astype(bfloat).astype(flt)
    cond_ref[...] = jnp.broadcast_to(cond, cond_ref.shape)
    cond_all[dp] = cond_ref[...]
    each = slot_ref.shape[1]
    per = slot_src.shape[1]
    pieces = 3 * (PATCH + 1)
    for piece in range(count * per):
        block, at = piece // per, piece % per
        if piece < pieces:
            lane = piece % 3 * WIDTH
            slot_src[block, at] = slot_ref[piece // 3, :, lane : lane + WIDTH]
        else:
            slot_src[block, at] = jnp.zeros((each, WIDTH), flt)
    for row in range(each):
        ident = jnp.full((1, WIDTH), ids_ref[0, row], jnp.int32).astype(flt)
        slot_src[pieces // per, pieces % per, row : row + 1] = ident
    greet(dp, here, range(1, count), bits, groups)
    copies = Copies(send_sem, recv_sem)
    forth = list(range(1, bits)) + [0]
    back = list(range(1, bits))[::-1] + [0]
    ones = Spread(
        copies,
        [lambda block: square_out.at[:, block], lambda block: qkv_out.at[block]],
        dp,
        bits,
        forth,
        [square_own, qkv_own],
    )
    twos = Spread(copies, [lambda block: mlp_out.at[:, block]], dp, bits, back, [mlp_own])
    conds = [
        copies.start(cond_ref, cond_all.at[dp], {"dp": (dp + step) % count})
        for step in range(1, count)
    ]
    arrivals = []
    slot_copies = [
        copies.start(
            slot_src.at[dp], slot_all.at[dp, here], {"vars": (here + step) % groups}
        )
        for step in range(1, groups)
    ]
    trees = [
        Spread(copies, [lambda block, at=at: slot_all.at[block, :, at]], dp, bits, order)
        for at, order in zip(range(per), (forth, back))
    ]
    ones.begin()
    twos.begin()
    for step in range(1, groups):
        to = (here + step) % groups
        arrivals.append(copies.start(field_src.at[to], field_all.at[here], {"vars": to}))
    field_all[here] = field_src[here]
    slot_all[dp, here] = slot_src[dp]
    for copy in conds:
        copy.wait_recv()
    cond = cond_all[:, 0, :].astype(bfloat)
    pick = lax.broadcasted_iota(jnp.int32, (D, own), 0) == dp * own + lax.broadcasted_iota(
        jnp.int32, (D, own), 1
    )
    cond_rows = matmul(cond, jnp.where(pick, 1.0, 0.0).astype(bfloat)).astype(bfloat)
    shares = matmul(cond_rows, wide_ref[:, 3 * D :].astype(bfloat))
    strips = shares.shape[1] // WIDTH
    for block in range(count):
        for strip in range(strips):
            part[block, strip : strip + 1] = shares[
                block : block + 1, strip * WIDTH : (strip + 1) * WIDTH
            ]
    part_copies = [
        copies.start(part.at[(dp + step) % count], part_in.at[step - 1], {"dp": (dp + step) % count})
        for step in range(1, count)
    ]
    for copy in slot_copies:
        copy.wait_recv()
    for tree in trees:
        tree.begin()
    for stream in (ones, twos, *trees):
        stream.advance(0)
    for copy in part_copies:
        copy.wait_recv()
    mine = part[dp]
    for step in range(1, count):
        mine = mine + part_in[step - 1]
    wide_parts = [
        jnp.concatenate([mine[3 * row + strip : 3 * row + strip + 1] for strip in range(3)], axis=1)
        for row in range(6)
    ]
    modulation = jnp.concatenate(wide_parts, axis=0) + vec_ref[5:11]
    columns = jnp.concatenate(
        [
            vec_ref[1:5],
            modulation,
            vec_ref[0:1],
            cond_ref[0:1],
            jnp.zeros((WIDTH - 12, D), flt),
        ],
        axis=0,
    )
    cols_out[...] = columns.T
    for level in range(1, bits - 1):
        for stream in (twos, ones, *trees):
            stream.advance(level)
    for tree in trees:
        tree.advance(bits - 1)
    spare = SLOT_ROWS - groups * each
    def slot_piece(piece, fill):
        rows = [slot_all[piece // per, source, piece % per] for source in range(groups)]
        rows.append(jnp.full((spare, WIDTH), fill, flt))
        return jnp.concatenate(rows, axis=0)

    for piece in range(pieces):
        base, lane = piece // 3 * SLOT_ROWS, piece % 3 * WIDTH
        slots_out[base : base + SLOT_ROWS, lane : lane + WIDTH] = slot_piece(piece, 0.0)
    mask_out[...] = jnp.where(slot_piece(pieces, float(NVARS)) < NVARS, 0.0, FAR)
    for copy in arrivals:
        copy.wait_recv()
    for p in range(PATCH):
        rows = [
            field_all[source, p * each : (p + 1) * each].astype(flt) for source in range(groups)
        ]
        rows.append(jnp.zeros((spare, field_ref.shape[2]), flt))
        patch_out[p] = jnp.concatenate(rows, axis=0).astype(bfloat)
    for stream in (ones, twos):
        stream.advance(bits - 1)
    for copy in kept:
        copy.wait()
    copies.finish()


def gather_all(count, groups, ids, field, slots, cond, square, wide, mlp, vectors):
    bits = count.bit_length() - 1
    own = square.shape[1]
    rows = -(-own // 16) * 16
    bfloat, flt = jnp.bfloat16, jnp.float32
    per = -(-(3 * (PATCH + 1) + 1) // count)
    copies = 2 * (groups - 1) + (5 + min(per, 2)) * (count - 1)
    length = field.shape[2]
    packed = -(-field.shape[1] // 16) * 16
    strips = (wide.shape[1] - 3 * D) // WIDTH
    vmem = pl.BlockSpec(memory_space=pltpu.VMEM)
    outs = [
        ((PATCH, SLOT_ROWS, length), bfloat),
        (((PATCH + 1) * SLOT_ROWS, D), flt),
        ((SLOT_ROWS, WIDTH), flt),
        ((D, WIDTH), flt),
        ((4, count, rows, D), bfloat),
        ((count, rows, 3 * D), bfloat),
        ((2, count, rows, 4 * D), bfloat),
    ]
    return pl.pallas_call(
        functools.partial(gather_kernel, count, groups),
        out_shape=tuple(jax.ShapeDtypeStruct(shape, dtype) for shape, dtype in outs),
        in_specs=[pl.BlockSpec(memory_space=pltpu.SMEM)] + [vmem] * 7,
        out_specs=(vmem,) * 4 + (pl.BlockSpec(memory_space=pl.ANY),) * 3,
        scratch_shapes=[
            pltpu.VMEM((groups, packed, length), bfloat),
            pltpu.VMEM((groups, packed, length), bfloat),
            pltpu.VMEM((count, per, slots.shape[1], WIDTH), flt),
            pltpu.VMEM((count, groups, per, slots.shape[1], WIDTH), flt),
            pltpu.VMEM((8, D), flt),
            pltpu.VMEM((count, 8, D), flt),
            pltpu.VMEM((count, strips, WIDTH), flt),
            pltpu.VMEM((count - 1, strips, WIDTH), flt),
            pltpu.VMEM((4, rows, D), bfloat),
            pltpu.VMEM((rows, 3 * D), bfloat),
            pltpu.VMEM((2, rows, 4 * D), bfloat),
            pltpu.SemaphoreType.DMA((3,)),
            pltpu.SemaphoreType.DMA((copies,)),
            pltpu.SemaphoreType.DMA((copies,)),
        ],
        compiler_params=pltpu.CompilerParams(
            collective_id=1, has_side_effects=True, vmem_limit_bytes=60 << 20
        ),
    )(ids, field, slots, cond, square, wide, mlp, vectors)


def on_device(
    fields,
    var_ids,
    segments,
    condition,
    cotangent,
    slot_weights,
    slot_momentum,
    slot_average,
    square,
    square_momentum,
    square_average,
    wide,
    wide_momentum,
    wide_average,
    mlp,
    mlp_momentum,
    mlp_average,
    vectors,
    vectors_momentum,
    vectors_average,
):
    bfloat = jnp.bfloat16
    length = fields.shape[4]
    count, groups = lax.axis_size("dp"), lax.axis_size("vars")
    own = square.shape[1]
    rows = -(-own // 16) * 16
    field = jnp.transpose(fields[:, 0], (1, 2, 0, 3)).reshape(groups, -1, length)
    gathered = gather_all(
        count,
        groups,
        var_ids[None],
        field,
        jnp.transpose(slot_weights, (1, 0, 2)),
        condition[0],
        square,
        wide,
        mlp,
        vectors,
    )
    patches, slot_rows, mask, columns = gathered[:4]
    square_full, qkv_full, mlp_full = (a[..., :own, :] for a in gathered[4:])
    block_out, grads, slots_packed, vec, field = block_step(
        count,
        groups,
        own,
        slot_weights.shape[0],
        segments[0],
        patches,
        slot_rows,
        mask,
        square_full.reshape(4, D, D),
        qkv_full.reshape(D, 3 * D),
        mlp_full.reshape(2, D, 4 * D),
        columns,
        cotangent[0, 0],
    )
    sums, slot_blocks, ada, vec_sums, field_back = reduce_all(
        count, groups, pack_rows(grads, count, rows), slots_packed, vec, field
    )
    updated = update_all(
        groups,
        sums,
        slot_blocks,
        ada,
        vec_sums,
        field_back,
        (
            *(jnp.transpose(a, (1, 0, 2)) for a in (slot_weights, slot_momentum, slot_average)),
            square,
            square_momentum,
            square_average,
            wide,
            wide_momentum,
            wide_average,
            mlp,
            mlp_momentum,
            mlp_average,
            vectors,
            vectors_momentum,
            vectors_average,
        ),
    )
    field_grad = updated[-1][:, None]
    slot_new = tuple(jnp.transpose(a, (1, 0, 2)) for a in updated[:4])
    return (block_out[None, None], field_grad) + slot_new + tuple(updated[4:-1])


def solution(mesh):
    placed = (
        P("vars", "dp", None, None, None),
        P("vars"),
        P("dp", "vars", None),
        P("dp", "vars", None),
        P("dp", "vars", None, None),
        P("vars", None, None),
        P("vars", None, None),
        P("vars", None, None),
        P(None, "dp", None),
        P(None, "dp", None),
        P(None, "dp", None),
        P("dp", None),
        P("dp", None),
        P("dp", None),
        P(None, "dp", None),
        P(None, "dp", None),
        P(None, "dp", None),
        P(),
        P(),
        P(),
    )
    return jax.shard_map(
        on_device,
        mesh=mesh,
        in_specs=placed,
        out_specs=(
            P("dp", "vars", None, None),
            P("vars", "dp", None, None, None),
            P("vars", None, None),
            P("vars", None, None),
            P("vars", None, None),
            P("vars", None, None),
            P(None, "dp", None),
            P(None, "dp", None),
            P(None, "dp", None),
            P(None, "dp", None),
            P("dp", None),
            P("dp", None),
            P("dp", None),
            P("dp", None),
            P(None, "dp", None),
            P(None, "dp", None),
            P(None, "dp", None),
            P(None, "dp", None),
            P(),
            P(),
            P(),
            P(),
        ),
        check_vma=False,
    )
```
